128 devices in a mesh: ty: 16 (over z_hi, y, core), tx: 8 (over z_lo, x).
Axes of the slice: x: 4, y: 4, z: 4 (z_hi: 2, z_lo: 2; z = z_hi * 2 + z_lo), core: 2. Of those that a mesh axis runs over, the one named last changes fastest.
Arguments:
- inputs: bfloat16 [768, 1024, 128], P('ty', 'tx'), may hold values from -6 to 6
- weight_one: bfloat16 [1152, 128], replicated, may hold values from -0.1875 to 0.1875
- weight_two: bfloat16 [1152, 128], replicated, may hold values from -0.1875 to 0.1875
- weight_three: bfloat16 [1152, 256], replicated, may hold values from -0.1875 to 0.1875
- noise_table: float32 [64, 256], replicated, may hold values from -1.5 to 1.5
- frequency: float32 [2, 128], replicated, may hold values from 0.002 to 0.3
- anchor: int32 [2], replicated, may hold values from 0 to 2048
- noise_index: int32 [1], replicated, may hold values from 0 to 63
- cotangent: bfloat16 [192, 256, 256], P('ty', 'tx'), may hold values from -6 to 6
Outputs:
- coarse_out: bfloat16 [192, 256, 256], P('ty', 'tx')
- grad_inputs: bfloat16 [768, 1024, 128], P('ty', 'tx')
- grad_weight_one: float32 [1152, 128], P(('ty', 'tx'))
- grad_weight_two: float32 [1152, 128], P(('ty', 'tx'))
- grad_weight_three: float32 [1152, 256], P(('ty', 'tx'))
The draws below stay inside these ranges and needn't reach their ends.
Inputs may be any that keep to these rules, and one draw needn't show every extreme that they name: `noise_index`: a row of noise_table.
All inputs are finite; a program needn't handle non-finite values.
Results may differ from the reference program's by a relative error of at most 0.017.
Values may be sent and summed in bfloat16 or wider, within the bound.
No kernel may reach another device: no remote copies, remote signals or barrier semaphores. Data moves between devices by JAX's collectives and lax.ppermute only.
A program may use at most 128 MiB of HBM per device.

```python
import math
import jax
import jax.numpy as jnp
from jax import lax

C1 = 128
C3 = 256
NOISE_LEVELS = 64
H1 = 768
W1 = 1024
H3 = 192
W3 = 256


def steps_of(own_key, dims, shards, smallest, high):
    level = 1.0
    for axis_at, shards_of in shards:
        draws = jax.random.uniform(jax.random.fold_in(jax.random.fold_in(own_key, 6), axis_at), (shards_of,), jnp.float32, smallest / len(shards), high / len(shards))
        level = level * jnp.repeat(jnp.exp(draws), dims[axis_at] // shards_of).reshape((-1,) + (1,) * (len(dims) - 1 - axis_at))
    return level


def noise(stream_key, extent, spread, most, pieces=(), kind=jnp.bfloat16):
    entries = jax.random.normal(stream_key, extent, jnp.float32) * spread
    if len(pieces) > 0:
        entries = steps_of(stream_key, extent, pieces, -0.22, 0.18) * entries
    return jnp.clip(entries, min=-most, max=most).astype(kind)


def setup_inputs(seed: int = 0) -> dict:
    key_of = jax.random.split(jax.random.key(seed), 10)
    inputs = noise(key_of[0], (H1, W1, C1), 1.0, 6.0, ((0, 16), (1, 8)))
    weight_one = noise(key_of[1], (9 * C1, C1), (9 * C1) ** -0.5, 0.1875)
    weight_two = noise(key_of[2], (9 * C1, C1), (9 * C1) ** -0.5, 0.1875)
    weight_three = noise(key_of[3], (9 * C1, C3), (9 * C1) ** -0.5, 0.1875)
    noise_table = noise(key_of[4], (NOISE_LEVELS, 2 * C1), 0.3, 1.5, (), jnp.float32)
    frequency = jnp.clip(jnp.exp(jax.random.uniform(key_of[5], (2, C1), jnp.float32, math.log(0.002), math.log(0.3))), 0.002, 0.3)
    anchor = jax.random.randint(key_of[6], (2,), 0, 2049).astype(jnp.int32)
    noise_index = jax.random.randint(key_of[7], (1,), 0, NOISE_LEVELS).astype(jnp.int32)
    cotangent = noise(key_of[8], (H3, W3, C3), 1.0, 6.0, ((0, 16), (1, 8)))
    return {"inputs": inputs, "weight_one": weight_one, "weight_two": weight_two, "weight_three": weight_three, "noise_table": noise_table, "frequency": frequency, "anchor": anchor, "noise_index": noise_index, "cotangent": cotangent}


def conv_plain(field, weight):
    kernel = weight.reshape(3, 3, field.shape[2], weight.shape[1])
    return lax.conv_general_dilated(field[None], kernel, (1, 1), ((1, 1), (1, 1)), dimension_numbers=('NHWC', 'HWIO', 'NHWC'), precision=lax.Precision.HIGHEST)[0]

def shrink(field):
    height, width, depth = field.shape
    return field.astype(jnp.float32).reshape(height // 2, 2, width // 2, 2, depth).mean(axis=(1, 3))

def enlarge(grad):
    return jnp.repeat(jnp.repeat(grad, 2, axis=0), 2, axis=1) * 0.25

def dsilu(value):
    sigma = jax.nn.sigmoid(value)
    return sigma * (1.0 + value * (1.0 - sigma))

def reference(inputs, weight_one, weight_two, weight_three, noise_table, frequency, anchor, noise_index, cotangent):
    height, width, depth = inputs.shape
    row_pos = (anchor[0] + jnp.arange(height, dtype=jnp.int32)).astype(jnp.float32)
    col_pos = (anchor[1] + jnp.arange(width, dtype=jnp.int32)).astype(jnp.float32)
    angle = row_pos[:, None, None] * frequency[0] + col_pos[None, :, None] * frequency[1]
    first = (inputs.astype(jnp.float32) + jnp.sin(angle)).astype(jnp.bfloat16)
    modulate = noise_table[noise_index[0]]
    scale_term = 1.0 + modulate[:depth]
    shift_term = modulate[depth:]
    pre_one, pull_one = jax.vjp(conv_plain, first.astype(jnp.float32), weight_one.astype(jnp.float32))
    gate_one = pre_one * scale_term + shift_term
    act_one = jax.nn.silu(gate_one).astype(jnp.bfloat16)
    down_one = shrink(act_one).astype(jnp.bfloat16)
    pre_two, pull_two = jax.vjp(conv_plain, down_one.astype(jnp.float32), weight_two.astype(jnp.float32))
    act_two = (down_one.astype(jnp.float32) + jax.nn.silu(pre_two)).astype(jnp.bfloat16)
    down_two = shrink(act_two).astype(jnp.bfloat16)
    pre_three, pull_three = jax.vjp(conv_plain, down_two.astype(jnp.float32), weight_three.astype(jnp.float32))
    coarse_out = jax.nn.silu(pre_three).astype(jnp.bfloat16)
    grad_three = (cotangent.astype(jnp.float32) * dsilu(pre_three)).astype(jnp.bfloat16)
    back_two, grad_weight_three = pull_three(grad_three.astype(jnp.float32))
    grad_act_two = enlarge(back_two)
    grad_two = (grad_act_two * dsilu(pre_two)).astype(jnp.bfloat16)
    back_one, grad_weight_two = pull_two(grad_two.astype(jnp.float32))
    grad_act_one = enlarge(grad_act_two + back_one)
    grad_one = (grad_act_one * dsilu(gate_one) * scale_term).astype(jnp.bfloat16)
    back_input, grad_weight_one = pull_one(grad_one.astype(jnp.float32))
    grad_inputs = back_input.astype(jnp.bfloat16)
    return (coarse_out, grad_inputs, grad_weight_one, grad_weight_two, grad_weight_three)
```

```python
import jax
import jax.numpy as jnp
from jax import lax
from jax.sharding import PartitionSpec as P


def padded_2(array, sides, width):
    for axis, dim in sides:
        devices, length = (lax.axis_size(axis), array.shape[dim])
        up = [(i, (i + 1) % devices) for i in range(devices - 1)]
        down = [(j, i) for i, j in up]
        last = lax.slice_in_dim(array, length - width, length, axis=dim)
        first = lax.slice_in_dim(array, 0, width, axis=dim)
        before = lax.ppermute(last, axis, up)
        after = lax.ppermute(first, axis, down)
        array = jnp.concatenate([before, array, after], axis=dim)
    return array


def window(padded, shift_row, shift_col, rows, cols, offset):
    return padded[
        offset + shift_row : offset + shift_row + rows,
        offset + shift_col : offset + shift_col + cols,
    ]


def conv_shifted(padded, weight, rows, cols, offset):
    inner = padded.shape[2]
    total = jnp.zeros((rows, cols, weight.shape[1]), jnp.float32)
    for shift_row in range(3):
        for shift_col in range(3):
            block = 3 * shift_row + shift_col
            total = total + jnp.dot(
                window(padded, shift_row, shift_col, rows, cols, offset),
                weight[block * inner : (block + 1) * inner],
                preferred_element_type=jnp.float32,
            )
    return total


def weight_local(padded, grad, offset):
    rows, cols = (grad.shape[0], grad.shape[1])
    blocks = []
    for shift_row in range(3):
        for shift_col in range(3):
            view = window(padded, shift_row, shift_col, rows, cols, offset)
            blocks.append(
                lax.dot_general(
                    view, grad, (((0, 1), (0, 1)), ((), ())), preferred_element_type=jnp.float32
                )
            )
    return jnp.concatenate(blocks, axis=0)


def flipped(weight):
    inner = weight.shape[0] // 9
    return (
        weight.reshape(9, inner, weight.shape[1])[::-1]
        .transpose(0, 2, 1)
        .reshape(9 * weight.shape[1], inner)
    )


def shrink(field):
    height, width, depth = field.shape
    return field.astype(jnp.float32).reshape(height // 2, 2, width // 2, 2, depth).mean(axis=(1, 3))


def enlarge(grad):
    return jnp.repeat(jnp.repeat(grad, 2, axis=0), 2, axis=1) * 0.25


def dsilu(value):
    sigma = jax.nn.sigmoid(value)
    return sigma * (1.0 + value * (1.0 - sigma))


def fine_rims(field):
    return padded_2(field, (("ty", 0), ("tx", 1)), 1)


def coarse_rims(field):
    return padded_2(field, (("ty", 0), ("tx", 1)), 1)


def by_owner(term):
    owners = lax.axis_size("ty") * lax.axis_size("tx")
    return term.astype(jnp.bfloat16).reshape(owners, -1)


def summed(pieces):
    return pieces.astype(jnp.float32).sum(axis=0)


def owned_one_step(term):
    parts = by_owner(term)
    got = lax.all_to_all(parts, ("ty", "tx"), 0, 0, tiled=True)
    return summed(got).reshape(-1, term.shape[1])


def owned_two_steps(term):
    rows, cols = (lax.axis_size("ty"), lax.axis_size("tx"))
    parts = by_owner(term).reshape(rows, cols, -1)
    got = lax.all_to_all(parts, "ty", 0, 0, tiled=True)
    line = summed(got).astype(jnp.bfloat16)
    got = lax.all_to_all(line, "tx", 0, 0, tiled=True)
    return summed(got).reshape(-1, term.shape[1])


def owned_scatter(term):
    parts = by_owner(term)
    line = lax.psum_scatter(parts, "ty", scatter_dimension=0, tiled=True)
    got = lax.all_to_all(line, "tx", 0, 0, tiled=True)
    return summed(got).reshape(-1, term.shape[1])


def body(
    inputs,
    weight_one,
    weight_two,
    weight_three,
    noise_table,
    frequency,
    anchor,
    noise_index,
    cotangent,
):
    tile_rows, tile_cols, depth = inputs.shape
    row_pos = (
        anchor[0] + lax.axis_index("ty") * tile_rows + jnp.arange(tile_rows, dtype=jnp.int32)
    ).astype(jnp.float32)
    col_pos = (
        anchor[1] + lax.axis_index("tx") * tile_cols + jnp.arange(tile_cols, dtype=jnp.int32)
    ).astype(jnp.float32)
    angle = row_pos[:, None, None] * frequency[0] + col_pos[None, :, None] * frequency[1]
    first = (inputs.astype(jnp.float32) + jnp.sin(angle)).astype(jnp.bfloat16)
    modulate = lax.dynamic_index_in_dim(noise_table, noise_index[0], 0, keepdims=False)
    scale_term = 1.0 + modulate[:depth]
    shift_term = modulate[depth:]
    mid_rows, mid_cols = (tile_rows // 2, tile_cols // 2)
    padded_first = fine_rims(first)
    first_offset = 0
    gate_one = (
        conv_shifted(padded_first, weight_one, tile_rows, tile_cols, 0) * scale_term + shift_term
    )
    act_one = jax.nn.silu(gate_one).astype(jnp.bfloat16)
    down_one = shrink(act_one).astype(jnp.bfloat16)
    padded_down = fine_rims(down_one)
    pre_two = conv_shifted(padded_down, weight_two, mid_rows, mid_cols, 0)
    act_two = (down_one.astype(jnp.float32) + jax.nn.silu(pre_two)).astype(jnp.bfloat16)
    down_two = shrink(act_two).astype(jnp.bfloat16)
    low_rows, low_cols = (down_two.shape[0], down_two.shape[1])
    padded_low = coarse_rims(down_two)
    pre_three = conv_shifted(padded_low, weight_three, low_rows, low_cols, 0)
    coarse_out = jax.nn.silu(pre_three).astype(jnp.bfloat16)
    grad_three = (cotangent.astype(jnp.float32) * dsilu(pre_three)).astype(jnp.bfloat16)
    term_three = weight_local(padded_low, grad_three, 0)
    back_two = conv_shifted(coarse_rims(grad_three), flipped(weight_three), low_rows, low_cols, 0)
    grad_act_two = enlarge(back_two)
    grad_two = (grad_act_two * dsilu(pre_two)).astype(jnp.bfloat16)
    term_two = weight_local(padded_down, grad_two, 0)
    back_one = conv_shifted(fine_rims(grad_two), flipped(weight_two), mid_rows, mid_cols, 0)
    grad_act_one = enlarge(grad_act_two + back_one)
    grad_one = (grad_act_one * dsilu(gate_one) * scale_term).astype(jnp.bfloat16)
    term_one = weight_local(padded_first, grad_one, first_offset)
    back_input = conv_shifted(fine_rims(grad_one), flipped(weight_one), tile_rows, tile_cols, 0)
    grad_inputs = back_input.astype(jnp.bfloat16)
    grad_weight_one = owned_scatter(term_one)
    grad_weight_two = owned_two_steps(term_two)
    grad_weight_three = owned_one_step(term_three)
    return (coarse_out, grad_inputs, grad_weight_one, grad_weight_two, grad_weight_three)


def solution(mesh):
    placed = (P("ty", "tx", None), P(), P(), P(), P(), P(), P(), P(), P("ty", "tx", None))
    return jax.shard_map(
        body,
        mesh=mesh,
        in_specs=placed,
        out_specs=(
            P("ty", "tx", None),
            P("ty", "tx", None),
            P(("ty", "tx"), None),
            P(("ty", "tx"), None),
            P(("ty", "tx"), None),
        ),
        check_vma=False,
    )
```

```python
import jax
import jax.numpy as jnp
from jax import lax
from jax.experimental import pallas as pl
from jax.experimental.pallas import tpu as pltpu
from jax.sharding import PartitionSpec as P

BF16 = jnp.bfloat16
F32 = jnp.float32

KO = 32
KP = 40
HALO = 16
ROWS = 48
PAD_ROWS = ROWS + 2 * HALO
PAIRS = PAD_ROWS // 2
LOWS = PAIRS // 2
VMEM_LIMIT = 60 * 1024 * 1024


def any_spec():
    return pl.BlockSpec(memory_space=pl.ANY)


def vmem_spec():
    return pl.BlockSpec(memory_space=pltpu.VMEM)


def smem_spec():
    return pl.BlockSpec(memory_space=pltpu.SMEM)


def pack_kernel(inputs, cot, down, up, right, left, side32):
    last = pl.ds(ROWS - HALO, HALO)
    first = pl.ds(0, HALO)
    body = pl.ds(0, HALO)
    down[body] = inputs[last]
    up[body] = inputs[first]
    for target, start in ((down, 10), (up, 0)):
        for r in range(2):
            for h in range(2):
                target[HALO, pl.ds((r * 2 + h) * 2, 2)] = cot[start + r, :, h * 128 : (h + 1) * 128].reshape(2, 16, 128)
    for target, unit, start in ((right, 7, 30), (left, 0, 0)):
        for r in range(12):
            line = cot[r].astype(F32)
            for h in range(2):
                side32[pl.ds(r * 4 + h * 2, 2)] = line[start : start + 2, h * 128 : (h + 1) * 128]
        side = side32[...].astype(BF16).reshape(3, 16, 128)
        target[pl.ds(1, ROWS)] = inputs[:, unit]
        target[pl.ds(0, 1)] = side[0:1]
        target[pl.ds(1 + ROWS, 3)] = side


def pack(inputs, cot):
    shapes = [(HALO + 1, 8, 16, 128)] * 2 + [(ROWS + 4, 16, 128)] * 2
    return pl.pallas_call(
        pack_kernel,
        out_shape=[jax.ShapeDtypeStruct(s, BF16) for s in shapes],
        in_specs=[vmem_spec()] * 2,
        out_specs=[vmem_spec()] * 4,
        scratch_shapes=[pltpu.VMEM((48, 128), F32)],
        compiler_params=pltpu.CompilerParams(vmem_limit_bytes=VMEM_LIMIT // 4),
        name="pack_halos",
    )(inputs.reshape(ROWS, 8, 16, 128), cot)


def prep_kernel(grid_rows, grid_cols, place, frequency, w1, w2, w3, w1t, w1b, w2t, w2b, w3b, rows_sc, cols_sc):
    zero = jnp.zeros((128, 128), BF16)
    for source, ahead, back in ((w1, w1t, w1b), (w2, w2t, w2b)):
        for u in range(3):
            for v in range(3):
                tap = source[pl.ds((3 * u + v) * 128, 128), :]
                turned = tap.astype(F32).T.astype(BF16)
                for i in range(2):
                    ahead[pl.ds((4 * u + v + i) * 128, 128), i * 128 : (i + 1) * 128] = tap
                    back[pl.ds((4 * (2 - u) + 2 - v + i) * 128, 128), i * 128 : (i + 1) * 128] = turned
            for target in (ahead, back):
                target[pl.ds((4 * u + 3) * 128, 128), 0:128] = zero
                target[pl.ds(4 * u * 128, 128), 128:256] = zero
    for u in range(3):
        for v in range(3):
            for h in range(2):
                tap = w3[pl.ds((3 * u + v) * 128, 128), h * 128 : (h + 1) * 128]
                at = (3 * (2 - u) + 2 - v) * 256 + h * 128
                w3b[pl.ds(at, 128), :] = tap.astype(F32).T.astype(BF16)
    row = lax.broadcasted_iota(jnp.int32, (PAD_ROWS, 128), 0) - HALO + place[0] * ROWS
    angle = (row + place[2]).astype(F32) * frequency[0:1, :]
    keep = jnp.where((row >= 0) & (row < grid_rows), 1.0, 0.0)
    rows_sc[0] = jnp.sin(angle) * keep
    rows_sc[1] = jnp.cos(angle) * keep
    for p in range(4):
        k = lax.broadcasted_iota(jnp.int32, (KP, 128), 0)
        col = 4 * jnp.where(k < KO + 4, k, k - KP) + p + place[1] * (4 * KO)
        angle = (col + place[3]).astype(F32) * frequency[1:2, :]
        keep = jnp.where((col >= 0) & (col < grid_cols), 1.0, 0.0)
        cols_sc[0, p] = jnp.sin(angle) * keep
        cols_sc[1, p] = jnp.cos(angle) * keep


def prep(grid_rows, grid_cols, place, frequency, w1, w2, w3):
    def kernel(*refs):
        prep_kernel(grid_rows, grid_cols, *refs)

    wide = jax.ShapeDtypeStruct((1536, 256), BF16)
    return pl.pallas_call(
        kernel,
        out_shape=[
            wide,
            wide,
            wide,
            wide,
            jax.ShapeDtypeStruct((2304, 128), BF16),
            jax.ShapeDtypeStruct((2, PAD_ROWS, 128), F32),
            jax.ShapeDtypeStruct((2, 4, KP, 128), F32),
        ],
        in_specs=[smem_spec()] + [vmem_spec()] * 4,
        out_specs=[vmem_spec()] * 7,
        compiler_params=pltpu.CompilerParams(vmem_limit_bytes=VMEM_LIMIT),
        name="prepare_weights",
    )(place, frequency, w1, w2, w3)


def stacked(one, two):
    return jnp.concatenate([one[:KO], two[:KO], one[KO:], two[KO:]], axis=0)


def folded(pair):
    return jnp.concatenate([pair[:32] + pair[32:64], pair[64:72] + pair[72:80]], axis=0)


def line_of(pair, s):
    return jnp.concatenate([pair[32 * s : 32 * s + 32], pair[64 + 8 * s : 72 + 8 * s]], axis=0)


def doubled(line):
    return stacked(line, line)


def before(line):
    return pltpu.roll(line, 1, 0)


def after(line):
    return pltpu.roll(line, KP - 1, 0)


def sigmoid(value):
    return 0.5 * jnp.tanh(0.5 * value) + 0.5


def rounded(value):
    return value.astype(BF16).astype(F32)


def lines_kernel(
    low_rows, low_cols,
    place, inputs, cot, top, bot, lef, rig, ctop, cbot,
    w1t, w2t, w2b, w3, w3b, rows_sc, cols_sc, noise,
    coarse, g1p_out, g1s_out, keep_msg, give_msg,
    pf, sf, stage, held, d1, xm, p2, s2, d2, xl, p3, s3, cp, side32, xg3, g3p, g3s, xb2, xg2, g2p, g2s, xt,
    g1p, g1s, held1, acc, acc3, gw, ms, mask, sems,
):
    k = lax.broadcasted_iota(jnp.int32, (KP, 128), 0)
    col = jnp.where(k < KO + 4, k, k - KP) + place[1] * KO
    inside = jnp.where((col >= 0) & (col < low_cols), 1.0, 0.0)

    def mask_step(at, _):
        row = at - 4 + place[0] * 12
        mask[at] = inside * jnp.where((row >= 0) & (row < low_rows), 1.0, 0.0)
        return 0

    lax.fori_loop(0, LOWS, mask_step, 0)
    modulate = noise[pl.ds(place[4], 1), :]
    scale = 1.0 + modulate[:, 0:128]
    shift = modulate[:, 128:256]

    def first_step(load, base, q, _):
        lines = []
        for i in range(4):
            row = 4 * q + i
            own, right, left = load(row)
            stage[i, 0:128] = own.astype(F32)
            stage[i, 128:144] = right.astype(F32)
            stage[i, 144:160] = left.astype(F32)
            sin_row = rows_sc[0, pl.ds(base + row, 1), :]
            cos_row = rows_sc[1, pl.ds(base + row, 1), :]
            planes = []
            for p in range(4):
                value = stage[i, pl.ds(p, KP, stride=4), :]
                planes.append(value + (sin_row * cols_sc[1, p] + cos_row * cols_sc[0, p]))
            lines.append([before(planes[3])] + planes + [after(planes[0])])
        at = base // 2 + 2 * q
        for j in range(6):
            lanes = slice(j * 128, (j + 1) * 128)
            sf[at, :, lanes] = stacked(held[j], lines[0][j]).astype(BF16)
            pf[at, :, lanes] = stacked(lines[0][j], lines[1][j]).astype(BF16)
            sf[at + 1, :, lanes] = stacked(lines[1][j], lines[2][j]).astype(BF16)
            pf[at + 1, :, lanes] = stacked(lines[2][j], lines[3][j]).astype(BF16)
            held[j] = lines[3][j]
        return 0

    def flat(block):
        return block.reshape(128, 128)

    held[...] = jnp.zeros_like(held)
    load_top = lambda r: (flat(top[r]), ctop[19 + r], ctop[r])
    load_own = lambda r: (flat(inputs[r]), rig[1 + r], lef[1 + r])
    load_bot = lambda r: (flat(bot[r]), cbot[18 + r], cbot[1 + r])
    lax.fori_loop(0, 4, lambda q, c: first_step(load_top, 0, q, c), 0)
    lax.fori_loop(0, 12, lambda q, c: first_step(load_own, HALO, q, c), 0)
    lax.fori_loop(0, 4, lambda q, c: first_step(load_bot, HALO + ROWS, q, c), 0)

    def around(s_ref, p_ref, at, count, lanes, lo=0, hi=80):
        parts = [
            s_ref[pl.ds(at, count), lo:hi, lanes],
            p_ref[pl.ds(at, count), lo:hi, lanes],
            s_ref[pl.ds(at + 1, count), lo:hi, lanes],
        ]
        rows = count * (hi - lo)
        return jnp.concatenate([part.reshape(rows, part.shape[-1]) for part in parts], axis=1)

    def conv_one_step(t, _):
        m = 1 + 2 * t
        one = around(sf, pf, m, 2, slice(0, 512))
        two = around(sf, pf, m, 2, slice(256, 768))
        total = jnp.dot(jnp.concatenate([one, two], axis=0), w1t[...], preferred_element_type=F32)
        for s in range(2):
            folds = []
            for p in range(4):
                at = (p // 2) * 160 + s * 80
                gate = total[at : at + 80, (p % 2) * 128 : (p % 2 + 1) * 128] * scale + shift
                sigma = sigmoid(gate)
                act = gate * sigma
                d1[m + s, :, p * 128 : (p + 1) * 128] = scale * (sigma + act * (1.0 - sigma))
                folds.append(folded(rounded(act)))
            keep = 0.25 * mask[(m + s) // 2]
            xm[m + s, 0] = rounded((folds[0] + folds[1]) * keep)
            xm[m + s, 1] = rounded((folds[2] + folds[3]) * keep)
        return 0

    lax.fori_loop(0, 19, conv_one_step, 0)

    def lines_four(x_ref, s_ref, p_ref, j, _):
        lines = []
        for i in range(3):
            zero, one = x_ref[2 * j - 1 + i, 0], x_ref[2 * j - 1 + i, 1]
            lines.append([before(one), zero, one, after(zero)])
        for n in range(4):
            lanes = slice(n * 128, (n + 1) * 128)
            s_ref[j, :, lanes] = stacked(lines[0][n], lines[1][n]).astype(BF16)
            p_ref[j, :, lanes] = stacked(lines[1][n], lines[2][n]).astype(BF16)
        return 0

    xm[39] = jnp.zeros((2, KP, 128), F32)
    lax.fori_loop(1, 20, lambda j, c: lines_four(xm, s2, p2, j, c), 0)

    def conv_two_step(t, _):
        j = 1 + 6 * t
        total = jnp.dot(around(s2, p2, j, 6, slice(0, 512)), w2t[...], preferred_element_type=F32)
        for s in range(6):
            folds = []
            for q in range(2):
                pre = total[s * 80 : (s + 1) * 80, q * 128 : (q + 1) * 128]
                sigma = sigmoid(pre)
                act = pre * sigma
                d2[j + s, :, q * 128 : (q + 1) * 128] = sigma + act * (1.0 - sigma)
                down = p2[j + s, :, (q + 1) * 128 : (q + 2) * 128].astype(F32)
                folds.append(folded(rounded(down + act)))
            xl[j + s] = rounded((folds[0] + folds[1]) * (0.25 * mask[j + s]))
        return 0

    lax.fori_loop(0, 3, conv_two_step, 0)

    xl[19] = jnp.zeros((KP, 128), F32)

    def lines_three(x_ref, s_ref, p_ref, width, i, _):
        lines = []
        for n in range(3):
            line = x_ref[2 * i - 1 + n]
            lines.append([before(line), line, after(line)])
        for n in range(3):
            lanes = slice(n * width, (n + 1) * width)
            s_ref[i, :, lanes] = stacked(lines[0][n], lines[1][n]).astype(BF16)
            p_ref[i, :, lanes] = stacked(lines[1][n], lines[2][n]).astype(BF16)
        return 0

    lax.fori_loop(1, 10, lambda i, c: lines_three(xl, s3, p3, 128, i, c), 0)

    cp[...] = jnp.zeros_like(cp)
    for h in range(2):
        lanes = slice(h * 128, (h + 1) * 128)
        for r in range(2):
            units = pl.ds((r * 2 + h) * 2, 2)
            cp[r, 0:KO, lanes] = top[HALO, units].reshape(KO, 128).astype(F32)
            cp[14 + r, 0:KO, lanes] = bot[HALO, units].reshape(KO, 128).astype(F32)
    for r in range(12):
        cp[2 + r, 0:KO, :] = cot[r].astype(F32)
    for ref, at in ((rig, KO), (lef, KP - 2)):
        side32[...] = ref[pl.ds(ROWS + 1, 3)].reshape(48, 128).astype(F32)
        for h in range(2):
            for r in range(12):
                cp[2 + r, at : at + 2, h * 128 : (h + 1) * 128] = side32[r * 4 + h * 2 : r * 4 + h * 2 + 2]
    for ref, unit, skip, row, at in (
        (ctop, 18, 8, 0, KP - 2),
        (ctop, 37, 8, 0, KO),
        (cbot, 0, 0, 14, KP - 2),
        (cbot, 17, 0, 14, KO),
    ):
        side32[0:16] = ref[unit].astype(F32)
        for h in range(2):
            for r in range(2):
                start = skip + r * 4 + h * 2
                cp[row + r, at : at + 2, h * 128 : (h + 1) * 128] = side32[start : start + 2]

    def conv_three_step(t, _):
        i = 1 + 4 * t
        total = jnp.dot(around(s3, p3, i, 4, slice(0, 384)), w3[...], preferred_element_type=F32)
        for s in range(4):
            pre = total[s * 80 : (s + 1) * 80]
            sigma = sigmoid(pre)
            act = pre * sigma
            slope = sigma + act * (1.0 - sigma)
            for r in range(2):
                row = 2 * (i + s) + r
                keep = mask[row]
                xg3[row] = cp[row - 2] * line_of(slope, r) * jnp.concatenate([keep, keep], axis=1)

                @pl.when((row >= 4) & (row < 16))
                def _():
                    coarse[row - 4] = act[32 * r : 32 * r + 32].astype(BF16)
        return 0

    lax.fori_loop(0, 2, conv_three_step, 0)
    empty = jnp.zeros((KP, 256), F32)
    xg3[1] = empty
    xg3[18] = empty
    xg3[19] = empty
    lax.fori_loop(1, 10, lambda i, c: lines_three(xg3, g3s, g3p, 256, i, c), 0)

    def weight_terms(grad, field):
        return lax.dot_general(grad, field, (((0,), (0,)), ((), ())), preferred_element_type=F32)

    acc3[...] = weight_terms(
        g3p[2:8, 0:64, 256:512].reshape(384, 256), around(s3, p3, 2, 6, slice(0, 384), 0, 64)
    )

    def back_three_step(t, _):
        i = 1 + 4 * t
        total = jnp.dot(around(g3s, g3p, i, 4, slice(0, 768)), w3b[...], preferred_element_type=F32)
        for s in range(4):
            for r in range(2):
                xb2[2 * (i + s) + r] = 0.25 * line_of(total[s * 80 : (s + 1) * 80], r)
        return 0

    lax.fori_loop(0, 2, back_three_step, 0)

    def grad_two_step(j, _):
        slope = xb2[j] * mask[j]
        for s in range(2):
            for q in range(2):
                d = d2[j, :, q * 128 : (q + 1) * 128]
                xg2[2 * j + s, q] = slope * line_of(d, s)
        return 0

    lax.fori_loop(3, 17, grad_two_step, 0)
    blank = jnp.zeros((2, KP, 128), F32)
    xg2[5] = blank
    xg2[34] = blank
    xg2[35] = blank
    lax.fori_loop(3, 18, lambda j, c: lines_four(xg2, g2s, g2p, j, c), 0)

    def fold_weights(at, taps):
        for u in range(3):
            for v in range(3):
                left = (4 * u + v) * 128
                term = acc[0:128, left : left + 128] + acc[128:256, left + 128 : left + 256]
                gw[at, pl.ds((3 * u + v) * 128, 128), :] = term.T

    acc[...] = weight_terms(
        g2p[4:16, 0:64, 128:384].reshape(768, 256), around(s2, p2, 4, 12, slice(0, 512), 0, 64)
    )
    fold_weights(1, None)

    def back_two_step(t, _):
        j = 3 + 7 * t
        total = jnp.dot(around(g2s, g2p, j, 7, slice(0, 512)), w2b[...], preferred_element_type=F32)
        for s in range(7):
            keep = 0.25 * mask[j + s]
            base = xb2[j + s]
            for q in range(2):
                pair = total[s * 80 : (s + 1) * 80, q * 128 : (q + 1) * 128]
                for r in range(2):
                    xt[2 * (j + s) + r, q] = (base + line_of(pair, r)) * keep
        return 0

    lax.fori_loop(0, 2, back_two_step, 0)

    def grad_line(m, s):
        planes = [xt[m, p // 2] * line_of(d1[m, :, p * 128 : (p + 1) * 128], s) for p in range(4)]
        lines = [before(planes[3])] + planes + [after(planes[0])]
        return [line[:KO] for line in lines]

    first_held = grad_line(7, 1)
    for n in range(6):
        held1[n] = first_held[n]

    def grad_one_step(at, _):
        m = at + 8
        even, odd = grad_line(m, 0), grad_line(m, 1)
        for n in range(6):
            lanes = slice(n * 128, (n + 1) * 128)
            g1s[at, :, lanes] = jnp.concatenate([held1[n], even[n]], axis=0).astype(BF16)
            g1p[at, :, lanes] = jnp.concatenate([even[n], odd[n]], axis=0).astype(BF16)
            held1[n] = odd[n]
        return 0

    lax.fori_loop(0, 25, grad_one_step, 0)
    copies = [
        pltpu.make_async_copy(g1p.at[pl.ds(0, 24)], g1p_out, sems.at[0]),
        pltpu.make_async_copy(g1s, g1s_out, sems.at[1]),
    ]
    for copy in copies:
        copy.start()

    acc[...] = jnp.zeros_like(acc)

    def weight_one_step(t, _):
        at = 8 * t
        grads = jnp.concatenate(
            [g1p[pl.ds(at, 8), :, lanes].reshape(512, 256) for lanes in (slice(128, 384), slice(384, 640))], axis=0
        )
        fields = jnp.concatenate(
            [around(sf, pf, at + 8, 8, lanes, 0, 64) for lanes in (slice(0, 512), slice(256, 768))], axis=0
        )
        acc[...] += weight_terms(grads, fields)
        return 0

    lax.fori_loop(0, 3, weight_one_step, 0)
    fold_weights(0, None)
    for tap in range(9):
        turned = acc3[:, tap * 128 : (tap + 1) * 128].T
        gw[2, pl.ds(tap * 128, 128), :] = turned[:, 0:128]
        gw[3, pl.ds(tap * 128, 128), :] = turned[:, 128:256]
    for n in range(10):
        for t in range(4):
            piece = gw[t, pl.ds(n, 128, stride=9), :] if n < 9 else jnp.zeros((128, 128), F32)
            ms[pl.ds(4 * n + t, 128, stride=40), :] = piece

    core = lax.rem(place[0], 2)

    def msg_step(n, _):
        rows = pl.ds(pl.multiple_of(n * 320, 320), 320)
        keep_msg[rows, :] = ms[pl.ds(pl.multiple_of((2 * n + core) * 320, 320), 320), :].astype(BF16)
        give_msg[rows, :] = ms[pl.ds(pl.multiple_of((2 * n + 1 - core) * 320, 320), 320), :].astype(BF16)
        return 0

    lax.fori_loop(0, 8, msg_step, 0)
    for copy in copies:
        copy.wait()


def levels(low_rows, low_cols, *args):
    def kernel(*refs):
        lines_kernel(low_rows, low_cols, *refs)

    vm = pltpu.VMEM
    return pl.pallas_call(
        kernel,
        out_shape=[
            jax.ShapeDtypeStruct((12, KO, 256), BF16),
            jax.ShapeDtypeStruct((24, 64, 768), BF16),
            jax.ShapeDtypeStruct((25, 64, 768), BF16),
            jax.ShapeDtypeStruct((2560, 128), BF16),
            jax.ShapeDtypeStruct((2560, 128), BF16),
        ],
        in_specs=[smem_spec()] + [vmem_spec()] * (len(args) - 1),
        out_specs=[vmem_spec(), any_spec(), any_spec(), vmem_spec(), vmem_spec()],
        scratch_shapes=[
            vm((PAIRS, 80, 768), BF16),
            vm((PAIRS, 80, 768), BF16),
            vm((4, 160, 128), F32),
            vm((6, KP, 128), F32),
            vm((PAIRS, 80, 512), F32),
            vm((PAIRS, 2, KP, 128), F32),
            vm((LOWS, 80, 512), BF16),
            vm((LOWS, 80, 512), BF16),
            vm((LOWS, 80, 256), F32),
            vm((LOWS, KP, 128), F32),
            vm((10, 80, 384), BF16),
            vm((10, 80, 384), BF16),
            vm((16, KP, 256), F32),
            vm((48, 128), F32),
            vm((LOWS, KP, 256), F32),
            vm((10, 80, 768), BF16),
            vm((10, 80, 768), BF16),
            vm((LOWS, KP, 128), F32),
            vm((PAIRS, 2, KP, 128), F32),
            vm((LOWS, 80, 512), BF16),
            vm((LOWS, 80, 512), BF16),
            vm((PAIRS, 2, KP, 128), F32),
            vm((25, 64, 768), BF16),
            vm((25, 64, 768), BF16),
            vm((6, KO, 128), F32),
            vm((256, 1536), F32),
            vm((256, 1152), F32),
            vm((4, 1152, 128), F32),
            vm((5120, 128), F32),
            vm((LOWS, KP, 128), F32),
            pltpu.SemaphoreType.DMA((2,)),
        ],
        compiler_params=pltpu.CompilerParams(vmem_limit_bytes=VMEM_LIMIT),
        name="encoder_levels",
    )(*args)


def input_kernel(g1p, g1s, w1b, out, stage):
    def step(t, _):
        at = 2 * t
        halves = []
        for lanes in (slice(0, 512), slice(256, 768)):
            parts = [g1s[pl.ds(at, 2), :, lanes], g1p[pl.ds(at, 2), :, lanes], g1s[pl.ds(at + 1, 2), :, lanes]]
            halves.append(jnp.concatenate([part.reshape(128, 512) for part in parts], axis=1))
        total = jnp.dot(jnp.concatenate(halves, axis=0), w1b[...], preferred_element_type=F32)
        for r in range(4):
            for p in range(4):
                rows = (p // 2) * 128 + r * 32
                value = total[rows : rows + 32, (p % 2) * 128 : (p % 2 + 1) * 128]
                stage[r, pl.ds(p, 32, stride=4), :] = value
            out[4 * t + r] = stage[r].astype(BF16)
        return 0

    lax.fori_loop(0, 12, step, 0)


def input_grad(g1p, g1s, w1b):
    return pl.pallas_call(
        input_kernel,
        out_shape=jax.ShapeDtypeStruct((ROWS, 128, 128), BF16),
        in_specs=[vmem_spec()] * 3,
        out_specs=vmem_spec(),
        scratch_shapes=[pltpu.VMEM((4, 128, 128), F32)],
        compiler_params=pltpu.CompilerParams(vmem_limit_bytes=VMEM_LIMIT),
        cost_estimate=pl.CostEstimate(flops=2 * 6144 * 1152 * 128, bytes_accessed=8 * 1024 * 1024, transcendentals=0),
        name="input_grad",
    )(g1p, g1s, w1b)


def collect_kernel(got, one, two, three, total):
    total[...] = got[...].astype(F32).sum(axis=0)
    one[...] = total[pl.ds(0, 9, stride=4), :]
    two[...] = total[pl.ds(1, 9, stride=4), :]
    three[:, 0:128] = total[pl.ds(2, 9, stride=4), :]
    three[:, 128:256] = total[pl.ds(3, 9, stride=4), :]


def collect(got):
    return pl.pallas_call(
        collect_kernel,
        out_shape=[
            jax.ShapeDtypeStruct((9, 128), F32),
            jax.ShapeDtypeStruct((9, 128), F32),
            jax.ShapeDtypeStruct((9, 256), F32),
        ],
        in_specs=[vmem_spec()],
        out_specs=[vmem_spec()] * 3,
        scratch_shapes=[pltpu.VMEM((40, 128), F32)],
        name="collect_weights",
    )(got)


ROW_AXES = ("chip", "core")


def shifted(block, axis, step):
    devices = lax.axis_size(axis)
    pairs = [(i, i + step) for i in range(devices) if 0 <= i + step < devices]
    return lax.ppermute(block, axis, pairs)


def body(inputs, weight_one, weight_two, weight_three, noise_table, frequency, anchor, noise_index, cotangent):
    rows, cols = (lax.axis_size(ROW_AXES), lax.axis_size("tx"))
    place = jnp.concatenate(
        [jnp.stack([lax.axis_index(ROW_AXES), lax.axis_index("tx")]).astype(jnp.int32), anchor, noise_index]
    )
    down, up, right, left = pack(inputs, cotangent)
    lef = shifted(right, "tx", 1)
    rig = shifted(left, "tx", -1)
    top = shifted(down, ROW_AXES, 1)
    bot = shifted(up, ROW_AXES, -1)
    ctop = shifted(jnp.concatenate([lef[33:52], rig[33:52]], axis=0), ROW_AXES, 1)
    cbot = shifted(jnp.concatenate([lef[0:17], rig[0:17]], axis=0), ROW_AXES, -1)
    w1t, w1b, w2t, w2b, w3b, rows_sc, cols_sc = prep(
        rows * ROWS, cols * 4 * KO, place, frequency, weight_one, weight_two, weight_three
    )
    coarse, g1p, g1s, keep_msg, give_msg = levels(
        rows * 12, cols * KO,
        place, inputs.reshape(ROWS, 8, 16, 128), cotangent, top, bot, lef, rig, ctop, cbot,
        w1t, w2t, w2b, weight_three, w3b, rows_sc, cols_sc, noise_table,
    )
    other = lax.ppermute(give_msg, "core", [(0, 1), (1, 0)])
    msg = (keep_msg.astype(F32) + other.astype(F32)).astype(BF16).reshape(64, 40, 128)
    got = lax.all_to_all(msg, ("chip", "tx"), 0, 0, tiled=True)
    grad_inputs = input_grad(g1p, g1s, w1b)
    return (coarse, grad_inputs, *collect(got))


def solution(mesh):
    halves = jax.sharding.Mesh(mesh.devices.reshape(-1, 2, mesh.devices.shape[1]), ("chip", "core", "tx"))
    placed = (P(ROW_AXES, "tx", None), P(), P(), P(), P(), P(), P(), P(), P(ROW_AXES, "tx", None))
    return jax.shard_map(
        body,
        mesh=halves,
        in_specs=placed,
        out_specs=(
            P(ROW_AXES, "tx", None),
            P(ROW_AXES, "tx", None),
            P((*ROW_AXES, "tx"), None),
            P((*ROW_AXES, "tx"), None),
            P((*ROW_AXES, "tx"), None),
        ),
        check_vma=False,
    )
```

```python
import jax
import jax.numpy as jnp
from jax import lax
from jax.experimental import pallas as pl
from jax.experimental.pallas import tpu as pltpu
from jax.sharding import PartitionSpec as P

BF16 = jnp.bfloat16
F32 = jnp.float32

KO = 32
KP = 40
HALO = 16
ROWS = 48
PAD_ROWS = ROWS + 2 * HALO
PAIRS = PAD_ROWS // 2
LOWS = PAIRS // 2
VMEM_LIMIT = 60 * 1024 * 1024


def any_spec():
    return pl.BlockSpec(memory_space=pl.ANY)


def vmem_spec():
    return pl.BlockSpec(memory_space=pltpu.VMEM)


def smem_spec():
    return pl.BlockSpec(memory_space=pltpu.SMEM)


ROW_AXES = ("chip", "core")


def own_place():
    return lax.axis_index(ROW_AXES), lax.axis_index("tx")


def side_kernel(inputs, cot, right, left, cots, side32, sems):
    copies = [
        pltpu.make_async_copy(inputs.at[:, 7], right.at[pl.ds(1, ROWS)], sems.at[0]),
        pltpu.make_async_copy(inputs.at[:, 0], left.at[pl.ds(1, ROWS)], sems.at[1]),
    ]
    for copy in copies:
        copy.start()
    for target, start in ((right, 30), (left, 0)):
        for r in range(12):
            line = cot[r].astype(F32)
            for h in range(2):
                side32[pl.ds(r * 4 + h * 2, 2)] = line[start : start + 2, h * 128 : (h + 1) * 128]
        side = side32[...].astype(BF16).reshape(3, 16, 128)
        target[pl.ds(0, 1)] = side[0:1]
        target[pl.ds(1 + ROWS, 3)] = side
    for at, start in ((0, 10), (1, 0)):
        for r in range(2):
            for h in range(2):
                cots[at, pl.ds((r * 2 + h) * 2, 2)] = cot[start + r, :, h * 128 : (h + 1) * 128].reshape(2, 16, 128)
    for copy in copies:
        copy.wait()


def sides(inputs, cot):
    return pl.pallas_call(
        side_kernel,
        out_shape=[jax.ShapeDtypeStruct((ROWS + 4, 16, 128), BF16)] * 2 + [jax.ShapeDtypeStruct((2, 8, 16, 128), BF16)],
        in_specs=[any_spec(), vmem_spec()],
        out_specs=[vmem_spec()] * 3,
        scratch_shapes=[pltpu.VMEM((48, 128), F32), pltpu.SemaphoreType.DMA((2,))],
        name="pack_columns",
    )(inputs, cot)


def rim(inputs, cots, lef, rig, row, cot_unit):
    sides = [side[1 + row : 3 + row, None] for side in (rig, lef)]
    cells = jnp.concatenate([inputs[row : row + 2], *sides], axis=1)
    units = jnp.concatenate([cots, rig[cot_unit : cot_unit + 1], lef[cot_unit : cot_unit + 1]], axis=0)
    return jnp.concatenate([cells, units[None]], axis=0)


def weight_forms(w1, w2, w3, w1t, w1b, w2t, w2b, w3b):
    zero = jnp.zeros((128, 128), BF16)
    for source, ahead, back in ((w1, w1t, w1b), (w2, w2t, w2b)):
        for u in range(3):
            for v in range(3):
                tap = source[pl.ds((3 * u + v) * 128, 128), :]
                for i in range(2):
                    side = slice(i * 128, (i + 1) * 128)
                    ahead[pl.ds((4 * u + v + i) * 128, 128), side] = tap
                    at = (4 * (2 - u) + 2 - v + i) * 128
                    back[side, at : at + 128] = tap
            for i, j in ((0, 3), (1, 0)):
                at = (4 * u + j) * 128
                side = slice(i * 128, (i + 1) * 128)
                ahead[pl.ds(at, 128), side] = zero
                back[side, at : at + 128] = zero
    for u in range(3):
        for v in range(3):
            at = (3 * (2 - u) + 2 - v) * 256
            w3b[:, at : at + 256] = w3[pl.ds((3 * u + v) * 128, 128), :]


def wave_tables(grid_rows, grid_cols, anchor, frequency, rows_sc, cols_sc):
    own_row, own_col = own_place()
    row = lax.broadcasted_iota(jnp.int32, (PAD_ROWS, 128), 0) - HALO + own_row * ROWS
    angle = (row + anchor[0]).astype(F32) * frequency[0:1, :]
    keep = jnp.where((row >= 0) & (row < grid_rows), 1.0, 0.0)
    rows_sc[0] = jnp.sin(angle) * keep
    rows_sc[1] = jnp.cos(angle) * keep
    for p in range(4):
        k = lax.broadcasted_iota(jnp.int32, (KP, 128), 0)
        col = 4 * jnp.where(k < KO + 4, k, k - KP) + p + own_col * (4 * KO)
        angle = (col + anchor[1]).astype(F32) * frequency[1:2, :]
        keep = jnp.where((col >= 0) & (col < grid_cols), 1.0, 0.0)
        cols_sc[0, p] = jnp.sin(angle) * keep
        cols_sc[1, p] = jnp.cos(angle) * keep


def prep_kernel(grid_rows, grid_cols, anchor, w1, w2, w3, frequency, w1t, w1b, w2t, w2b, w3b, rows_sc, cols_sc):
    weight_forms(w1, w2, w3, w1t, w1b, w2t, w2b, w3b)
    wave_tables(grid_rows, grid_cols, anchor, frequency, rows_sc, cols_sc)


def prep(grid_rows, grid_cols, anchor, w1, w2, w3, frequency):
    def kernel(*refs):
        prep_kernel(grid_rows, grid_cols, *refs)

    shape = jax.ShapeDtypeStruct
    return pl.pallas_call(
        kernel,
        out_shape=[
            shape((1536, 256), BF16),
            shape((256, 1536), BF16),
            shape((1536, 256), BF16),
            shape((256, 1536), BF16),
            shape((128, 2304), BF16),
            shape((2, PAD_ROWS, 128), F32),
            shape((2, 4, KP, 128), F32),
        ],
        in_specs=[smem_spec()] + [vmem_spec()] * 4,
        out_specs=[vmem_spec()] * 7,
        compiler_params=pltpu.CompilerParams(vmem_limit_bytes=VMEM_LIMIT),
        name="weight_forms",
    )(anchor, w1, w2, w3, frequency)


def fill_mask(low_rows, low_cols, mask):
    own_row, own_col = own_place()
    k = lax.broadcasted_iota(jnp.int32, (KP, 128), 0)
    col = jnp.where(k < KO + 4, k, k - KP) + own_col * KO
    inside = jnp.where((col >= 0) & (col < low_cols), 1.0, 0.0)

    def step(at, _):
        row = at - 4 + own_row * 12
        mask[at] = inside * jnp.where((row >= 0) & (row < low_rows), 1.0, 0.0)
        return 0

    lax.fori_loop(0, LOWS, step, 0)


def stacked(one, two):
    return jnp.concatenate([one[:KO], two[:KO], one[KO:], two[KO:]], axis=0)


def folded(pair):
    return jnp.concatenate([pair[:32] + pair[32:64], pair[64:72] + pair[72:80]], axis=0)


def line_of(pair, s):
    return jnp.concatenate([pair[32 * s : 32 * s + 32], pair[64 + 8 * s : 72 + 8 * s]], axis=0)


def doubled(line):
    return stacked(line, line)


def before(line):
    return pltpu.roll(line, 1, 0)


def after(line):
    return pltpu.roll(line, KP - 1, 0)


def silu_parts(half):
    th = jnp.tanh(half)
    act = half + half * th
    return act, (1.0 + act) + th * (1.0 - act)


def rounded(value):
    return value.astype(BF16).astype(F32)


def flat(block):
    return block.reshape(128, 128)


def modulation(noise, noise_index):
    modulate = noise[pl.ds(noise_index[0], 1), :]
    return 1.0 + modulate[:, 0:128], modulate[:, 128:256]


def first_lines(load, base, at, tables, stage, held, sf, pf):
    rows_sc, cols_sc = tables
    lines = []
    for i in range(4):
        own, right, left = load(i)
        stage[i, 0:128] = own.astype(F32)
        stage[i, 128:144] = right.astype(F32)
        stage[i, 144:160] = left.astype(F32)
        sin_row = rows_sc[0, pl.ds(base + i, 1), :]
        cos_row = rows_sc[1, pl.ds(base + i, 1), :]
        planes = []
        for p in range(4):
            value = stage[i, pl.ds(p, KP, stride=4), :]
            planes.append(value + (sin_row * cols_sc[1, p] + cos_row * cols_sc[0, p]))
        lines.append([before(planes[3])] + planes + [after(planes[0])])
    for j in range(6):
        lanes = slice(j * 128, (j + 1) * 128)
        sf[at, :, lanes] = stacked(held[j], lines[0][j]).astype(BF16)
        pf[at, :, lanes] = stacked(lines[0][j], lines[1][j]).astype(BF16)
        sf[at + 1, :, lanes] = stacked(lines[1][j], lines[2][j]).astype(BF16)
        pf[at + 1, :, lanes] = stacked(lines[2][j], lines[3][j]).astype(BF16)
        held[j] = lines[3][j]


def around(s_ref, p_ref, at, count, lanes, lo=0, hi=80):
    parts = [
        s_ref[pl.ds(at, count), lo:hi, lanes],
        p_ref[pl.ds(at, count), lo:hi, lanes],
        s_ref[pl.ds(at + 1, count), lo:hi, lanes],
    ]
    rows = count * (hi - lo)
    return jnp.concatenate([part.reshape(rows, part.shape[-1]) for part in parts], axis=1)


def product(left, right):
    return jnp.dot(left, right, preferred_element_type=F32)


def product_turned(left, right):
    return lax.dot_general(left, right, (((1,), (1,)), ((), ())), preferred_element_type=F32)


def weight_terms(grad, field):
    return lax.dot_general(grad, field, (((0,), (0,)), ((), ())), preferred_element_type=F32)


def pipeline(steps, dot, post, z0, z1):
    def put(z, t):
        total = dot(t)
        z[0 : total.shape[0], :] = total

    put(z0, 0)

    def two(i, _):
        put(z1, 2 * i + 1)
        post(2 * i, z0)
        put(z0, 2 * i + 2)
        post(2 * i + 1, z1)
        return 0

    if steps > 2:
        lax.fori_loop(0, (steps - 1) // 2, two, 0)
    if steps % 2 == 0:
        put(z1, steps - 1)
        post(steps - 2, z0)
        post(steps - 1, z1)
    else:
        post(steps - 1, z0)


def conv_one_dot(sf, pf, m, w1t):
    one = around(sf, pf, m, 2, slice(0, 512))
    two = around(sf, pf, m, 2, slice(256, 768))
    return product(jnp.concatenate([one, two], axis=0), w1t[...])


def conv_one_post(z, scale, shift, keeps, xm, d1, at):
    for s in range(2):
        folds = []
        for p in range(4):
            rows = (p // 2) * 160 + s * 80
            half = z[rows : rows + 80, (p % 2) * 128 : (p % 2 + 1) * 128] * (0.5 * scale) + 0.5 * shift
            act, slope = silu_parts(half)
            d1[at + s, :, p * 128 : (p + 1) * 128] = (0.5 * scale) * slope
            folds.append(folded(rounded(act)))
        keep = 0.25 * keeps[s]
        xm[at + s, 0] = rounded((folds[0] + folds[1]) * keep)
        xm[at + s, 1] = rounded((folds[2] + folds[3]) * keep)


def own_kernel(
    grid_rows, grid_cols,
    noise_index, inputs, lef, rig, top, bot, w1t, rows_sc, cols_sc, noise,
    pf_out, sf_out, d1_out, xm_out, low_msg, high_msg,
    pf, sf, stage, held, d1, xm, mask, z0, z1, sems,
):
    fill_mask(grid_rows // 4, grid_cols // 4, mask)
    scale, shift = modulation(noise, noise_index)
    held[...] = jnp.zeros_like(held)

    def own(r):
        return flat(inputs[r]), rig[1 + r], lef[1 + r]

    def rim_row(ref, r):
        return flat(ref[r, 0:8]), ref[r, 8], ref[r, 9]

    def fill(load, q):
        first_lines(load, HALO - 2 + 4 * q, 2 * q, (rows_sc, cols_sc), stage, held, sf, pf)

    def first_step(q, _):
        fill(lambda i: own(4 * q - 2 + i), q)
        return 0

    fill(lambda i: rim_row(top, i) if i < 2 else own(i - 2), 0)
    lax.fori_loop(1, 12, first_step, 0)
    fill(lambda i: own(ROWS - 2 + i) if i < 2 else rim_row(bot, i - 2), 12)
    for j in range(6):
        sf[26, :, j * 128 : (j + 1) * 128] = stacked(held[j], jnp.zeros((KP, 128), F32)).astype(BF16)
    copies = [
        pltpu.make_async_copy(pf.at[pl.ds(1, 24), pl.ds(0, 64)], pf_out, sems.at[0]),
        pltpu.make_async_copy(sf.at[pl.ds(1, 25), pl.ds(0, 64)], sf_out, sems.at[1]),
    ]
    for copy in copies:
        copy.start()

    def post(t, z):
        low = [(7 + 2 * t) // 2, (8 + 2 * t) // 2]
        conv_one_post(z, scale, shift, [mask[low[0]], mask[low[1]]], xm, d1, 2 * t)
        part = pl.ds(2 * t, 2)
        pltpu.make_async_copy(d1.at[part], d1_out.at[part], sems.at[2]).start()

    pipeline(13, lambda t: conv_one_dot(sf, pf, 2 * t, w1t), post, z0, z1)
    last = pltpu.make_async_copy(xm.at[pl.ds(1, 24)], xm_out, sems.at[3])
    last.start()
    low_msg[...] = xm[1:8].astype(BF16)
    high_msg[...] = xm[18:25].astype(BF16)
    for copy in copies:
        copy.wait()
    pltpu.make_async_copy(d1, d1_out, sems.at[2]).wait()
    last.wait()


def own_rows(grid_rows, grid_cols, *args):
    def kernel(*refs):
        own_kernel(grid_rows, grid_cols, *refs)

    vm = pltpu.VMEM
    shape = jax.ShapeDtypeStruct
    return pl.pallas_call(
        kernel,
        out_shape=[
            shape((24, 64, 768), BF16),
            shape((25, 64, 768), BF16),
            shape((26, 80, 512), F32),
            shape((24, 2, KP, 128), F32),
            shape((7, 2, KP, 128), BF16),
            shape((7, 2, KP, 128), BF16),
        ],
        in_specs=[smem_spec()] + [vmem_spec()] * (len(args) - 1),
        out_specs=[any_spec()] * 4 + [vmem_spec()] * 2,
        scratch_shapes=[
            vm((26, 80, 768), BF16),
            vm((27, 80, 768), BF16),
            vm((4, 160, 128), F32),
            vm((6, KP, 128), F32),
            vm((26, 80, 512), F32),
            vm((26, 2, KP, 128), F32),
            vm((LOWS, KP, 128), F32),
            vm((320, 256), F32),
            vm((320, 256), F32),
            pltpu.SemaphoreType.DMA((4,)),
        ],
        compiler_params=pltpu.CompilerParams(vmem_limit_bytes=VMEM_LIMIT),
        cost_estimate=pl.CostEstimate(flops=4 * 10**9, bytes_accessed=30 * 10**6, transcendentals=0),
        name="own_rows",
    )(*args)


def lines_kernel(
    grid_rows, grid_cols,
    cot, top, bot, lef, rig, above, below,
    w2t_in, w2b_in, w3_in, w3b_in, pf_in, sf_in, d1_in, xm_in,
    coarse, g1p_out, g1s_out, keep_msg, give_msg,
    pf, sf, d1, xm, p2, s2, d2, xl, p3, s3, cp, side32, xg3, g3p, g3s, xb2, xg2, g2p, g2s, xt,
    g1p, g1s, held1, acc, acc3, gw, ms, mask, z0, z1, w2t, w2b, w3, w3b, sems,
):
    def fetch(source, target, at):
        copy = pltpu.make_async_copy(source, target, sems.at[at])
        copy.start()
        return copy

    got_xm = fetch(xm_in, xm.at[pl.ds(8, 24)], 2)
    got_w2t = fetch(w2t_in, w2t, 3)
    got_w3 = [fetch(w3_in, w3, 4), fetch(w3b_in, w3b, 5)]
    got_w2b = fetch(w2b_in, w2b, 6)
    got_d1 = fetch(d1_in, d1, 7)
    got_first = [fetch(pf_in, pf, 8), fetch(sf_in, sf, 9)]
    fill_mask(grid_rows // 4, grid_cols // 4, mask)
    xm[1:8] = above[...].astype(F32)
    xm[32:39] = below[...].astype(F32)

    def lines_four(x_ref, s_ref, p_ref, j, _):
        lines = []
        for i in range(3):
            zero, one = x_ref[2 * j - 1 + i, 0], x_ref[2 * j - 1 + i, 1]
            lines.append([before(one), zero, one, after(zero)])
        for n in range(4):
            lanes = slice(n * 128, (n + 1) * 128)
            s_ref[j, :, lanes] = stacked(lines[0][n], lines[1][n]).astype(BF16)
            p_ref[j, :, lanes] = stacked(lines[1][n], lines[2][n]).astype(BF16)
        return 0

    xm[39] = jnp.zeros((2, KP, 128), F32)
    got_xm.wait()
    lax.fori_loop(1, 20, lambda j, c: lines_four(xm, s2, p2, j, c), 0)
    got_w2t.wait()

    def conv_two_post(t, z):
        j = 1 + 3 * t
        for s in range(3):
            folds = []
            for q in range(2):
                half = 0.5 * z[s * 80 : (s + 1) * 80, q * 128 : (q + 1) * 128]
                act, slope = silu_parts(half)
                d2[j + s, :, q * 128 : (q + 1) * 128] = 0.5 * slope
                down = p2[j + s, :, (q + 1) * 128 : (q + 2) * 128].astype(F32)
                folds.append(folded(rounded(down + act)))
            xl[j + s] = rounded((folds[0] + folds[1]) * (0.25 * mask[j + s]))

    pipeline(
        6, lambda t: product(around(s2, p2, 1 + 3 * t, 3, slice(0, 512)), w2t[...]), conv_two_post, z0, z1
    )
    xl[19] = jnp.zeros((KP, 128), F32)

    def lines_three(x_ref, s_ref, p_ref, width, i, _):
        lines = []
        for n in range(3):
            line = x_ref[2 * i - 1 + n]
            lines.append([before(line), line, after(line)])
        for n in range(3):
            lanes = slice(n * width, (n + 1) * width)
            s_ref[i, :, lanes] = stacked(lines[0][n], lines[1][n]).astype(BF16)
            p_ref[i, :, lanes] = stacked(lines[1][n], lines[2][n]).astype(BF16)
        return 0

    lax.fori_loop(1, 10, lambda i, c: lines_three(xl, s3, p3, 128, i, c), 0)

    cp[...] = jnp.zeros_like(cp)
    for h in range(2):
        lanes = slice(h * 128, (h + 1) * 128)
        for r in range(2):
            units = pl.ds((r * 2 + h) * 2, 2)
            cp[r, 0:KO, lanes] = top[2, units].reshape(KO, 128).astype(F32)
            cp[14 + r, 0:KO, lanes] = bot[2, units].reshape(KO, 128).astype(F32)
    for r in range(12):
        cp[2 + r, 0:KO, :] = cot[r].astype(F32)
    for ref, at in ((rig, KO), (lef, KP - 2)):
        side32[...] = ref[pl.ds(ROWS + 1, 3)].reshape(48, 128).astype(F32)
        for h in range(2):
            for r in range(12):
                cp[2 + r, at : at + 2, h * 128 : (h + 1) * 128] = side32[r * 4 + h * 2 : r * 4 + h * 2 + 2]
    for ref, unit, skip, row, at in (
        (top, 9, 8, 0, KP - 2),
        (top, 8, 8, 0, KO),
        (bot, 9, 0, 14, KP - 2),
        (bot, 8, 0, 14, KO),
    ):
        side32[0:16] = ref[2, unit].astype(F32)
        for h in range(2):
            for r in range(2):
                start = skip + r * 4 + h * 2
                cp[row + r, at : at + 2, h * 128 : (h + 1) * 128] = side32[start : start + 2]
    for copy in got_w3:
        copy.wait()

    def conv_three_post(t, z):
        i = 1 + 2 * t
        for s in range(2):
            act, slope = silu_parts(0.5 * z[s * 80 : (s + 1) * 80, :])
            for r in range(2):
                row = 2 * (i + s) + r
                keep = 0.5 * mask[row]
                xg3[row] = cp[row - 2] * line_of(slope, r) * jnp.concatenate([keep, keep], axis=1)

                @pl.when((row >= 4) & (row < 16))
                def _():
                    coarse[row - 4] = act[32 * r : 32 * r + 32].astype(BF16)

    pipeline(
        4, lambda t: product(around(s3, p3, 1 + 2 * t, 2, slice(0, 384)), w3[...]), conv_three_post, z0, z1
    )
    empty = jnp.zeros((KP, 256), F32)
    xg3[1] = empty
    xg3[18] = empty
    xg3[19] = empty
    lax.fori_loop(1, 10, lambda i, c: lines_three(xg3, g3s, g3p, 256, i, c), 0)
    acc3[...] = weight_terms(
        g3p[2:8, 0:64, 256:512].reshape(384, 256), around(s3, p3, 2, 6, slice(0, 384), 0, 64)
    )
    total = product_turned(around(g3s, g3p, 1, 8, slice(0, 768)), w3b[...])
    for i in range(8):
        for r in range(2):
            xb2[2 * i + 2 + r] = 0.25 * line_of(total[i * 80 : (i + 1) * 80], r)

    def grad_two_step(j, _):
        slope = xb2[j] * mask[j]
        for s in range(2):
            for q in range(2):
                d = d2[j, :, q * 128 : (q + 1) * 128]
                xg2[2 * j + s, q] = slope * line_of(d, s)
        return 0

    lax.fori_loop(3, 17, grad_two_step, 0)
    blank = jnp.zeros((2, KP, 128), F32)
    xg2[5] = blank
    xg2[34] = blank
    xg2[35] = blank
    lax.fori_loop(3, 18, lambda j, c: lines_four(xg2, g2s, g2p, j, c), 0)
    got_w2b.wait()

    def fold_weights(at):
        for u in range(3):
            for v in range(3):
                left = (4 * u + v) * 128
                term = acc[0:128, left : left + 128] + acc[128:256, left + 128 : left + 256]
                gw[at, pl.ds((3 * u + v) * 128, 128), :] = term.T

    acc[...] = weight_terms(
        g2p[4:16, 0:64, 128:384].reshape(768, 256), around(s2, p2, 4, 12, slice(0, 512), 0, 64)
    )
    fold_weights(1)
    for tap in range(9):
        turned = acc3[:, tap * 128 : (tap + 1) * 128].T
        gw[2, pl.ds(tap * 128, 128), :] = turned[:, 0:128]
        gw[3, pl.ds(tap * 128, 128), :] = turned[:, 128:256]

    def back_two_post(t, z):
        j = 3 + 2 * t
        for s in range(2):
            keep = 0.25 * mask[j + s]
            base = xb2[j + s]
            for q in range(2):
                pair = z[s * 80 : (s + 1) * 80, q * 128 : (q + 1) * 128]
                for r in range(2):
                    xt[2 * (j + s) + r, q] = (base + line_of(pair, r)) * keep

    pipeline(
        7, lambda t: product_turned(around(g2s, g2p, 3 + 2 * t, 2, slice(0, 512)), w2b[...]), back_two_post, z0, z1
    )
    got_d1.wait()

    def grad_line(m, s):
        planes = [xt[m, p // 2] * line_of(d1[m - 7, :, p * 128 : (p + 1) * 128], s) for p in range(4)]
        lines = [before(planes[3])] + planes + [after(planes[0])]
        return [line[:KO] for line in lines]

    first_held = grad_line(7, 1)
    for n in range(6):
        held1[n] = first_held[n]

    def grad_one_step(at, _):
        m = at + 8
        even, odd = grad_line(m, 0), grad_line(m, 1)
        for n in range(6):
            lanes = slice(n * 128, (n + 1) * 128)
            g1s[at, :, lanes] = jnp.concatenate([held1[n], even[n]], axis=0).astype(BF16)
            g1p[at, :, lanes] = jnp.concatenate([even[n], odd[n]], axis=0).astype(BF16)
            held1[n] = odd[n]
        return 0

    lax.fori_loop(0, 25, grad_one_step, 0)
    copies = [
        pltpu.make_async_copy(g1p.at[pl.ds(0, 24)], g1p_out, sems.at[0]),
        pltpu.make_async_copy(g1s, g1s_out, sems.at[1]),
    ]
    for copy in copies:
        copy.start()
    for copy in got_first:
        copy.wait()
    acc[...] = jnp.zeros_like(acc)

    def weight_one_step(t, _):
        at = 8 * t
        grads = jnp.concatenate(
            [g1p[pl.ds(at, 8), :, lanes].reshape(512, 256) for lanes in (slice(128, 384), slice(384, 640))], axis=0
        )
        fields = jnp.concatenate(
            [around(sf, pf, at, 8, lanes, 0, 64) for lanes in (slice(0, 512), slice(256, 768))], axis=0
        )
        acc[...] += weight_terms(grads, fields)
        return 0

    lax.fori_loop(0, 3, weight_one_step, 0)
    fold_weights(0)
    for n in range(10):
        for t in range(4):
            piece = gw[t, pl.ds(n, 128, stride=9), :] if n < 9 else jnp.zeros((128, 128), F32)
            ms[pl.ds(4 * n + t, 128, stride=40), :] = piece
    core = lax.axis_index("core")

    def msg_step(n, _):
        rows = pl.ds(pl.multiple_of(n * 320, 320), 320)
        keep_msg[rows, :] = ms[pl.ds(pl.multiple_of((2 * n + core) * 320, 320), 320), :].astype(BF16)
        give_msg[rows, :] = ms[pl.ds(pl.multiple_of((2 * n + 1 - core) * 320, 320), 320), :].astype(BF16)
        return 0

    lax.fori_loop(0, 8, msg_step, 0)
    for copy in copies:
        copy.wait()


def levels(grid_rows, grid_cols, *args):
    def kernel(*refs):
        lines_kernel(grid_rows, grid_cols, *refs)

    vm = pltpu.VMEM
    return pl.pallas_call(
        kernel,
        out_shape=[
            jax.ShapeDtypeStruct((12, KO, 256), BF16),
            jax.ShapeDtypeStruct((24, 64, 768), BF16),
            jax.ShapeDtypeStruct((25, 64, 768), BF16),
            jax.ShapeDtypeStruct((2560, 128), BF16),
            jax.ShapeDtypeStruct((2560, 128), BF16),
        ],
        in_specs=[vmem_spec()] * 7 + [any_spec()] * 8,
        out_specs=[vmem_spec(), any_spec(), any_spec(), vmem_spec(), vmem_spec()],
        scratch_shapes=[
            vm((24, 64, 768), BF16),
            vm((25, 64, 768), BF16),
            vm((26, 80, 512), F32),
            vm((PAIRS, 2, KP, 128), F32),
            vm((LOWS, 80, 512), BF16),
            vm((LOWS, 80, 512), BF16),
            vm((LOWS, 80, 256), F32),
            vm((LOWS, KP, 128), F32),
            vm((10, 80, 384), BF16),
            vm((10, 80, 384), BF16),
            vm((16, KP, 256), F32),
            vm((48, 128), F32),
            vm((LOWS, KP, 256), F32),
            vm((10, 80, 768), BF16),
            vm((10, 80, 768), BF16),
            vm((LOWS, KP, 128), F32),
            vm((PAIRS, 2, KP, 128), F32),
            vm((LOWS, 80, 512), BF16),
            vm((LOWS, 80, 512), BF16),
            vm((PAIRS, 2, KP, 128), F32),
            vm((25, 64, 768), BF16),
            vm((25, 64, 768), BF16),
            vm((6, KO, 128), F32),
            vm((256, 1536), F32),
            vm((256, 1152), F32),
            vm((4, 1152, 128), F32),
            vm((5120, 128), F32),
            vm((LOWS, KP, 128), F32),
            vm((320, 256), F32),
            vm((320, 256), F32),
            vm((1536, 256), BF16),
            vm((256, 1536), BF16),
            vm((1152, 256), BF16),
            vm((128, 2304), BF16),
            pltpu.SemaphoreType.DMA((10,)),
        ],
        compiler_params=pltpu.CompilerParams(vmem_limit_bytes=VMEM_LIMIT),
        name="encoder_levels",
    )(*args)


def input_kernel(g1p, g1s, g1s_next, w1b, out, stage):
    for t in range(2):
        halves = []
        for lanes in (slice(0, 512), slice(256, 768)):
            after_last = g1s[3:4, :, lanes] if t == 0 else g1s_next[:, :, lanes]
            parts = [
                g1s[2 * t : 2 * t + 2, :, lanes],
                g1p[2 * t : 2 * t + 2, :, lanes],
                g1s[1:3, :, lanes] if t == 0 else jnp.concatenate([g1s[3:4, :, lanes], after_last], axis=0),
            ]
            halves.append(jnp.concatenate([part.reshape(128, 512) for part in parts], axis=1))
        total = product_turned(jnp.concatenate(halves, axis=0), w1b[...])
        for r in range(4):
            for p in range(4):
                rows = (p // 2) * 128 + r * 32
                value = total[rows : rows + 32, (p % 2) * 128 : (p % 2 + 1) * 128]
                stage[4 * t + r, pl.ds(p, 32, stride=4), :] = value
            out[4 * t + r] = stage[4 * t + r].astype(BF16)


def input_grad(g1p, g1s, w1b):
    return pl.pallas_call(
        input_kernel,
        grid=(6,),
        out_shape=jax.ShapeDtypeStruct((ROWS, 128, 128), BF16),
        in_specs=[
            pl.BlockSpec((4, 64, 768), lambda i: (i, 0, 0)),
            pl.BlockSpec((4, 64, 768), lambda i: (i, 0, 0)),
            pl.BlockSpec((1, 64, 768), lambda i: (4 * i + 4, 0, 0)),
            pl.BlockSpec((256, 1536), lambda i: (0, 0)),
        ],
        out_specs=pl.BlockSpec((8, 128, 128), lambda i: (i, 0, 0)),
        scratch_shapes=[pltpu.VMEM((8, 128, 128), F32)],
        compiler_params=pltpu.CompilerParams(vmem_limit_bytes=VMEM_LIMIT),
        cost_estimate=pl.CostEstimate(flops=2 * 6144 * 1152 * 128, bytes_accessed=8 * 1024 * 1024, transcendentals=0),
        name="input_grad",
    )(g1p, g1s, g1s, w1b)


def add_kernel(keep, other, out):
    out[...] = (keep[...].astype(F32) + other[...].astype(F32)).astype(BF16)


def add(keep, other):
    return pl.pallas_call(
        add_kernel,
        out_shape=jax.ShapeDtypeStruct(keep.shape, BF16),
        in_specs=[vmem_spec()] * 2,
        out_specs=vmem_spec(),
        name="add_core_terms",
    )(keep, other)


def collect(got):
    sums = got.astype(F32).sum(axis=0)[0:36].reshape(9, 4, 128)
    return sums[:, 0], sums[:, 1], jnp.concatenate([sums[:, 2], sums[:, 3]], axis=1)


def shifted(block, axis, step):
    devices = lax.axis_size(axis)
    pairs = [(i, i + step) for i in range(devices) if 0 <= i + step < devices]
    return lax.ppermute(block, axis, pairs)


def body(inputs, weight_one, weight_two, weight_three, noise_table, frequency, anchor, noise_index, cotangent):
    grid = (lax.axis_size(ROW_AXES) * ROWS, lax.axis_size("tx") * 4 * KO)
    inputs = inputs.reshape(ROWS, 8, 16, 128)
    right, left, cots = sides(inputs, cotangent)
    lef = shifted(right, "tx", 1)
    rig = shifted(left, "tx", -1)
    w1t, w1b, w2t, w2b, w3b, rows_sc, cols_sc = prep(*grid, anchor, weight_one, weight_two, weight_three, frequency)
    lef, rig, rows_sc = lax.optimization_barrier((lef, rig, rows_sc))
    top = shifted(rim(inputs, cots[0], lef, rig, ROWS - 2, 3 + ROWS), ROW_AXES, 1)
    bot = shifted(rim(inputs, cots[1], lef, rig, 0, 0), ROW_AXES, -1)
    pf, sf, d1, xm, low_msg, high_msg = own_rows(
        *grid, noise_index, inputs, lef, rig, top, bot, w1t, rows_sc, cols_sc, noise_table
    )
    above = shifted(high_msg, ROW_AXES, 1)
    below = shifted(low_msg, ROW_AXES, -1)
    coarse, g1p, g1s, keep_msg, give_msg = levels(
        *grid, cotangent, top, bot, lef, rig, above, below, w2t, w2b, weight_three, w3b, pf, sf, d1, xm
    )
    other = lax.ppermute(give_msg, "core", [(0, 1), (1, 0)])
    msg = add(keep_msg, other).reshape(64, 40, 128)
    got = lax.all_to_all(msg, ("chip", "tx"), 0, 0, tiled=True)
    grad_inputs = input_grad(g1p, g1s, w1b)
    return (coarse, grad_inputs, *collect(got))


def solution(mesh):
    halves = jax.sharding.Mesh(mesh.devices.reshape(-1, 2, mesh.devices.shape[1]), ("chip", "core", "tx"))
    placed = (P(ROW_AXES, "tx", None), P(), P(), P(), P(), P(), P(), P(), P(ROW_AXES, "tx", None))
    return jax.shard_map(
        body,
        mesh=halves,
        in_specs=placed,
        out_specs=(
            P(ROW_AXES, "tx", None),
            P(ROW_AXES, "tx", None),
            P((*ROW_AXES, "tx"), None),
            P((*ROW_AXES, "tx"), None),
            P((*ROW_AXES, "tx"), None),
        ),
        check_vma=False,
    )
```

```python
import jax
import jax.numpy as jnp
from jax import lax
from jax.experimental import pallas as pl
from jax.experimental.pallas import tpu as pltpu
from jax.sharding import PartitionSpec as P

BF16 = jnp.bfloat16
F32 = jnp.float32

KO = 32
KP = 40
KW = 48
HALO = 16
ROWS = 48
PAD_ROWS = ROWS + 2 * HALO
PAIRS = PAD_ROWS // 2
LOWS = PAIRS // 2
VMEM_LIMIT = 60 * 1024 * 1024


def any_spec():
    return pl.BlockSpec(memory_space=pl.ANY)


def vmem_spec():
    return pl.BlockSpec(memory_space=pltpu.VMEM)


def smem_spec():
    return pl.BlockSpec(memory_space=pltpu.SMEM)


ROW_AXES = ("chip", "core")


def own_place():
    return lax.axis_index(ROW_AXES), lax.axis_index("tx")


def odd_column():
    return lax.rem(lax.axis_index("tx"), 2)


def side_kernel(inputs, cot, one, two, cots, side32, sems):
    odd = odd_column()
    copies = [
        pltpu.make_async_copy(inputs.at[:, 7 - 7 * odd], one.at[pl.ds(1, ROWS)], sems.at[0]),
        pltpu.make_async_copy(inputs.at[:, 7 * odd], two.at[pl.ds(1, ROWS)], sems.at[1]),
    ]
    for copy in copies:
        copy.start()
    for target, at_left in ((one, odd == 1), (two, odd == 0)):
        for r in range(12):
            line = cot[r].astype(F32)
            for h in range(2):
                lanes = slice(h * 128, (h + 1) * 128)
                side32[pl.ds(r * 4 + h * 2, 2)] = jnp.where(at_left, line[0:2, lanes], line[30:32, lanes])
        side = side32[...].astype(BF16).reshape(3, 16, 128)
        target[pl.ds(0, 1)] = side[0:1]
        target[pl.ds(1 + ROWS, 3)] = side
    for at, start in ((0, 10), (1, 0)):
        for r in range(2):
            for h in range(2):
                cots[at, pl.ds((r * 2 + h) * 2, 2)] = cot[start + r, :, h * 128 : (h + 1) * 128].reshape(2, 16, 128)
    for copy in copies:
        copy.wait()


def sides(inputs, cot):
    return pl.pallas_call(
        side_kernel,
        out_shape=[jax.ShapeDtypeStruct((ROWS + 4, 16, 128), BF16)] * 2 + [jax.ShapeDtypeStruct((2, 8, 16, 128), BF16)],
        in_specs=[any_spec(), vmem_spec()],
        out_specs=[vmem_spec()] * 3,
        scratch_shapes=[pltpu.VMEM((48, 128), F32), pltpu.SemaphoreType.DMA((2,))],
        name="pack_columns",
    )(inputs, cot)


def rim_kernel(inputs, cots, one, two, _, off, near, sems):
    core = lax.axis_index("core")
    copies = []

    def fetch(source, target):
        copy = pltpu.make_async_copy(source, target, sems.at[len(copies)])
        copy.start()
        copies.append(copy)

    body = pl.ds(0, HALO)
    for target, low in ((off, core), (near, 1 - core)):
        row = (ROWS - HALO) * low
        fetch(inputs.at[pl.ds(row, HALO)], target.at[body, pl.ds(0, 8)])
        fetch(cots.at[1 - low], target.at[HALO, pl.ds(0, 8)])
        for unit, side in ((8, one), (9, two)):
            fetch(side.at[pl.ds(1 + row, HALO)], target.at[body, unit])
            fetch(side.at[(3 + ROWS) * low], target.at[HALO, unit])
    for copy in copies:
        copy.wait()


def rims(*args):
    return pl.pallas_call(
        rim_kernel,
        out_shape=[jax.ShapeDtypeStruct((HALO + 1, 10, 16, 128), BF16)] * 2,
        in_specs=[any_spec()] * len(args),
        out_specs=[vmem_spec()] * 2,
        scratch_shapes=[pltpu.SemaphoreType.DMA((12,))],
        name="pack_rows",
    )(*args)


def weight_forms(w1, w2, w3, w1t, w1b, w2t, w2b, w3b):
    zero = jnp.zeros((128, 128), BF16)
    for source, ahead, back in ((w1, w1t, w1b), (w2, w2t, w2b)):
        for u in range(3):
            for v in range(3):
                tap = source[pl.ds((3 * u + v) * 128, 128), :]
                for i in range(2):
                    side = slice(i * 128, (i + 1) * 128)
                    ahead[pl.ds((4 * u + v + i) * 128, 128), side] = tap
                    at = (4 * (2 - u) + 2 - v + i) * 128
                    back[side, at : at + 128] = tap
            for i, j in ((0, 3), (1, 0)):
                at = (4 * u + j) * 128
                side = slice(i * 128, (i + 1) * 128)
                ahead[pl.ds(at, 128), side] = zero
                back[side, at : at + 128] = zero
    for u in range(3):
        for v in range(3):
            at = (3 * (2 - u) + 2 - v) * 256
            w3b[:, at : at + 256] = w3[pl.ds((3 * u + v) * 128, 128), :]


def wave_tables(grid_rows, grid_cols, anchor, frequency, rows_sc, cols_sc):
    own_row, own_col = own_place()
    row = lax.broadcasted_iota(jnp.int32, (PAD_ROWS, 128), 0) - HALO + own_row * ROWS
    angle = (row + anchor[0]).astype(F32) * frequency[0:1, :]
    keep = jnp.where((row >= 0) & (row < grid_rows), 1.0, 0.0)
    rows_sc[0] = jnp.sin(angle) * keep
    rows_sc[1] = jnp.cos(angle) * keep
    for p in range(4):
        k = lax.broadcasted_iota(jnp.int32, (KP, 128), 0)
        col = 4 * jnp.where(k < KO + 4, k, k - KP) + p + own_col * (4 * KO)
        angle = (col + anchor[1]).astype(F32) * frequency[1:2, :]
        keep = jnp.where((col >= 0) & (col < grid_cols), 1.0, 0.0)
        cols_sc[0, p] = jnp.sin(angle) * keep
        cols_sc[1, p] = jnp.cos(angle) * keep


def prep_kernel(grid_rows, grid_cols, anchor, w1, w2, w3, frequency, w1t, w1b, w2t, w2b, w3b, rows_sc, cols_sc):
    weight_forms(w1, w2, w3, w1t, w1b, w2t, w2b, w3b)
    wave_tables(grid_rows, grid_cols, anchor, frequency, rows_sc, cols_sc)


def prep(grid_rows, grid_cols, anchor, w1, w2, w3, frequency):
    def kernel(*refs):
        prep_kernel(grid_rows, grid_cols, *refs)

    shape = jax.ShapeDtypeStruct
    return pl.pallas_call(
        kernel,
        out_shape=[
            shape((1536, 256), BF16),
            shape((256, 1536), BF16),
            shape((1536, 256), BF16),
            shape((256, 1536), BF16),
            shape((128, 2304), BF16),
            shape((2, PAD_ROWS, 128), F32),
            shape((2, 4, KP, 128), F32),
        ],
        in_specs=[smem_spec()] + [vmem_spec()] * 4,
        out_specs=[vmem_spec()] * 7,
        compiler_params=pltpu.CompilerParams(vmem_limit_bytes=VMEM_LIMIT),
        name="weight_forms",
    )(anchor, w1, w2, w3, frequency)


def fill_mask(low_rows, low_cols, mask):
    own_row, own_col = own_place()
    k = lax.broadcasted_iota(jnp.int32, (KP, 128), 0)
    col = jnp.where(k < KO + 4, k, k - KP) + own_col * KO
    inside = jnp.where((col >= 0) & (col < low_cols), 1.0, 0.0)

    def step(at, _):
        row = at - 4 + own_row * 12
        mask[at] = inside * jnp.where((row >= 0) & (row < low_rows), 1.0, 0.0)
        return 0

    lax.fori_loop(0, LOWS, step, 0)


def widened(line):
    rest = jnp.zeros((KW - KP, line.shape[1]), F32)
    return jnp.concatenate([line, rest], axis=0).astype(BF16)


def put_line(ref, row, planes):
    width = planes[0].shape[1]
    for n, plane in enumerate(planes):
        ref[row, :, n * width : (n + 1) * width] = widened(plane)


def before(line):
    return pltpu.roll(line, 1, 0)


def after(line):
    return pltpu.roll(line, KP - 1, 0)


def silu_parts(half):
    th = jnp.tanh(half)
    act = half + half * th
    return act, (1.0 + act) + th * (1.0 - act)


def rounded(value):
    return value.astype(BF16).astype(F32)


def flat(block):
    return block.reshape(128, 128)


def modulation(noise, noise_index):
    modulate = noise[pl.ds(noise_index[0], 1), :]
    return 1.0 + modulate[:, 0:128], modulate[:, 128:256]


def first_lines(load, base, at, tables, stage, x1):
    rows_sc, cols_sc = tables
    for i in range(4):
        own, right, left = load(i)
        stage[i, 0:128] = own.astype(F32)
        stage[i, 128:144] = right.astype(F32)
        stage[i, 144:160] = left.astype(F32)
        sin_row = rows_sc[0, pl.ds(base + i, 1), :]
        cos_row = rows_sc[1, pl.ds(base + i, 1), :]
        planes = []
        for p in range(4):
            value = stage[i, pl.ds(p, KP, stride=4), :]
            planes.append(value + (sin_row * cols_sc[1, p] + cos_row * cols_sc[0, p]))
        put_line(x1, at + i, [before(planes[3])] + planes + [after(planes[0])])


def around(ref, at, count, lanes, cols=KW):
    parts = [ref[pl.ds(at - 1 + u, count), 0:cols, lanes] for u in range(3)]
    return jnp.concatenate([part.reshape(count * cols, part.shape[-1]) for part in parts], axis=1)


def product(left, right):
    return jnp.dot(left, right, preferred_element_type=F32)


def product_turned(left, right):
    return lax.dot_general(left, right, (((1,), (1,)), ((), ())), preferred_element_type=F32)


def weight_terms(grad, field):
    return lax.dot_general(grad, field, (((0,), (0,)), ((), ())), preferred_element_type=F32)


def pipeline(steps, dot, post, z0, z1):
    def put(z, t):
        total = dot(t)
        z[0 : total.shape[0], :] = total

    put(z0, 0)

    def two(i, _):
        put(z1, 2 * i + 1)
        post(2 * i, z0)
        put(z0, 2 * i + 2)
        post(2 * i + 1, z1)
        return 0

    if steps > 2:
        lax.fori_loop(0, (steps - 1) // 2, two, 0)
    if steps % 2 == 0:
        put(z1, steps - 1)
        post(steps - 2, z0)
        post(steps - 1, z1)
    else:
        post(steps - 1, z0)


def conv_one_dot(x1, row, w1t):
    one = around(x1, row, 4, slice(0, 512))
    two = around(x1, row, 4, slice(256, 768))
    return product(jnp.concatenate([one, two], axis=0), w1t[...])


def conv_one_post(z, scale, shift, keeps, d1, d1_row, x2, x2_row):
    for s in range(2):
        halves = []
        for q in range(2):
            total = None
            for p in (2 * q, 2 * q + 1):
                for r in range(2):
                    at = q * 4 * KW + (2 * s + r) * KW
                    half = z[at : at + KP, (p % 2) * 128 : (p % 2 + 1) * 128] * (0.5 * scale) + 0.5 * shift
                    act, slope = silu_parts(half)
                    d1[d1_row + 2 * s + r, :, p * 128 : (p + 1) * 128] = (0.5 * scale) * slope
                    act = rounded(act)
                    total = act if total is None else total + act
            halves.append(total * (0.25 * keeps[s]))
        put_line(x2, x2_row + s, [before(halves[1]), halves[0], halves[1], after(halves[0])])


def own_kernel(
    grid_rows, grid_cols,
    noise_index, inputs, one, two, w1t, rows_sc, cols_sc, noise,
    x1_out, d1_out, x2_out,
    x1, stage, d1, x2, mask, side, z0, z1, sems,
):
    odd = odd_column()
    halos = [
        pltpu.make_async_copy(one, side.at[1 - odd], sems.at[0]),
        pltpu.make_async_copy(two, side.at[odd], sems.at[1]),
    ]
    for copy in halos:
        copy.start()
    fill_mask(grid_rows // 4, grid_cols // 4, mask)
    scale, shift = modulation(noise, noise_index)
    for copy in halos:
        copy.wait()

    def first(q):
        def load(i):
            row = 4 * q + i
            return flat(inputs[row]), side[1, 1 + row], side[0, 1 + row]

        first_lines(load, HALO + 4 * q, 4 * q, (rows_sc, cols_sc), stage, x1)
        part = pl.ds(4 * q, 4)
        pltpu.make_async_copy(x1.at[part], x1_out.at[part], sems.at[2]).start()

    def dot(t):
        return conv_one_dot(x1, 4 * t + 2, w1t)

    def post(t, z):
        keeps = [mask[(9 + 2 * t) // 2], mask[(10 + 2 * t) // 2]]
        conv_one_post(z, scale, shift, keeps, d1, 4 * t, x2, 2 * t)
        part = pl.ds(4 * t, 4)
        pltpu.make_async_copy(d1.at[part], d1_out.at[part], sems.at[3]).start()

    first(0)
    first(1)
    z0[...] = dot(0)
    first(2)

    def two_steps(i, _):
        t = 2 * i + 1
        z1[...] = dot(t)
        first(t + 2)
        post(t - 1, z0)
        z0[...] = dot(t + 1)
        first(t + 3)
        post(t, z1)
        return 0

    lax.fori_loop(0, 4, two_steps, 0)
    z1[...] = dot(9)
    first(11)
    post(8, z0)
    z0[...] = dot(10)
    post(9, z1)
    post(10, z0)
    last = pltpu.make_async_copy(x2, x2_out, sems.at[4])
    last.start()
    pltpu.make_async_copy(x1, x1_out, sems.at[2]).wait()
    pltpu.make_async_copy(d1, d1_out, sems.at[3]).wait()
    last.wait()


def own_rows(grid_rows, grid_cols, *args):
    def kernel(*refs):
        own_kernel(grid_rows, grid_cols, *refs)

    vm = pltpu.VMEM
    shape = jax.ShapeDtypeStruct
    return pl.pallas_call(
        kernel,
        out_shape=[shape((48, KW, 768), BF16), shape((44, KP, 512), F32), shape((22, KW, 512), BF16)],
        in_specs=[smem_spec(), vmem_spec(), any_spec(), any_spec()] + [vmem_spec()] * 4,
        out_specs=[any_spec()] * 3,
        scratch_shapes=[
            vm((48, KW, 768), BF16),
            vm((4, 160, 128), F32),
            vm((44, KP, 512), F32),
            vm((22, KW, 512), BF16),
            vm((LOWS, KP, 128), F32),
            vm((2, ROWS + 4, 16, 128), BF16),
            vm((8 * KW, 256), F32),
            vm((8 * KW, 256), F32),
            pltpu.SemaphoreType.DMA((5,)),
        ],
        compiler_params=pltpu.CompilerParams(vmem_limit_bytes=VMEM_LIMIT),
        cost_estimate=pl.CostEstimate(flops=4 * 10**9, bytes_accessed=30 * 10**6, transcendentals=0),
        name="own_rows",
    )(*args)


def lines_kernel(
    grid_rows, grid_cols,
    noise_index, cot, w1t, rows_sc, cols_sc, noise,
    off, near, one, two, w2t_in, w2b_in, w3_in, w3b_in, x1_in, d1_in, x2_in,
    coarse_out, g1_out, keep_msg, give_msg,
    rim, stage, x1, d1, x2, d2, x3, cp, side, side32, g3, xb2, g2, g1, coarse,
    acc, acc3, gw, ms, mask, z0, z1, w2t, w2b, w3, w3b, sems,
):
    core = lax.axis_index("core")
    odd = odd_column()

    def fetch(source, target, at):
        copy = pltpu.make_async_copy(source, target, sems.at[at])
        copy.start()
        return copy

    got_rims = [fetch(off, rim.at[core], 0), fetch(near, rim.at[1 - core], 1)]
    got_edges = [
        fetch(x1_in.at[pl.ds(0, 4)], x1.at[pl.ds(16, 4)], 2),
        fetch(x1_in.at[pl.ds(44, 4)], x1.at[pl.ds(60, 4)], 3),
    ]
    got_x2 = fetch(x2_in, x2.at[pl.ds(9, 22)], 4)
    units = pl.ds(ROWS + 1, 3)
    got_sides = [fetch(one.at[units], side.at[1 - odd], 5), fetch(two.at[units], side.at[odd], 6)]
    got_w2t = fetch(w2t_in, w2t, 7)
    got_w3 = [fetch(w3_in, w3, 8), fetch(w3b_in, w3b, 9)]
    got_w2b = fetch(w2b_in, w2b, 10)
    got_d1 = fetch(d1_in, d1.at[pl.ds(18, 44)], 11)
    got_x1 = fetch(x1_in.at[pl.ds(4, 40)], x1.at[pl.ds(20, 40)], 12)
    fill_mask(grid_rows // 4, grid_cols // 4, mask)
    scale, shift = modulation(noise, noise_index)
    for copy in got_rims:
        copy.wait()

    def first(n):
        below = n // 4
        start = 4 * (n % 4)
        base = start + (HALO + ROWS) * below

        def load(i):
            row = start + i
            return flat(rim[below, row, 0:8]), rim[below, row, 8 + odd], rim[below, row, 9 - odd]

        first_lines(load, base, base, (rows_sc, cols_sc), stage, x1)

    def mid_of(t):
        return jnp.where(t < 4, 1 + 2 * t, 23 + 2 * t)

    def dot(t):
        return conv_one_dot(x1, 2 * mid_of(t), w1t)

    def post(t, z):
        m = mid_of(t)
        conv_one_post(z, scale, shift, [mask[m // 2], mask[(m + 1) // 2]], d1, 2 * m, x2, m)

    first(0)
    first(1)
    for copy in got_edges:
        copy.wait()
    z0[...] = dot(0)
    first(2)

    def two_steps(i, _):
        t = 2 * i + 1
        z1[...] = dot(t)
        first(t + 2)
        post(t - 1, z0)
        z0[...] = dot(t + 1)
        first(t + 3)
        post(t, z1)
        return 0

    lax.fori_loop(0, 2, two_steps, 0)
    z1[...] = dot(5)
    first(7)
    post(4, z0)
    z0[...] = dot(6)
    post(5, z1)
    z1[...] = dot(7)
    post(6, z0)
    post(7, z1)
    got_x2.wait()
    got_w2t.wait()

    def conv_two_post(t, z):
        for s in range(3):
            low = 1 + 3 * t + s
            total = None
            for q in range(2):
                lanes = slice(q * 128, (q + 1) * 128)
                for r in range(2):
                    row, at = 2 * low + r, (2 * s + r) * KW
                    act, slope = silu_parts(0.5 * z[at : at + KP, lanes])
                    d2[row, :, lanes] = 0.5 * slope
                    down = x2[row, :, (q + 1) * 128 : (q + 2) * 128].astype(F32)[:KP]
                    act = rounded(down + act)
                    total = act if total is None else total + act
            line = total * (0.25 * mask[low])
            put_line(x3, low, [before(line), line, after(line)])

    pipeline(6, lambda t: product(around(x2, 2 + 6 * t, 6, slice(0, 512)), w2t[...]), conv_two_post, z0, z1)

    cp[...] = jnp.zeros_like(cp)
    for copy in got_sides:
        copy.wait()
    for h in range(2):
        lanes = slice(h * 128, (h + 1) * 128)
        for r in range(2):
            units = pl.ds((r * 2 + h) * 2, 2)
            cp[r, 0:KO, lanes] = rim[0, HALO, units].reshape(KO, 128).astype(F32)
            cp[14 + r, 0:KO, lanes] = rim[1, HALO, units].reshape(KO, 128).astype(F32)
    for r in range(12):
        cp[2 + r, 0:KO, :] = cot[r].astype(F32)
    for which, at in ((1, KO), (0, KP - 2)):
        side32[...] = side[which].reshape(48, 128).astype(F32)
        for h in range(2):
            for r in range(12):
                cp[2 + r, at : at + 2, h * 128 : (h + 1) * 128] = side32[r * 4 + h * 2 : r * 4 + h * 2 + 2]
    for below, skip, row in ((0, 8, 0), (1, 0, 14)):
        for unit, at in ((9 - odd, KP - 2), (8 + odd, KO)):
            side32[0:16] = rim[below, HALO, unit].astype(F32)
            for h in range(2):
                for r in range(2):
                    start = skip + r * 4 + h * 2
                    cp[row + r, at : at + 2, h * 128 : (h + 1) * 128] = side32[start : start + 2]
    for copy in got_w3:
        copy.wait()
    g3[1] = jnp.zeros((KW, 768), BF16)
    g3[18] = jnp.zeros((KW, 768), BF16)

    def conv_three_post(t, z):
        for i in range(4):
            row = 2 + 4 * t + i
            act, slope = silu_parts(0.5 * z[i * KW : i * KW + KP, :])
            keep = 0.5 * mask[row]
            line = cp[row - 2] * slope * jnp.concatenate([keep, keep], axis=1)
            put_line(g3, row, [before(line), line, after(line)])
            coarse[row - 2] = act[:KO].astype(BF16)

    pipeline(4, lambda t: product(around(x3, 2 + 4 * t, 4, slice(0, 384)), w3[...]), conv_three_post, z0, z1)
    put_coarse = fetch(coarse.at[pl.ds(2, 12)], coarse_out, 0)

    def back_three_post(t, z):
        for i in range(4):
            low = 2 + 4 * t + i
            line = 0.25 * z[i * KW : i * KW + KP, 0:128]
            xb2[low] = line
            line = line * mask[low]
            for r in range(2):
                row = 2 * low + r
                zero, one = (line * d2[row, :, q * 128 : (q + 1) * 128] for q in range(2))
                put_line(g2, row, [before(one), zero, one, after(zero)])

    def back_three_dot(t):
        total = product_turned(around(g3, 2 + 4 * t, 4, slice(0, 768)), w3b[...])
        return jnp.concatenate([total, total], axis=1)

    pipeline(4, back_three_dot, back_three_post, z0, z1)
    acc3[...] = weight_terms(
        g3[4:16, 0:KO, 256:512].reshape(12 * KO, 256), around(x3, 4, 12, slice(0, 384), KO)
    )
    acc[...] = weight_terms(
        g2[8:32, 0:KO, 128:384].reshape(24 * KO, 256), around(x2, 8, 24, slice(0, 512), KO)
    )
    got_w2b.wait()
    got_d1.wait()

    def back_two_post(t, z):
        for i in range(4):
            m = 6 + 4 * t + i
            low = m // 2
            keep = 0.25 * mask[low]
            base = xb2[low]
            both = [(base + z[i * KW : i * KW + KP, q * 128 : (q + 1) * 128]) * keep for q in range(2)]
            for r in range(2):
                row = 2 * m + r
                planes = [both[p // 2] * d1[row, :, p * 128 : (p + 1) * 128] for p in range(4)]
                for n, line in enumerate([before(planes[3])] + planes + [after(planes[0])]):
                    g1[row - 12, :, n * 128 : (n + 1) * 128] = line[:KO].astype(BF16)

    pipeline(
        7, lambda t: product_turned(around(g2, 6 + 4 * t, 4, slice(0, 512)), w2b[...]), back_two_post, z0, z1
    )
    put_g1 = fetch(g1.at[pl.ds(3, 50)], g1_out, 1)
    got_x1.wait()

    def fold_weights(at):
        for u in range(3):
            for v in range(3):
                left = (4 * u + v) * 128
                term = acc[0:128, left : left + 128] + acc[128:256, left + 128 : left + 256]
                gw[at, pl.ds((3 * u + v) * 128, 128), :] = term.T

    def nines(t):
        for owner in range(128):
            at = owner * 40 + t * 9
            ms[at : at + 9, :] = gw[t, owner * 9 : owner * 9 + 9, :]

    def one_chunk(t):
        grads = jnp.concatenate(
            [g1[4 + 16 * t : 20 + 16 * t, :, lanes].reshape(512, 256) for lanes in (slice(128, 384), slice(384, 640))],
            axis=0,
        )
        fields = jnp.concatenate(
            [around(x1, 16 + 16 * t, 16, lanes, KO) for lanes in (slice(0, 512), slice(256, 768))], axis=0
        )
        return weight_terms(grads, fields)

    fold_weights(1)
    acc[...] = one_chunk(0)
    for tap in range(9):
        turned = acc3[:, tap * 128 : (tap + 1) * 128].T
        gw[2, pl.ds(tap * 128, 128), :] = turned[:, 0:128]
        gw[3, pl.ds(tap * 128, 128), :] = turned[:, 128:256]
    nines(1)
    acc[...] += one_chunk(1)
    nines(2)
    nines(3)
    acc[...] += one_chunk(2)
    for owner in range(128):
        ms[owner * 40 + 36 : owner * 40 + 40, :] = jnp.zeros((4, 128), F32)
    fold_weights(0)
    nines(0)

    def msg_step(n, _):
        rows = pl.ds(pl.multiple_of(n * 320, 320), 320)
        keep_msg[rows, :] = ms[pl.ds(pl.multiple_of((2 * n + core) * 320, 320), 320), :].astype(BF16)
        give_msg[rows, :] = ms[pl.ds(pl.multiple_of((2 * n + 1 - core) * 320, 320), 320), :].astype(BF16)
        return 0

    lax.fori_loop(0, 8, msg_step, 0)
    put_coarse.wait()
    put_g1.wait()


def levels(grid_rows, grid_cols, *args):
    def kernel(*refs):
        lines_kernel(grid_rows, grid_cols, *refs)

    vm = pltpu.VMEM
    return pl.pallas_call(
        kernel,
        out_shape=[
            jax.ShapeDtypeStruct((12, KO, 256), BF16),
            jax.ShapeDtypeStruct((50, KO, 768), BF16),
            jax.ShapeDtypeStruct((2560, 128), BF16),
            jax.ShapeDtypeStruct((2560, 128), BF16),
        ],
        in_specs=[smem_spec()] + [vmem_spec()] * 5 + [any_spec()] * 11,
        out_specs=[any_spec(), any_spec(), vmem_spec(), vmem_spec()],
        scratch_shapes=[
            vm((2, HALO + 1, 10, 16, 128), BF16),
            vm((4, 160, 128), F32),
            vm((PAD_ROWS, KW, 768), BF16),
            vm((PAD_ROWS, KP, 512), F32),
            vm((PAIRS, KW, 512), BF16),
            vm((PAIRS, KP, 256), F32),
            vm((LOWS, KW, 384), BF16),
            vm((16, KP, 256), F32),
            vm((2, 3, 16, 128), BF16),
            vm((48, 128), F32),
            vm((LOWS, KW, 768), BF16),
            vm((LOWS, KP, 128), F32),
            vm((PAIRS, KW, 512), BF16),
            vm((56, KO, 768), BF16),
            vm((16, KO, 256), BF16),
            vm((256, 1536), F32),
            vm((256, 1152), F32),
            vm((4, 1152, 128), F32),
            vm((5120, 128), F32),
            vm((LOWS, KP, 128), F32),
            vm((8 * KW, 256), F32),
            vm((8 * KW, 256), F32),
            vm((1536, 256), BF16),
            vm((256, 1536), BF16),
            vm((1152, 256), BF16),
            vm((128, 2304), BF16),
            pltpu.SemaphoreType.DMA((13,)),
        ],
        compiler_params=pltpu.CompilerParams(vmem_limit_bytes=VMEM_LIMIT),
        name="encoder_levels",
    )(*args)


def input_kernel(g1, g1_next, w1b, out, stage):
    for t in range(2):
        halves = []
        for lanes in (slice(0, 512), slice(256, 768)):
            rows = jnp.concatenate([g1[:, :, lanes], g1_next[:, :, lanes]], axis=0)
            parts = [rows[4 * t + u : 4 * t + u + 4].reshape(128, 512) for u in range(3)]
            halves.append(jnp.concatenate(parts, axis=1))
        total = product_turned(jnp.concatenate(halves, axis=0), w1b[...])
        for r in range(4):
            for p in range(4):
                rows = (p // 2) * 128 + r * 32
                value = total[rows : rows + 32, (p % 2) * 128 : (p % 2 + 1) * 128]
                stage[4 * t + r, pl.ds(p, 32, stride=4), :] = value
            out[4 * t + r] = stage[4 * t + r].astype(BF16)


def input_grad(g1, w1b):
    return pl.pallas_call(
        input_kernel,
        grid=(6,),
        out_shape=jax.ShapeDtypeStruct((ROWS, 128, 128), BF16),
        in_specs=[
            pl.BlockSpec((8, KO, 768), lambda i: (i, 0, 0)),
            pl.BlockSpec((2, KO, 768), lambda i: (4 * i + 4, 0, 0)),
            pl.BlockSpec((256, 1536), lambda i: (0, 0)),
        ],
        out_specs=pl.BlockSpec((8, 128, 128), lambda i: (i, 0, 0)),
        scratch_shapes=[pltpu.VMEM((8, 128, 128), F32)],
        compiler_params=pltpu.CompilerParams(vmem_limit_bytes=VMEM_LIMIT),
        cost_estimate=pl.CostEstimate(flops=2 * 6144 * 1152 * 128, bytes_accessed=8 * 1024 * 1024, transcendentals=0),
        name="input_grad",
    )(g1, g1, w1b)


def add_kernel(keep, other, out):
    out[...] = (keep[...].astype(F32) + other[...].astype(F32)).astype(BF16)


def add(keep, other):
    return pl.pallas_call(
        add_kernel,
        out_shape=jax.ShapeDtypeStruct(keep.shape, BF16),
        in_specs=[vmem_spec()] * 2,
        out_specs=vmem_spec(),
        name="add_core_terms",
    )(keep, other)


def collect(got):
    sums = got.astype(F32).sum(axis=0)
    return sums[0:9], sums[9:18], jnp.concatenate([sums[18:27], sums[27:36]], axis=1)


def swapped(block, axis, odd_first):
    devices = lax.axis_size(axis)
    pairs = []
    for i in range(1 if odd_first else 0, devices - 1, 2):
        pairs += [(i, i + 1), (i + 1, i)]
    return lax.ppermute(block, axis, pairs)


def body(inputs, weight_one, weight_two, weight_three, noise_table, frequency, anchor, noise_index, cotangent):
    grid = (lax.axis_size(ROW_AXES) * ROWS, lax.axis_size("tx") * 4 * KO)
    inputs = inputs.reshape(ROWS, 8, 16, 128)
    one, two, cots = sides(inputs, cotangent)
    one = swapped(one, "tx", False)
    two = swapped(two, "tx", True)
    w1t, w1b, w2t, w2b, w3b, rows_sc, cols_sc = prep(*grid, anchor, weight_one, weight_two, weight_three, frequency)
    off, near = rims(inputs, cots, one, two, rows_sc)
    off = swapped(off, ROW_AXES, True)
    near = lax.ppermute(near, "core", [(0, 1), (1, 0)])
    x1, d1, x2 = own_rows(*grid, noise_index, inputs, one, two, w1t, rows_sc, cols_sc, noise_table)
    coarse, g1, keep_msg, give_msg = levels(
        *grid, noise_index, cotangent, w1t, rows_sc, cols_sc, noise_table,
        off, near, one, two, w2t, w2b, weight_three, w3b, x1, d1, x2,
    )
    other = lax.ppermute(give_msg, "core", [(0, 1), (1, 0)])
    msg = add(keep_msg, other).reshape(64, 40, 128)
    got = lax.all_to_all(msg, ("chip", "tx"), 0, 0, tiled=True)
    grad_inputs = input_grad(g1, w1b)
    return (coarse, grad_inputs, *collect(got))


def solution(mesh):
    halves = jax.sharding.Mesh(mesh.devices.reshape(-1, 2, mesh.devices.shape[1]), ("chip", "core", "tx"))
    placed = (P(ROW_AXES, "tx", None), P(), P(), P(), P(), P(), P(), P(), P(ROW_AXES, "tx", None))
    return jax.shard_map(
        body,
        mesh=halves,
        in_specs=placed,
        out_specs=(
            P(ROW_AXES, "tx", None),
            P(ROW_AXES, "tx", None),
            P((*ROW_AXES, "tx"), None),
            P((*ROW_AXES, "tx"), None),
            P((*ROW_AXES, "tx"), None),
        ),
        check_vma=False,
    )
```

```python
import jax
import jax.numpy as jnp
from jax import lax
from jax.experimental import pallas as pl
from jax.experimental.pallas import tpu as pltpu
from jax.sharding import PartitionSpec as P

BF16 = jnp.bfloat16
F32 = jnp.float32

KO = 32
KP = 40
KW = 48
HALO = 16
ROWS = 48
PAD_ROWS = ROWS + 2 * HALO
PAIRS = PAD_ROWS // 2
LOWS = PAIRS // 2
VMEM_LIMIT = 60 * 1024 * 1024


def any_spec():
    return pl.BlockSpec(memory_space=pl.ANY)


def vmem_spec():
    return pl.BlockSpec(memory_space=pltpu.VMEM)


def smem_spec():
    return pl.BlockSpec(memory_space=pltpu.SMEM)


ROW_AXES = ("chip", "core")


def own_place():
    return lax.axis_index(ROW_AXES), lax.axis_index("tx")


def odd_column():
    return lax.rem(lax.axis_index("tx"), 2)


def side_kernel(inputs, cot, one, two, cots, side32, sems):
    odd = odd_column()
    copies = [
        pltpu.make_async_copy(inputs.at[:, 7 - 7 * odd], one.at[pl.ds(1, ROWS)], sems.at[0]),
        pltpu.make_async_copy(inputs.at[:, 7 * odd], two.at[pl.ds(1, ROWS)], sems.at[1]),
    ]
    for copy in copies:
        copy.start()
    for target, at_left in ((one, odd == 1), (two, odd == 0)):
        for r in range(12):
            line = cot[r].astype(F32)
            for h in range(2):
                lanes = slice(h * 128, (h + 1) * 128)
                side32[pl.ds(r * 4 + h * 2, 2)] = jnp.where(at_left, line[0:2, lanes], line[30:32, lanes])
        side = side32[...].astype(BF16).reshape(3, 16, 128)
        target[pl.ds(0, 1)] = side[0:1]
        target[pl.ds(1 + ROWS, 3)] = side
    for at, start in ((0, 10), (1, 0)):
        for r in range(2):
            for h in range(2):
                cots[at, pl.ds((r * 2 + h) * 2, 2)] = cot[start + r, :, h * 128 : (h + 1) * 128].reshape(2, 16, 128)
    for copy in copies:
        copy.wait()


def sides(inputs, cot):
    return pl.pallas_call(
        side_kernel,
        out_shape=[jax.ShapeDtypeStruct((ROWS + 4, 16, 128), BF16)] * 2 + [jax.ShapeDtypeStruct((2, 8, 16, 128), BF16)],
        in_specs=[any_spec(), vmem_spec()],
        out_specs=[vmem_spec()] * 3,
        scratch_shapes=[pltpu.VMEM((48, 128), F32), pltpu.SemaphoreType.DMA((2,))],
        compiler_params=pltpu.CompilerParams(vmem_limit_bytes=VMEM_LIMIT),
        name="pack_columns",
    )(inputs, cot)


def rim_kernel(inputs, cots, one, two, _, off, near, sems):
    core = lax.axis_index("core")
    copies = []

    def fetch(source, target):
        copy = pltpu.make_async_copy(source, target, sems.at[len(copies)])
        copy.start()
        copies.append(copy)

    body = pl.ds(0, HALO)
    for target, low in ((off, core), (near, 1 - core)):
        row = (ROWS - HALO) * low
        fetch(inputs.at[pl.ds(row, HALO)], target.at[body, pl.ds(0, 8)])
        fetch(cots.at[1 - low], target.at[HALO, pl.ds(0, 8)])
        for unit, side in ((8, one), (9, two)):
            fetch(side.at[pl.ds(1 + row, HALO)], target.at[body, unit])
            fetch(side.at[(3 + ROWS) * low], target.at[HALO, unit])
    for copy in copies:
        copy.wait()


def rims(*args):
    return pl.pallas_call(
        rim_kernel,
        out_shape=[jax.ShapeDtypeStruct((HALO + 1, 10, 16, 128), BF16)] * 2,
        in_specs=[any_spec()] * len(args),
        out_specs=[vmem_spec()] * 2,
        scratch_shapes=[pltpu.SemaphoreType.DMA((12,))],
        compiler_params=pltpu.CompilerParams(vmem_limit_bytes=VMEM_LIMIT),
        name="pack_rows",
    )(*args)


def weight_forms(w1, w2, w3, w1t, w1b, w2t, w2b, w3b):
    zero = jnp.zeros((128, 128), BF16)
    for source, ahead, back in ((w1, w1t, w1b), (w2, w2t, w2b)):
        for u in range(3):
            for v in range(3):
                tap = source[pl.ds((3 * u + v) * 128, 128), :]
                for i in range(2):
                    side = slice(i * 128, (i + 1) * 128)
                    ahead[pl.ds((4 * u + v + i) * 128, 128), side] = tap
                    at = (4 * (2 - u) + 2 - v + i) * 128
                    back[side, at : at + 128] = tap
            for i, j in ((0, 3), (1, 0)):
                at = (4 * u + j) * 128
                side = slice(i * 128, (i + 1) * 128)
                ahead[pl.ds(at, 128), side] = zero
                back[side, at : at + 128] = zero
    for u in range(3):
        for v in range(3):
            at = (3 * (2 - u) + 2 - v) * 256
            w3b[:, at : at + 256] = w3[pl.ds((3 * u + v) * 128, 128), :]


def wave_tables(grid_rows, grid_cols, anchor, frequency, rows_sc, cols_sc):
    own_row, own_col = own_place()
    row = lax.broadcasted_iota(jnp.int32, (PAD_ROWS, 128), 0) - HALO + own_row * ROWS
    angle = (row + anchor[0]).astype(F32) * frequency[0:1, :]
    keep = jnp.where((row >= 0) & (row < grid_rows), 1.0, 0.0)
    rows_sc[0] = jnp.sin(angle) * keep
    rows_sc[1] = jnp.cos(angle) * keep
    for p in range(4):
        k = lax.broadcasted_iota(jnp.int32, (KP, 128), 0)
        col = 4 * jnp.where(k < KO + 4, k, k - KP) + p + own_col * (4 * KO)
        angle = (col + anchor[1]).astype(F32) * frequency[1:2, :]
        keep = jnp.where((col >= 0) & (col < grid_cols), 1.0, 0.0)
        cols_sc[0, p] = jnp.sin(angle) * keep
        cols_sc[1, p] = jnp.cos(angle) * keep


def prep_kernel(grid_rows, grid_cols, anchor, w1, w2, w3, frequency, w1t, w1b, w2t, w2b, w3b, rows_sc, cols_sc):
    weight_forms(w1, w2, w3, w1t, w1b, w2t, w2b, w3b)
    wave_tables(grid_rows, grid_cols, anchor, frequency, rows_sc, cols_sc)


def prep(grid_rows, grid_cols, anchor, w1, w2, w3, frequency):
    def kernel(*refs):
        prep_kernel(grid_rows, grid_cols, *refs)

    shape = jax.ShapeDtypeStruct
    return pl.pallas_call(
        kernel,
        out_shape=[
            shape((1536, 256), BF16),
            shape((256, 1536), BF16),
            shape((1536, 256), BF16),
            shape((256, 1536), BF16),
            shape((128, 2304), BF16),
            shape((2, PAD_ROWS, 128), F32),
            shape((2, 4, KP, 128), F32),
        ],
        in_specs=[smem_spec()] + [vmem_spec()] * 4,
        out_specs=[vmem_spec()] * 7,
        compiler_params=pltpu.CompilerParams(vmem_limit_bytes=VMEM_LIMIT),
        name="weight_forms",
    )(anchor, w1, w2, w3, frequency)


def fill_mask(low_rows, low_cols, mask):
    own_row, own_col = own_place()
    k = lax.broadcasted_iota(jnp.int32, (KP, 128), 0)
    col = jnp.where(k < KO + 4, k, k - KP) + own_col * KO
    inside = jnp.where((col >= 0) & (col < low_cols), 1.0, 0.0)

    def step(at, _):
        row = at - 4 + own_row * 12
        mask[at] = inside * jnp.where((row >= 0) & (row < low_rows), 1.0, 0.0)
        return 0

    lax.fori_loop(0, LOWS, step, 0)


def widened(line):
    rest = jnp.zeros((KW - KP, line.shape[1]), F32)
    return jnp.concatenate([line, rest], axis=0).astype(BF16)


def put_line(ref, row, planes):
    width = planes[0].shape[1]
    for n, plane in enumerate(planes):
        ref[row, :, n * width : (n + 1) * width] = widened(plane)


def before(line):
    return pltpu.roll(line, 1, 0)


def after(line):
    return pltpu.roll(line, KP - 1, 0)


def silu_parts(half):
    th = jnp.tanh(half)
    act = half + half * th
    return act, (1.0 + act) + th * (1.0 - act)


def rounded(value):
    return value.astype(BF16).astype(F32)


def flat(block):
    return block.reshape(128, 128)


def modulation(noise, noise_index):
    modulate = noise[pl.ds(noise_index[0], 1), :]
    return 1.0 + modulate[:, 0:128], modulate[:, 128:256]


def first_lines(load, base, at, tables, stage, x1):
    rows_sc, cols_sc = tables
    for i in range(4):
        own, right, left = load(i)
        stage[i, 0:128] = own.astype(F32)
        stage[i, 128:144] = right.astype(F32)
        stage[i, 144:160] = left.astype(F32)
        sin_row = rows_sc[0, pl.ds(base + i, 1), :]
        cos_row = rows_sc[1, pl.ds(base + i, 1), :]
        planes = []
        for p in range(4):
            value = stage[i, pl.ds(p, KP, stride=4), :]
            planes.append(value + (sin_row * cols_sc[1, p] + cos_row * cols_sc[0, p]))
        put_line(x1, at + i, [before(planes[3])] + planes + [after(planes[0])])


def around(ref, at, count, lanes, cols=KW):
    parts = [ref[pl.ds(at - 1 + u, count), 0:cols, lanes] for u in range(3)]
    return jnp.concatenate([part.reshape(count * cols, part.shape[-1]) for part in parts], axis=1)


def product(left, right):
    return jnp.dot(left, right, preferred_element_type=F32)


def product_turned(left, right):
    return lax.dot_general(left, right, (((1,), (1,)), ((), ())), preferred_element_type=F32)


def weight_terms(grad, field):
    return lax.dot_general(grad, field, (((0,), (0,)), ((), ())), preferred_element_type=F32)


def pipeline(steps, dot, post, z0, z1):
    def put(z, t):
        total = dot(t)
        z[0 : total.shape[0], :] = total

    put(z0, 0)

    def two(i, _):
        put(z1, 2 * i + 1)
        post(2 * i, z0)
        put(z0, 2 * i + 2)
        post(2 * i + 1, z1)
        return 0

    if steps > 2:
        lax.fori_loop(0, (steps - 1) // 2, two, 0)
    if steps % 2 == 0:
        put(z1, steps - 1)
        post(steps - 2, z0)
        post(steps - 1, z1)
    else:
        post(steps - 1, z0)


def conv_one_dot(x1, row, w1t):
    one = around(x1, row, 4, slice(0, 512))
    two = around(x1, row, 4, slice(256, 768))
    return product(jnp.concatenate([one, two], axis=0), w1t[...])


def conv_one_post(z, scale, shift, keeps, d1, d1_row, x2, x2_row):
    half_scale, half_shift = 0.5 * scale, 0.5 * shift
    slope_scale = half_scale.astype(BF16)
    for s in range(2):
        halves = []
        for q in range(2):
            sums = []
            for p in (2 * q, 2 * q + 1):
                lanes = slice((p % 2) * 128, (p % 2 + 1) * 128)
                acts = []
                for r in range(2):
                    at = q * 4 * KW + (2 * s + r) * KW
                    act, slope = silu_parts((z[at : at + KW, lanes] * half_scale + half_shift).astype(BF16))
                    d1[d1_row + 2 * s + r, :, p * 128 : (p + 1) * 128] = slope_scale * slope
                    acts.append(act)
                sums.append((acts[0] + acts[1]).astype(F32))
            halves.append((sums[0] + sums[1])[:KP] * (0.25 * keeps[s]))
        put_line(x2, x2_row + s, [before(halves[1]), halves[0], halves[1], after(halves[0])])


def own_kernel(
    grid_rows, grid_cols,
    noise_index, rows_sc, cols_sc, noise, inputs_in, one, two, w1t_in,
    x1_out, d1_out, x2_out,
    x1, stage, d1, x2, mask, side, inputs, w1t, z0, z1, sems,
):
    odd = odd_column()
    halos = [
        pltpu.make_async_copy(one, side.at[1 - odd], sems.at[0]),
        pltpu.make_async_copy(two, side.at[odd], sems.at[1]),
    ]
    early = pltpu.make_async_copy(inputs_in.at[pl.ds(0, 12)], inputs.at[pl.ds(0, 12)], sems.at[5])
    got_w1t = pltpu.make_async_copy(w1t_in, w1t, sems.at[6])
    late = pltpu.make_async_copy(inputs_in.at[pl.ds(12, 36)], inputs.at[pl.ds(12, 36)], sems.at[7])
    for copy in (*halos, early, got_w1t, late):
        copy.start()
    fill_mask(grid_rows // 4, grid_cols // 4, mask)
    scale, shift = modulation(noise, noise_index)
    for copy in (*halos, early):
        copy.wait()

    def first(q):
        def load(i):
            row = 4 * q + i
            return flat(inputs[row]), side[1, 1 + row], side[0, 1 + row]

        first_lines(load, HALO + 4 * q, 4 * q, (rows_sc, cols_sc), stage, x1)
        part = pl.ds(4 * q, 4)
        pltpu.make_async_copy(x1.at[part], x1_out.at[part], sems.at[2]).start()

    def dot(t):
        return conv_one_dot(x1, 4 * t + 2, w1t)

    def post(t, z):
        keeps = [mask[(9 + 2 * t) // 2], mask[(10 + 2 * t) // 2]]
        conv_one_post(z, scale, shift, keeps, d1, 4 * t, x2, 2 * t)
        part = pl.ds(4 * t, 4)
        pltpu.make_async_copy(d1.at[part], d1_out.at[part], sems.at[3]).start()

    first(0)
    first(1)
    got_w1t.wait()
    z0[...] = dot(0)
    first(2)
    late.wait()

    def two_steps(i, _):
        t = 2 * i + 1
        z1[...] = dot(t)
        first(t + 2)
        post(t - 1, z0)
        z0[...] = dot(t + 1)
        first(t + 3)
        post(t, z1)
        return 0

    lax.fori_loop(0, 4, two_steps, 0)
    z1[...] = dot(9)
    first(11)
    post(8, z0)
    z0[...] = dot(10)
    post(9, z1)
    post(10, z0)
    last = pltpu.make_async_copy(x2, x2_out, sems.at[4])
    last.start()
    pltpu.make_async_copy(x1, x1_out, sems.at[2]).wait()
    pltpu.make_async_copy(d1, d1_out, sems.at[3]).wait()
    last.wait()


def own_rows(grid_rows, grid_cols, *args):
    def kernel(*refs):
        own_kernel(grid_rows, grid_cols, *refs)

    vm = pltpu.VMEM
    shape = jax.ShapeDtypeStruct
    return pl.pallas_call(
        kernel,
        out_shape=[shape((48, KW, 768), BF16), shape((44, KW, 512), BF16), shape((22, KW, 512), BF16)],
        in_specs=[smem_spec()] + [vmem_spec()] * 3 + [any_spec()] * 4,
        out_specs=[any_spec()] * 3,
        scratch_shapes=[
            vm((48, KW, 768), BF16),
            vm((4, 160, 128), F32),
            vm((44, KW, 512), BF16),
            vm((22, KW, 512), BF16),
            vm((LOWS, KP, 128), F32),
            vm((2, ROWS + 4, 16, 128), BF16),
            vm((ROWS, 8, 16, 128), BF16),
            vm((1536, 256), BF16),
            vm((8 * KW, 256), F32),
            vm((8 * KW, 256), F32),
            pltpu.SemaphoreType.DMA((8,)),
        ],
        compiler_params=pltpu.CompilerParams(vmem_limit_bytes=VMEM_LIMIT),
        cost_estimate=pl.CostEstimate(flops=4 * 10**9, bytes_accessed=30 * 10**6, transcendentals=0),
        name="own_rows",
    )(*args)


def lines_kernel(
    grid_rows, grid_cols,
    noise_index, rows_sc, cols_sc, noise,
    cot_in, w1t_in, off, near, one, two, w2t_in, w2b_in, w3_in, w3b_in, x1_in, d1_in, x2_in,
    coarse_out, g1_out, keep_out, give_out,
    rim, stage, x1, d1, x2, d2, x3, cp, side, side32, g3, xb2, g2, g1, coarse,
    acc, acc3, gw, msg, mask, z0, z1, cot, w1t, w2t, w2b, w3, w3b, sems,
):
    core = lax.axis_index("core")
    odd = odd_column()

    def fetch(source, target, at):
        copy = pltpu.make_async_copy(source, target, sems.at[at])
        copy.start()
        return copy

    got_rims = [fetch(off, rim.at[core], 0), fetch(near, rim.at[1 - core], 1)]
    got_edges = [
        fetch(x1_in.at[pl.ds(0, 4)], x1.at[pl.ds(16, 4)], 2),
        fetch(x1_in.at[pl.ds(44, 4)], x1.at[pl.ds(60, 4)], 3),
    ]
    got_w1t = fetch(w1t_in, w1t, 13)
    got_x2 = fetch(x2_in, x2.at[pl.ds(9, 22)], 4)
    units = pl.ds(ROWS + 1, 3)
    got_sides = [fetch(one.at[units], side.at[1 - odd], 5), fetch(two.at[units], side.at[odd], 6)]
    got_cot = fetch(cot_in, cot, 14)
    got_w2t = fetch(w2t_in, w2t, 7)
    got_w3 = [fetch(w3_in, w3, 8), fetch(w3b_in, w3b, 9)]
    got_w2b = fetch(w2b_in, w2b, 10)
    got_d1 = fetch(d1_in, d1.at[pl.ds(18, 44)], 11)
    got_x1 = fetch(x1_in.at[pl.ds(4, 40)], x1.at[pl.ds(20, 40)], 12)
    fill_mask(grid_rows // 4, grid_cols // 4, mask)
    gw[:, 0:8, :] = jnp.zeros((4, 8, 128), F32)
    gw[:, 1160:1168, :] = jnp.zeros((4, 8, 128), F32)
    scale, shift = modulation(noise, noise_index)
    for copy in got_rims:
        copy.wait()

    def first(n):
        below = n // 4
        start = 4 * (n % 4)
        base = start + (HALO + ROWS) * below

        def load(i):
            row = start + i
            return flat(rim[below, row, 0:8]), rim[below, row, 8 + odd], rim[below, row, 9 - odd]

        first_lines(load, base, base, (rows_sc, cols_sc), stage, x1)

    def mid_of(t):
        return jnp.where(t < 4, 1 + 2 * t, 23 + 2 * t)

    def dot(t):
        return conv_one_dot(x1, 2 * mid_of(t), w1t)

    def post(t, z):
        m = mid_of(t)
        conv_one_post(z, scale, shift, [mask[m // 2], mask[(m + 1) // 2]], d1, 2 * m, x2, m)

    first(0)
    first(1)
    for copy in (*got_edges, got_w1t):
        copy.wait()
    z0[...] = dot(0)
    first(2)

    def two_steps(i, _):
        t = 2 * i + 1
        z1[...] = dot(t)
        first(t + 2)
        post(t - 1, z0)
        z0[...] = dot(t + 1)
        first(t + 3)
        post(t, z1)
        return 0

    lax.fori_loop(0, 2, two_steps, 0)
    z1[...] = dot(5)
    first(7)
    post(4, z0)
    z0[...] = dot(6)
    post(5, z1)
    z1[...] = dot(7)
    post(6, z0)
    post(7, z1)
    got_x2.wait()
    got_w2t.wait()

    def conv_two_post(t, z):
        for s in range(3):
            low = 1 + 3 * t + s
            total = None
            for q in range(2):
                lanes = slice(q * 128, (q + 1) * 128)
                for r in range(2):
                    row, at = 2 * low + r, (2 * s + r) * KW
                    act, slope = silu_parts(0.5 * z[at : at + KP, lanes])
                    d2[row, :, lanes] = 0.5 * slope
                    down = x2[row, :, (q + 1) * 128 : (q + 2) * 128].astype(F32)[:KP]
                    act = rounded(down + act)
                    total = act if total is None else total + act
            line = total * (0.25 * mask[low])
            put_line(x3, low, [before(line), line, after(line)])

    pipeline(6, lambda t: product(around(x2, 2 + 6 * t, 6, slice(0, 512)), w2t[...]), conv_two_post, z0, z1)

    cp[...] = jnp.zeros_like(cp)
    for copy in (*got_sides, got_cot):
        copy.wait()
    for h in range(2):
        lanes = slice(h * 128, (h + 1) * 128)
        for r in range(2):
            units = pl.ds((r * 2 + h) * 2, 2)
            cp[r, 0:KO, lanes] = rim[0, HALO, units].reshape(KO, 128).astype(F32)
            cp[14 + r, 0:KO, lanes] = rim[1, HALO, units].reshape(KO, 128).astype(F32)
    for r in range(12):
        cp[2 + r, 0:KO, :] = cot[r].astype(F32)
    for which, at in ((1, KO), (0, KP - 2)):
        side32[...] = side[which].reshape(48, 128).astype(F32)
        for h in range(2):
            for r in range(12):
                cp[2 + r, at : at + 2, h * 128 : (h + 1) * 128] = side32[r * 4 + h * 2 : r * 4 + h * 2 + 2]
    for below, skip, row in ((0, 8, 0), (1, 0, 14)):
        for unit, at in ((9 - odd, KP - 2), (8 + odd, KO)):
            side32[0:16] = rim[below, HALO, unit].astype(F32)
            for h in range(2):
                for r in range(2):
                    start = skip + r * 4 + h * 2
                    cp[row + r, at : at + 2, h * 128 : (h + 1) * 128] = side32[start : start + 2]
    for copy in got_w3:
        copy.wait()
    g3[1] = jnp.zeros((KW, 768), BF16)
    g3[18] = jnp.zeros((KW, 768), BF16)

    def conv_three_post(t, z):
        for i in range(4):
            row = 2 + 4 * t + i
            act, slope = silu_parts(0.5 * z[i * KW : i * KW + KP, :])
            keep = 0.5 * mask[row]
            line = cp[row - 2] * slope * jnp.concatenate([keep, keep], axis=1)
            put_line(g3, row, [before(line), line, after(line)])
            coarse[row - 2] = act[:KO].astype(BF16)

    pipeline(4, lambda t: product(around(x3, 2 + 4 * t, 4, slice(0, 384)), w3[...]), conv_three_post, z0, z1)
    put_coarse = fetch(coarse.at[pl.ds(2, 12)], coarse_out, 0)

    def back_three_post(t, z):
        for i in range(4):
            low = 2 + 4 * t + i
            line = 0.25 * z[i * KW : i * KW + KP, 0:128]
            xb2[low] = line
            line = line * mask[low]
            for r in range(2):
                row = 2 * low + r
                zero, one = (line * d2[row, :, q * 128 : (q + 1) * 128] for q in range(2))
                put_line(g2, row, [before(one), zero, one, after(zero)])

    def back_three_dot(t):
        total = product_turned(around(g3, 2 + 4 * t, 4, slice(0, 768)), w3b[...])
        return jnp.concatenate([total, total], axis=1)

    pipeline(4, back_three_dot, back_three_post, z0, z1)
    acc3[...] = weight_terms(
        g3[4:16, 0:KO, 256:512].reshape(12 * KO, 256), around(x3, 4, 12, slice(0, 384), KO)
    )
    acc[...] = weight_terms(
        g2[8:32, 0:KO, 128:384].reshape(24 * KO, 256), around(x2, 8, 24, slice(0, 512), KO)
    )
    got_w2b.wait()
    got_d1.wait()

    def back_two_post(t, z):
        for i in range(4):
            m = 6 + 4 * t + i
            low = m // 2
            keep = 0.25 * mask[low]
            base = xb2[low]
            both = [(base + z[i * KW : i * KW + KP, q * 128 : (q + 1) * 128]) * keep for q in range(2)]
            for r in range(2):
                row = 2 * m + r
                slopes = [d1[row, :, p * 128 : (p + 1) * 128].astype(F32)[:KP] for p in range(4)]
                planes = [both[p // 2] * slopes[p] for p in range(4)]
                for n, line in enumerate([before(planes[3])] + planes + [after(planes[0])]):
                    g1[row - 12, :, n * 128 : (n + 1) * 128] = line[:KO].astype(BF16)

    pipeline(
        7, lambda t: product_turned(around(g2, 6 + 4 * t, 4, slice(0, 512)), w2b[...]), back_two_post, z0, z1
    )
    put_g1 = fetch(g1.at[pl.ds(3, 50)], g1_out, 1)
    got_x1.wait()

    def fold_weights(at):
        for u in range(3):
            for v in range(3):
                left = (4 * u + v) * 128
                term = acc[0:128, left : left + 128] + acc[128:256, left + 128 : left + 256]
                gw[at, pl.ds(8 + (3 * u + v) * 128, 128), :] = term.T

    def one_chunk(t):
        grads = jnp.concatenate(
            [g1[4 + 16 * t : 20 + 16 * t, :, lanes].reshape(512, 256) for lanes in (slice(128, 384), slice(384, 640))],
            axis=0,
        )
        fields = jnp.concatenate(
            [around(x1, 16 + 16 * t, 16, lanes, KO) for lanes in (slice(0, 512), slice(256, 768))], axis=0
        )
        return weight_terms(grads, fields)

    fold_weights(1)
    acc[...] = one_chunk(0)
    for tap in range(9):
        turned = acc3[:, tap * 128 : (tap + 1) * 128].T
        gw[2, pl.ds(8 + tap * 128, 128), :] = turned[:, 0:128]
        gw[3, pl.ds(8 + tap * 128, 128), :] = turned[:, 128:256]
    acc[...] += one_chunk(1)
    acc[...] += one_chunk(2)
    fold_weights(0)
    line = lax.broadcasted_iota(jnp.int32, (8, 128), 0)
    none = jnp.zeros((8, 128), F32)
    for owner in range(128):
        at = 8 + 9 * owner
        parts = [gw[0, at : at + 8, :]]
        for t in range(1, 5):
            rest = gw[t - 1, at + 9 - t : at + 17 - t, :]
            start = gw[t, at - t : at + 8 - t, :] if t < 4 else none
            parts.append(jnp.where(line < t, rest, start))
        row, col = divmod(owner, 8)
        msg[row % 2, (row // 2) * 8 + col] = jnp.concatenate(parts, axis=0).astype(BF16)
    put_keep = fetch(msg.at[core], keep_out, 2)
    put_give = fetch(msg.at[1 - core], give_out, 3)
    put_keep.wait()
    put_give.wait()
    put_coarse.wait()
    put_g1.wait()


def levels(grid_rows, grid_cols, *args):
    def kernel(*refs):
        lines_kernel(grid_rows, grid_cols, *refs)

    vm = pltpu.VMEM
    return pl.pallas_call(
        kernel,
        out_shape=[
            jax.ShapeDtypeStruct((12, KO, 256), BF16),
            jax.ShapeDtypeStruct((50, KO, 768), BF16),
            jax.ShapeDtypeStruct((64, 40, 128), BF16),
            jax.ShapeDtypeStruct((64, 40, 128), BF16),
        ],
        in_specs=[smem_spec()] + [vmem_spec()] * 3 + [any_spec()] * 13,
        out_specs=[any_spec()] * 4,
        scratch_shapes=[
            vm((2, HALO + 1, 10, 16, 128), BF16),
            vm((4, 160, 128), F32),
            vm((PAD_ROWS, KW, 768), BF16),
            vm((PAD_ROWS, KW, 512), BF16),
            vm((PAIRS, KW, 512), BF16),
            vm((PAIRS, KP, 256), F32),
            vm((LOWS, KW, 384), BF16),
            vm((16, KP, 256), F32),
            vm((2, 3, 16, 128), BF16),
            vm((48, 128), F32),
            vm((LOWS, KW, 768), BF16),
            vm((LOWS, KP, 128), F32),
            vm((PAIRS, KW, 512), BF16),
            vm((56, KO, 768), BF16),
            vm((16, KO, 256), BF16),
            vm((256, 1536), F32),
            vm((256, 1152), F32),
            vm((4, 1168, 128), F32),
            vm((2, 64, 40, 128), BF16),
            vm((LOWS, KP, 128), F32),
            vm((8 * KW, 256), F32),
            vm((8 * KW, 256), F32),
            vm((12, KO, 256), BF16),
            vm((1536, 256), BF16),
            vm((1536, 256), BF16),
            vm((256, 1536), BF16),
            vm((1152, 256), BF16),
            vm((128, 2304), BF16),
            pltpu.SemaphoreType.DMA((15,)),
        ],
        compiler_params=pltpu.CompilerParams(vmem_limit_bytes=VMEM_LIMIT),
        name="encoder_levels",
    )(*args)


def input_kernel(g1, g1_next, w1b, out, stage):
    for t in range(2):
        halves = []
        for lanes in (slice(0, 512), slice(256, 768)):
            rows = jnp.concatenate([g1[:, :, lanes], g1_next[:, :, lanes]], axis=0)
            parts = [rows[4 * t + u : 4 * t + u + 4].reshape(128, 512) for u in range(3)]
            halves.append(jnp.concatenate(parts, axis=1))
        total = product_turned(jnp.concatenate(halves, axis=0), w1b[...])
        for r in range(4):
            for p in range(4):
                rows = (p // 2) * 128 + r * 32
                value = total[rows : rows + 32, (p % 2) * 128 : (p % 2 + 1) * 128]
                stage[4 * t + r, pl.ds(p, 32, stride=4), :] = value
            out[4 * t + r] = stage[4 * t + r].astype(BF16)


def input_grad(g1, w1b):
    return pl.pallas_call(
        input_kernel,
        grid=(6,),
        out_shape=jax.ShapeDtypeStruct((ROWS, 128, 128), BF16),
        in_specs=[
            pl.BlockSpec((8, KO, 768), lambda i: (i, 0, 0)),
            pl.BlockSpec((2, KO, 768), lambda i: (4 * i + 4, 0, 0)),
            pl.BlockSpec((256, 1536), lambda i: (0, 0)),
        ],
        out_specs=pl.BlockSpec((8, 128, 128), lambda i: (i, 0, 0)),
        scratch_shapes=[pltpu.VMEM((8, 128, 128), F32)],
        compiler_params=pltpu.CompilerParams(vmem_limit_bytes=VMEM_LIMIT),
        cost_estimate=pl.CostEstimate(flops=2 * 6144 * 1152 * 128, bytes_accessed=8 * 1024 * 1024, transcendentals=0),
        name="input_grad",
    )(g1, g1, w1b)


def add_kernel(keep, other, out):
    out[...] = (keep[...].astype(F32) + other[...].astype(F32)).astype(BF16)


def add(keep, other):
    block = pl.BlockSpec((16, 40, 128), lambda i: (i, 0, 0))
    return pl.pallas_call(
        add_kernel,
        grid=(4,),
        out_shape=jax.ShapeDtypeStruct(keep.shape, BF16),
        in_specs=[block] * 2,
        out_specs=block,
        compiler_params=pltpu.CompilerParams(vmem_limit_bytes=VMEM_LIMIT),
        name="add_core_terms",
    )(keep, other)


def collect(got):
    sums = got.astype(F32).sum(axis=0)
    return sums[0:9], sums[9:18], jnp.concatenate([sums[18:27], sums[27:36]], axis=1)


def swapped(block, axis, odd_first):
    devices = lax.axis_size(axis)
    pairs = []
    for i in range(1 if odd_first else 0, devices - 1, 2):
        pairs += [(i, i + 1), (i + 1, i)]
    return lax.ppermute(block, axis, pairs)


def body(inputs, weight_one, weight_two, weight_three, noise_table, frequency, anchor, noise_index, cotangent):
    grid = (lax.axis_size(ROW_AXES) * ROWS, lax.axis_size("tx") * 4 * KO)
    inputs = inputs.reshape(ROWS, 8, 16, 128)
    one, two, cots = sides(inputs, cotangent)
    two = swapped(two, "tx", True)
    one = swapped(one, "tx", False)
    w1t, w1b, w2t, w2b, w3b, rows_sc, cols_sc = prep(*grid, anchor, weight_one, weight_two, weight_three, frequency)
    off, near = rims(inputs, cots, one, two, rows_sc)
    off = swapped(off, ROW_AXES, True)
    near = lax.ppermute(near, "core", [(0, 1), (1, 0)])
    x1, d1, x2 = own_rows(*grid, noise_index, rows_sc, cols_sc, noise_table, inputs, one, two, w1t)
    coarse, g1, keep_msg, give_msg = levels(
        *grid, noise_index, rows_sc, cols_sc, noise_table, cotangent, w1t,
        off, near, one, two, w2t, w2b, weight_three, w3b, x1, d1, x2,
    )
    other = lax.ppermute(give_msg, "core", [(0, 1), (1, 0)])
    msg = add(keep_msg, other)
    got = lax.all_to_all(msg, ("chip", "tx"), 0, 0, tiled=True)
    grad_inputs = input_grad(g1, w1b)
    return (coarse, grad_inputs, *collect(got))


def solution(mesh):
    halves = jax.sharding.Mesh(mesh.devices.reshape(-1, 2, mesh.devices.shape[1]), ("chip", "core", "tx"))
    placed = (P(ROW_AXES, "tx", None), P(), P(), P(), P(), P(), P(), P(), P(ROW_AXES, "tx", None))
    return jax.shard_map(
        body,
        mesh=halves,
        in_specs=placed,
        out_specs=(
            P(ROW_AXES, "tx", None),
            P(ROW_AXES, "tx", None),
            P((*ROW_AXES, "tx"), None),
            P((*ROW_AXES, "tx"), None),
            P((*ROW_AXES, "tx"), None),
        ),
        check_vma=False,
    )
```

```python
import jax
import jax.numpy as jnp
from jax import lax
from jax.experimental import pallas as pl
from jax.experimental.pallas import tpu as pltpu
from jax.sharding import PartitionSpec as P

BF16 = jnp.bfloat16
F32 = jnp.float32

KO = 32
KP = 40
KW = 48
HALO = 16
ROWS = 48
PAD_ROWS = ROWS + 2 * HALO
PAIRS = PAD_ROWS // 2
LOWS = PAIRS // 2
MIB = 1024 * 1024


def any_spec():
    return pl.BlockSpec(memory_space=pl.ANY)


def vmem_spec():
    return pl.BlockSpec(memory_space=pltpu.VMEM)


def smem_spec():
    return pl.BlockSpec(memory_space=pltpu.SMEM)


ROW_AXES = ("chip", "core")


def own_place():
    return lax.axis_index(ROW_AXES), lax.axis_index("tx")


def odd_column():
    return lax.rem(lax.axis_index("tx"), 2)


def side_kernel(inputs, cot, one, two, cots, side32, sems):
    odd = odd_column()
    copies = [
        pltpu.make_async_copy(inputs.at[:, 7 - 7 * odd], one.at[pl.ds(1, ROWS)], sems.at[0]),
        pltpu.make_async_copy(inputs.at[:, 7 * odd], two.at[pl.ds(1, ROWS)], sems.at[1]),
    ]
    for copy in copies:
        copy.start()
    for target, at_left in ((one, odd == 1), (two, odd == 0)):
        for r in range(12):
            line = cot[r].astype(F32)
            for h in range(2):
                lanes = slice(h * 128, (h + 1) * 128)
                side32[pl.ds(r * 4 + h * 2, 2)] = jnp.where(at_left, line[0:2, lanes], line[30:32, lanes])
        side = side32[...].astype(BF16).reshape(3, 16, 128)
        target[pl.ds(0, 1)] = side[0:1]
        target[pl.ds(1 + ROWS, 3)] = side
    for at, start in ((0, 10), (1, 0)):
        for r in range(2):
            for h in range(2):
                cots[at, pl.ds((r * 2 + h) * 2, 2)] = cot[start + r, :, h * 128 : (h + 1) * 128].reshape(2, 16, 128)
    for copy in copies:
        copy.wait()


def sides(inputs, cot):
    return pl.pallas_call(
        side_kernel,
        out_shape=[jax.ShapeDtypeStruct((ROWS + 4, 16, 128), BF16)] * 2 + [jax.ShapeDtypeStruct((2, 8, 16, 128), BF16)],
        in_specs=[any_spec(), vmem_spec()],
        out_specs=[vmem_spec()] * 3,
        scratch_shapes=[pltpu.VMEM((48, 128), F32), pltpu.SemaphoreType.DMA((2,))],
        compiler_params=pltpu.CompilerParams(vmem_limit_bytes=8 * MIB),
        name="pack_columns",
    )(inputs, cot)


def rim_kernel(inputs, cots, one, two, _, off, near, sems):
    core = lax.axis_index("core")
    copies = []

    def fetch(source, target):
        copy = pltpu.make_async_copy(source, target, sems.at[len(copies)])
        copy.start()
        copies.append(copy)

    body = pl.ds(0, HALO)
    for target, low in ((off, core), (near, 1 - core)):
        row = (ROWS - HALO) * low
        fetch(inputs.at[pl.ds(row, HALO)], target.at[body, pl.ds(0, 8)])
        fetch(cots.at[1 - low], target.at[HALO, pl.ds(0, 8)])
        for unit, side in ((8, one), (9, two)):
            fetch(side.at[pl.ds(1 + row, HALO)], target.at[body, unit])
            fetch(side.at[(3 + ROWS) * low], target.at[HALO, unit])
    for copy in copies:
        copy.wait()


def rims(*args):
    return pl.pallas_call(
        rim_kernel,
        out_shape=[jax.ShapeDtypeStruct((HALO + 1, 10, 16, 128), BF16)] * 2,
        in_specs=[any_spec()] * len(args),
        out_specs=[vmem_spec()] * 2,
        scratch_shapes=[pltpu.SemaphoreType.DMA((12,))],
        compiler_params=pltpu.CompilerParams(vmem_limit_bytes=8 * MIB),
        name="pack_rows",
    )(*args)


def weight_forms(w1, w2, w3, w1t, w1b, w2t, w2b, w3b):
    zero = jnp.zeros((128, 128), BF16)
    for source, ahead, back in ((w1, w1t, w1b), (w2, w2t, w2b)):
        for u in range(3):
            for v in range(3):
                tap = source[pl.ds((3 * u + v) * 128, 128), :]
                for i in range(2):
                    side = slice(i * 128, (i + 1) * 128)
                    ahead[pl.ds((4 * u + v + i) * 128, 128), side] = tap
                    at = (4 * (2 - u) + 2 - v + i) * 128
                    back[side, at : at + 128] = tap
            for i, j in ((0, 3), (1, 0)):
                at = (4 * u + j) * 128
                side = slice(i * 128, (i + 1) * 128)
                ahead[pl.ds(at, 128), side] = zero
                back[side, at : at + 128] = zero
    for u in range(3):
        for v in range(3):
            at = (3 * (2 - u) + 2 - v) * 256
            w3b[:, at : at + 256] = w3[pl.ds((3 * u + v) * 128, 128), :]


def wave_tables(grid_rows, grid_cols, anchor, frequency, rows_sc, cols_sc):
    own_row, own_col = own_place()
    row = lax.broadcasted_iota(jnp.int32, (PAD_ROWS, 128), 0) - HALO + own_row * ROWS
    angle = (row + anchor[0]).astype(F32) * frequency[0:1, :]
    keep = jnp.where((row >= 0) & (row < grid_rows), 1.0, 0.0)
    rows_sc[0] = jnp.sin(angle) * keep
    rows_sc[1] = jnp.cos(angle) * keep
    for p in range(4):
        k = lax.broadcasted_iota(jnp.int32, (KP, 128), 0)
        col = 4 * jnp.where(k < KO + 4, k, k - KP) + p + own_col * (4 * KO)
        angle = (col + anchor[1]).astype(F32) * frequency[1:2, :]
        keep = jnp.where((col >= 0) & (col < grid_cols), 1.0, 0.0)
        cols_sc[0, p] = jnp.sin(angle) * keep
        cols_sc[1, p] = jnp.cos(angle) * keep


def prep_kernel(grid_rows, grid_cols, anchor, w1, w2, w3, frequency, w1t, w1b, w2t, w2b, w3b, rows_sc, cols_sc):
    weight_forms(w1, w2, w3, w1t, w1b, w2t, w2b, w3b)
    wave_tables(grid_rows, grid_cols, anchor, frequency, rows_sc, cols_sc)


def prep(grid_rows, grid_cols, anchor, w1, w2, w3, frequency):
    def kernel(*refs):
        prep_kernel(grid_rows, grid_cols, *refs)

    shape = jax.ShapeDtypeStruct
    return pl.pallas_call(
        kernel,
        out_shape=[
            shape((1536, 256), BF16),
            shape((256, 1536), BF16),
            shape((1536, 256), BF16),
            shape((256, 1536), BF16),
            shape((128, 2304), BF16),
            shape((2, PAD_ROWS, 128), F32),
            shape((2, 4, KP, 128), F32),
        ],
        in_specs=[smem_spec()] + [vmem_spec()] * 4,
        out_specs=[vmem_spec()] * 7,
        compiler_params=pltpu.CompilerParams(vmem_limit_bytes=12 * MIB),
        name="weight_forms",
    )(anchor, w1, w2, w3, frequency)


def fill_mask(low_rows, low_cols, mask):
    own_row, own_col = own_place()
    k = lax.broadcasted_iota(jnp.int32, (KP, 128), 0)
    col = jnp.where(k < KO + 4, k, k - KP) + own_col * KO
    inside = jnp.where((col >= 0) & (col < low_cols), 1.0, 0.0)

    def step(at, _):
        row = at - 4 + own_row * 12
        mask[at] = inside * jnp.where((row >= 0) & (row < low_rows), 1.0, 0.0)
        return 0

    lax.fori_loop(0, LOWS, step, 0)


def widened(line):
    rest = jnp.zeros((KW - KP, line.shape[1]), F32)
    return jnp.concatenate([line, rest], axis=0).astype(BF16)


def put_line(ref, row, planes):
    width = planes[0].shape[1]
    for n, plane in enumerate(planes):
        ref[row, :, n * width : (n + 1) * width] = widened(plane)


def before(line):
    return pltpu.roll(line, 1, 0)


def after(line):
    return pltpu.roll(line, KP - 1, 0)


def silu_parts(half):
    th = jnp.tanh(half)
    act = half + half * th
    return act, (1.0 + act) + th * (1.0 - act)


def rounded(value):
    return value.astype(BF16).astype(F32)


def flat(block):
    return block.reshape(128, 128)


def modulation(noise, noise_index):
    modulate = noise[pl.ds(noise_index[0], 1), :]
    return 1.0 + modulate[:, 0:128], modulate[:, 128:256]


def first_lines(load, base, at, tables, stage, x1):
    rows_sc, cols_sc = tables
    for i in range(4):
        own, right, left = load(i)
        stage[i, 0:128] = own.astype(F32)
        stage[i, 128:144] = right.astype(F32)
        stage[i, 144:160] = left.astype(F32)
        sin_row = rows_sc[0, pl.ds(base + i, 1), :]
        cos_row = rows_sc[1, pl.ds(base + i, 1), :]
        planes = []
        for p in range(4):
            value = stage[i, pl.ds(p, KP, stride=4), :]
            planes.append(value + (sin_row * cols_sc[1, p] + cos_row * cols_sc[0, p]))
        put_line(x1, at + i, [before(planes[3])] + planes + [after(planes[0])])


def around(ref, at, count, lanes, cols=KW):
    parts = [ref[pl.ds(at - 1 + u, count), 0:cols, lanes] for u in range(3)]
    return jnp.concatenate([part.reshape(count * cols, part.shape[-1]) for part in parts], axis=1)


def product(left, right):
    return jnp.dot(left, right, preferred_element_type=F32)


def product_turned(left, right):
    return lax.dot_general(left, right, (((1,), (1,)), ((), ())), preferred_element_type=F32)


def weight_terms(grad, field):
    return lax.dot_general(grad, field, (((0,), (0,)), ((), ())), preferred_element_type=F32)


def pipeline(steps, dot, post, z0, z1):
    def put(z, t):
        total = dot(t)
        z[0 : total.shape[0], :] = total

    put(z0, 0)

    def two(i, _):
        put(z1, 2 * i + 1)
        post(2 * i, z0)
        put(z0, 2 * i + 2)
        post(2 * i + 1, z1)
        return 0

    if steps > 2:
        lax.fori_loop(0, (steps - 1) // 2, two, 0)
    if steps % 2 == 0:
        put(z1, steps - 1)
        post(steps - 2, z0)
        post(steps - 1, z1)
    else:
        post(steps - 1, z0)


def conv_one_dot(x1, row, w1t):
    one = around(x1, row, 4, slice(0, 512))
    two = around(x1, row, 4, slice(256, 768))
    return product(jnp.concatenate([one, two], axis=0), w1t[...])


def conv_one_post(z, scale, shift, keeps, d1, d1_row, x2, x2_row):
    half_scale, half_shift = 0.5 * scale, 0.5 * shift
    slope_scale = half_scale.astype(BF16)
    for s in range(2):
        halves = []
        for q in range(2):
            sums = []
            for p in (2 * q, 2 * q + 1):
                lanes = slice((p % 2) * 128, (p % 2 + 1) * 128)
                acts = []
                for r in range(2):
                    at = q * 4 * KW + (2 * s + r) * KW
                    act, slope = silu_parts((z[at : at + KW, lanes] * half_scale + half_shift).astype(BF16))
                    d1[d1_row + 2 * s + r, :, p * 128 : (p + 1) * 128] = slope_scale * slope
                    acts.append(act)
                sums.append((acts[0] + acts[1]).astype(F32))
            halves.append((sums[0] + sums[1])[:KP] * (0.25 * keeps[s]))
        put_line(x2, x2_row + s, [before(halves[1]), halves[0], halves[1], after(halves[0])])


def own_kernel(
    grid_rows, grid_cols,
    noise_index, rows_sc, cols_sc, noise, inputs_in, one, two, w1t_in,
    x1_out, d1_out, x2_out,
    x1, stage, d1, x2, mask, side, inputs, w1t, z0, z1, sems,
):
    odd = odd_column()
    halos = [
        pltpu.make_async_copy(one, side.at[1 - odd], sems.at[0]),
        pltpu.make_async_copy(two, side.at[odd], sems.at[1]),
    ]
    early = pltpu.make_async_copy(inputs_in.at[pl.ds(0, 12)], inputs.at[pl.ds(0, 12)], sems.at[5])
    got_w1t = pltpu.make_async_copy(w1t_in, w1t, sems.at[6])
    late = pltpu.make_async_copy(inputs_in.at[pl.ds(12, 36)], inputs.at[pl.ds(12, 36)], sems.at[7])
    for copy in (*halos, early, got_w1t, late):
        copy.start()
    fill_mask(grid_rows // 4, grid_cols // 4, mask)
    scale, shift = modulation(noise, noise_index)
    for copy in (*halos, early):
        copy.wait()

    def first(q):
        def load(i):
            row = 4 * q + i
            return flat(inputs[row]), side[1, 1 + row], side[0, 1 + row]

        first_lines(load, HALO + 4 * q, 4 * q, (rows_sc, cols_sc), stage, x1)

    def dot(t):
        return conv_one_dot(x1, 4 * t + 2, w1t)

    def post(t, z):
        keeps = [mask[(9 + 2 * t) // 2], mask[(10 + 2 * t) // 2]]
        conv_one_post(z, scale, shift, keeps, d1, 4 * t, x2, 2 * t)

    first(0)
    first(1)
    got_w1t.wait()
    late.wait()
    z = (z0, z1)
    for t in range(11):
        z[t % 2][...] = dot(t)
        if t + 2 < 12:
            first(t + 2)
        if t > 0:
            post(t - 1, z[(t - 1) % 2])
        if t == 9:
            put_x1 = pltpu.make_async_copy(x1, x1_out, sems.at[2])
            put_x1.start()
    post(10, z0)
    put_d1 = pltpu.make_async_copy(d1, d1_out, sems.at[3])
    put_x2 = pltpu.make_async_copy(x2, x2_out, sems.at[4])
    put_d1.start()
    put_x2.start()
    put_x1.wait()
    put_d1.wait()
    put_x2.wait()


def own_rows(grid_rows, grid_cols, *args):
    def kernel(*refs):
        own_kernel(grid_rows, grid_cols, *refs)

    vm = pltpu.VMEM
    shape = jax.ShapeDtypeStruct
    return pl.pallas_call(
        kernel,
        out_shape=[shape((48, KW, 768), BF16), shape((44, KW, 512), BF16), shape((22, KW, 512), BF16)],
        in_specs=[smem_spec()] + [vmem_spec()] * 3 + [any_spec()] * 4,
        out_specs=[any_spec()] * 3,
        scratch_shapes=[
            vm((48, KW, 768), BF16),
            vm((4, 160, 128), F32),
            vm((44, KW, 512), BF16),
            vm((22, KW, 512), BF16),
            vm((LOWS, KP, 128), F32),
            vm((2, ROWS + 4, 16, 128), BF16),
            vm((ROWS, 8, 16, 128), BF16),
            vm((1536, 256), BF16),
            vm((8 * KW, 256), F32),
            vm((8 * KW, 256), F32),
            pltpu.SemaphoreType.DMA((8,)),
        ],
        compiler_params=pltpu.CompilerParams(vmem_limit_bytes=18 * MIB),
        cost_estimate=pl.CostEstimate(flops=4 * 10**9, bytes_accessed=30 * 10**6, transcendentals=0),
        name="own_rows",
    )(*args)


def lines_kernel(
    grid_rows, grid_cols,
    noise_index, rows_sc, cols_sc, noise,
    cot_in, w1t_in, off, near, one, two, w2t_in, w2b_in, w3_in, w3b_in, x1_in, d1_in, x2_in,
    coarse_out, g1_out, keep_out, give_out,
    rim, stage, x1, d1, x2, d2, x3, cp, side, side32, g3, xb2, g2, g1, coarse,
    acc, acc3, gw, msg, mask, z0, z1, cot, w1t, w2t, w2b, w3, w3b, sems,
):
    core = lax.axis_index("core")
    odd = odd_column()

    def fetch(source, target, at):
        copy = pltpu.make_async_copy(source, target, sems.at[at])
        copy.start()
        return copy

    got_rims = [fetch(off, rim.at[core], 0), fetch(near, rim.at[1 - core], 1)]
    got_edges = [
        fetch(x1_in.at[pl.ds(0, 4)], x1.at[pl.ds(16, 4)], 2),
        fetch(x1_in.at[pl.ds(44, 4)], x1.at[pl.ds(60, 4)], 3),
    ]
    got_w1t = fetch(w1t_in, w1t, 13)
    got_x2 = fetch(x2_in, x2.at[pl.ds(9, 22)], 4)
    units = pl.ds(ROWS + 1, 3)
    got_sides = [fetch(one.at[units], side.at[1 - odd], 5), fetch(two.at[units], side.at[odd], 6)]
    got_cot = fetch(cot_in, cot, 14)
    got_w2t = fetch(w2t_in, w2t, 7)
    got_w3 = [fetch(w3_in, w3, 8), fetch(w3b_in, w3b, 9)]
    got_w2b = fetch(w2b_in, w2b, 10)
    got_d1 = fetch(d1_in, d1.at[pl.ds(18, 44)], 11)
    got_x1 = fetch(x1_in.at[pl.ds(4, 40)], x1.at[pl.ds(20, 40)], 12)
    fill_mask(grid_rows // 4, grid_cols // 4, mask)
    gw[:, 0:8, :] = jnp.zeros((4, 8, 128), F32)
    gw[:, 1160:1168, :] = jnp.zeros((4, 8, 128), F32)
    scale, shift = modulation(noise, noise_index)
    for copy in got_rims:
        copy.wait()

    def first(n):
        below, start = n // 4, 4 * (n % 4)
        base = start + (HALO + ROWS) * below

        def load(i):
            row = start + i
            return flat(rim[below, row, 0:8]), rim[below, row, 8 + odd], rim[below, row, 9 - odd]

        first_lines(load, base, base, (rows_sc, cols_sc), stage, x1)

    def mid_of(t):
        return 1 + 2 * t if t < 4 else 23 + 2 * t

    def dot(t):
        return conv_one_dot(x1, 2 * mid_of(t), w1t)

    def post(t, z):
        m = mid_of(t)
        conv_one_post(z, scale, shift, [mask[m // 2], mask[(m + 1) // 2]], d1, 2 * m, x2, m)

    first(0)
    first(1)
    for copy in (*got_edges, got_w1t):
        copy.wait()
    z = (z0, z1)
    for t in range(8):
        z[t % 2][...] = dot(t)
        if t + 2 < 8:
            first(t + 2)
        if t > 0:
            post(t - 1, z[(t - 1) % 2])
    post(7, z1)
    got_x2.wait()
    got_w2t.wait()

    def conv_two_post(t, z):
        for s in range(3):
            low = 1 + 3 * t + s
            total = None
            for q in range(2):
                lanes = slice(q * 128, (q + 1) * 128)
                for r in range(2):
                    row, at = 2 * low + r, (2 * s + r) * KW
                    act, slope = silu_parts(0.5 * z[at : at + KP, lanes])
                    d2[row, :, lanes] = 0.5 * slope
                    down = x2[row, :, (q + 1) * 128 : (q + 2) * 128].astype(F32)[:KP]
                    act = rounded(down + act)
                    total = act if total is None else total + act
            line = total * (0.25 * mask[low])
            put_line(x3, low, [before(line), line, after(line)])

    pipeline(6, lambda t: product(around(x2, 2 + 6 * t, 6, slice(0, 512)), w2t[...]), conv_two_post, z0, z1)

    cp[...] = jnp.zeros_like(cp)
    for copy in (*got_sides, got_cot):
        copy.wait()
    for h in range(2):
        lanes = slice(h * 128, (h + 1) * 128)
        for r in range(2):
            units = pl.ds((r * 2 + h) * 2, 2)
            cp[r, 0:KO, lanes] = rim[0, HALO, units].reshape(KO, 128).astype(F32)
            cp[14 + r, 0:KO, lanes] = rim[1, HALO, units].reshape(KO, 128).astype(F32)
    for r in range(12):
        cp[2 + r, 0:KO, :] = cot[r].astype(F32)
    for which, at in ((1, KO), (0, KP - 2)):
        side32[...] = side[which].reshape(48, 128).astype(F32)
        for h in range(2):
            for r in range(12):
                cp[2 + r, at : at + 2, h * 128 : (h + 1) * 128] = side32[r * 4 + h * 2 : r * 4 + h * 2 + 2]
    for below, skip, row in ((0, 8, 0), (1, 0, 14)):
        for unit, at in ((9 - odd, KP - 2), (8 + odd, KO)):
            side32[0:16] = rim[below, HALO, unit].astype(F32)
            for h in range(2):
                for r in range(2):
                    start = skip + r * 4 + h * 2
                    cp[row + r, at : at + 2, h * 128 : (h + 1) * 128] = side32[start : start + 2]
    for copy in got_w3:
        copy.wait()
    g3[1] = jnp.zeros((KW, 768), BF16)
    g3[18] = jnp.zeros((KW, 768), BF16)

    def conv_three_post(t, z):
        for i in range(4):
            row = 2 + 4 * t + i
            act, slope = silu_parts(0.5 * z[i * KW : i * KW + KP, :])
            keep = 0.5 * mask[row]
            line = cp[row - 2] * slope * jnp.concatenate([keep, keep], axis=1)
            put_line(g3, row, [before(line), line, after(line)])
            coarse[row - 2] = act[:KO].astype(BF16)

    pipeline(4, lambda t: product(around(x3, 2 + 4 * t, 4, slice(0, 384)), w3[...]), conv_three_post, z0, z1)
    put_coarse = fetch(coarse.at[pl.ds(2, 12)], coarse_out, 0)

    def back_three_post(t, z):
        for i in range(4):
            low = 2 + 4 * t + i
            line = 0.25 * z[i * KW : i * KW + KP, 0:128]
            xb2[low] = line
            line = line * mask[low]
            for r in range(2):
                row = 2 * low + r
                zero, one = (line * d2[row, :, q * 128 : (q + 1) * 128] for q in range(2))
                put_line(g2, row, [before(one), zero, one, after(zero)])

    def back_three_dot(t):
        total = product_turned(around(g3, 2 + 4 * t, 4, slice(0, 768)), w3b[...])
        return jnp.concatenate([total, total], axis=1)

    pipeline(4, back_three_dot, back_three_post, z0, z1)
    acc3[...] = weight_terms(
        g3[4:16, 0:KO, 256:512].reshape(12 * KO, 256), around(x3, 4, 12, slice(0, 384), KO)
    )
    acc[...] = weight_terms(
        g2[8:32, 0:KO, 128:384].reshape(24 * KO, 256), around(x2, 8, 24, slice(0, 512), KO)
    )
    got_w2b.wait()
    got_d1.wait()

    def back_two_post(t, z):
        for i in range(4):
            m = 6 + 4 * t + i
            low = m // 2
            keep = 0.25 * mask[low]
            base = xb2[low]
            both = [(base + z[i * KW : i * KW + KP, q * 128 : (q + 1) * 128]) * keep for q in range(2)]
            for r in range(2):
                row = 2 * m + r
                slopes = [d1[row, :, p * 128 : (p + 1) * 128].astype(F32)[:KP] for p in range(4)]
                planes = [both[p // 2] * slopes[p] for p in range(4)]
                for n, line in enumerate([before(planes[3])] + planes + [after(planes[0])]):
                    g1[row - 12, :, n * 128 : (n + 1) * 128] = line[:KO].astype(BF16)

    pipeline(
        7, lambda t: product_turned(around(g2, 6 + 4 * t, 4, slice(0, 512)), w2b[...]), back_two_post, z0, z1
    )
    put_g1 = fetch(g1.at[pl.ds(3, 50)], g1_out, 1)
    got_x1.wait()

    def fold_weights(at):
        for u in range(3):
            for v in range(3):
                left = (4 * u + v) * 128
                term = acc[0:128, left : left + 128] + acc[128:256, left + 128 : left + 256]
                gw[at, pl.ds(8 + (3 * u + v) * 128, 128), :] = term.T

    def one_chunk(t):
        grads = jnp.concatenate(
            [g1[4 + 16 * t : 20 + 16 * t, :, lanes].reshape(512, 256) for lanes in (slice(128, 384), slice(384, 640))],
            axis=0,
        )
        fields = jnp.concatenate(
            [around(x1, 16 + 16 * t, 16, lanes, KO) for lanes in (slice(0, 512), slice(256, 768))], axis=0
        )
        return weight_terms(grads, fields)

    fold_weights(1)
    acc[...] = one_chunk(0)
    for tap in range(9):
        turned = acc3[:, tap * 128 : (tap + 1) * 128].T
        gw[2, pl.ds(8 + tap * 128, 128), :] = turned[:, 0:128]
        gw[3, pl.ds(8 + tap * 128, 128), :] = turned[:, 128:256]
    acc[...] += one_chunk(1)
    acc[...] += one_chunk(2)
    fold_weights(0)
    line = lax.broadcasted_iota(jnp.int32, (8, 128), 0)
    none = jnp.zeros((8, 128), F32)
    for owner in range(128):
        at = 8 + 9 * owner
        parts = [gw[0, at : at + 8, :]]
        for t in range(1, 5):
            rest = gw[t - 1, at + 9 - t : at + 17 - t, :]
            start = gw[t, at - t : at + 8 - t, :] if t < 4 else none
            parts.append(jnp.where(line < t, rest, start))
        row, col = divmod(owner, 8)
        msg[row % 2, (row // 2) * 8 + col] = jnp.concatenate(parts, axis=0).astype(BF16)
    put_keep = fetch(msg.at[core], keep_out, 2)
    put_give = fetch(msg.at[1 - core], give_out, 3)
    put_keep.wait()
    put_give.wait()
    put_coarse.wait()
    put_g1.wait()


def levels(grid_rows, grid_cols, *args):
    def kernel(*refs):
        lines_kernel(grid_rows, grid_cols, *refs)

    vm = pltpu.VMEM
    return pl.pallas_call(
        kernel,
        out_shape=[
            jax.ShapeDtypeStruct((12, KO, 256), BF16),
            jax.ShapeDtypeStruct((50, KO, 768), BF16),
            jax.ShapeDtypeStruct((64, 40, 128), BF16),
            jax.ShapeDtypeStruct((64, 40, 128), BF16),
        ],
        in_specs=[smem_spec()] + [vmem_spec()] * 3 + [any_spec()] * 13,
        out_specs=[any_spec()] * 4,
        scratch_shapes=[
            vm((2, HALO + 1, 10, 16, 128), BF16),
            vm((4, 160, 128), F32),
            vm((PAD_ROWS, KW, 768), BF16),
            vm((PAD_ROWS, KW, 512), BF16),
            vm((PAIRS, KW, 512), BF16),
            vm((PAIRS, KP, 256), F32),
            vm((LOWS, KW, 384), BF16),
            vm((16, KP, 256), F32),
            vm((2, 3, 16, 128), BF16),
            vm((48, 128), F32),
            vm((LOWS, KW, 768), BF16),
            vm((LOWS, KP, 128), F32),
            vm((PAIRS, KW, 512), BF16),
            vm((56, KO, 768), BF16),
            vm((16, KO, 256), BF16),
            vm((256, 1536), F32),
            vm((256, 1152), F32),
            vm((4, 1168, 128), F32),
            vm((2, 64, 40, 128), BF16),
            vm((LOWS, KP, 128), F32),
            vm((8 * KW, 256), F32),
            vm((8 * KW, 256), F32),
            vm((12, KO, 256), BF16),
            vm((1536, 256), BF16),
            vm((1536, 256), BF16),
            vm((256, 1536), BF16),
            vm((1152, 256), BF16),
            vm((128, 2304), BF16),
            pltpu.SemaphoreType.DMA((15,)),
        ],
        compiler_params=pltpu.CompilerParams(vmem_limit_bytes=46 * MIB),
        name="encoder_levels",
    )(*args)


def input_kernel(g1, g1_next, w1b, out, stage):
    for t in range(2):
        halves = []
        for lanes in (slice(0, 512), slice(256, 768)):
            rows = jnp.concatenate([g1[:, :, lanes], g1_next[:, :, lanes]], axis=0)
            parts = [rows[4 * t + u : 4 * t + u + 4].reshape(128, 512) for u in range(3)]
            halves.append(jnp.concatenate(parts, axis=1))
        total = product_turned(jnp.concatenate(halves, axis=0), w1b[...])
        for r in range(4):
            for p in range(4):
                rows = (p // 2) * 128 + r * 32
                value = total[rows : rows + 32, (p % 2) * 128 : (p % 2 + 1) * 128]
                stage[4 * t + r, pl.ds(p, 32, stride=4), :] = value
            out[4 * t + r] = stage[4 * t + r].astype(BF16)


def input_grad(g1, w1b):
    return pl.pallas_call(
        input_kernel,
        grid=(6,),
        out_shape=jax.ShapeDtypeStruct((ROWS, 128, 128), BF16),
        in_specs=[
            pl.BlockSpec((8, KO, 768), lambda i: (i, 0, 0)),
            pl.BlockSpec((2, KO, 768), lambda i: (4 * i + 4, 0, 0)),
            pl.BlockSpec((256, 1536), lambda i: (0, 0)),
        ],
        out_specs=pl.BlockSpec((8, 128, 128), lambda i: (i, 0, 0)),
        scratch_shapes=[pltpu.VMEM((8, 128, 128), F32)],
        compiler_params=pltpu.CompilerParams(vmem_limit_bytes=16 * MIB),
        cost_estimate=pl.CostEstimate(flops=2 * 6144 * 1152 * 128, bytes_accessed=8 * 1024 * 1024, transcendentals=0),
        name="input_grad",
    )(g1, g1, w1b)


def collect(got):
    sums = got.astype(F32).sum(axis=0)
    return sums[0:9], sums[9:18], jnp.concatenate([sums[18:27], sums[27:36]], axis=1)


def swapped(block, axis, odd_first):
    devices = lax.axis_size(axis)
    pairs = []
    for i in range(1 if odd_first else 0, devices - 1, 2):
        pairs += [(i, i + 1), (i + 1, i)]
    return lax.ppermute(block, axis, pairs)


def body(inputs, weight_one, weight_two, weight_three, noise_table, frequency, anchor, noise_index, cotangent):
    grid = (lax.axis_size(ROW_AXES) * ROWS, lax.axis_size("tx") * 4 * KO)
    inputs = inputs.reshape(ROWS, 8, 16, 128)
    one, two, cots = sides(inputs, cotangent)
    two = swapped(two, "tx", True)
    one = swapped(one, "tx", False)
    w1t, w1b, w2t, w2b, w3b, rows_sc, cols_sc = prep(*grid, anchor, weight_one, weight_two, weight_three, frequency)
    off, near = rims(inputs, cots, one, two, rows_sc)
    off = swapped(off, ROW_AXES, True)
    near = lax.ppermute(near, "core", [(0, 1), (1, 0)])
    x1, d1, x2 = own_rows(*grid, noise_index, rows_sc, cols_sc, noise_table, inputs, one, two, w1t)
    coarse, g1, keep_msg, give_msg = levels(
        *grid, noise_index, rows_sc, cols_sc, noise_table, cotangent, w1t,
        off, near, one, two, w2t, w2b, weight_three, w3b, x1, d1, x2,
    )
    other = lax.ppermute(give_msg, "core", [(0, 1), (1, 0)])
    msg = (keep_msg.astype(F32) + other.astype(F32)).astype(BF16)
    got = lax.all_to_all(msg, ("chip", "tx"), 0, 0, tiled=True)
    grad_inputs = input_grad(g1, w1b)
    return (coarse, grad_inputs, *collect(got))


def solution(mesh):
    halves = jax.sharding.Mesh(mesh.devices.reshape(-1, 2, mesh.devices.shape[1]), ("chip", "core", "tx"))
    placed = (P(ROW_AXES, "tx", None), P(), P(), P(), P(), P(), P(), P(), P(ROW_AXES, "tx", None))
    return jax.shard_map(
        body,
        mesh=halves,
        in_specs=placed,
        out_specs=(
            P(ROW_AXES, "tx", None),
            P(ROW_AXES, "tx", None),
            P((*ROW_AXES, "tx"), None),
            P((*ROW_AXES, "tx"), None),
            P((*ROW_AXES, "tx"), None),
        ),
        check_vma=False,
    )
```

```python
import jax
import jax.numpy as jnp
from jax import lax
from jax.experimental import pallas as pl
from jax.experimental.pallas import tpu as pltpu
from jax.sharding import PartitionSpec as P

BF16 = jnp.bfloat16
F32 = jnp.float32

KO = 32
KP = 40
KW = 48
HALO = 16
ROWS = 48
PAD_ROWS = ROWS + 2 * HALO
PAIRS = PAD_ROWS // 2
LOWS = PAIRS // 2
MIB = 1024 * 1024


def any_spec():
    return pl.BlockSpec(memory_space=pl.ANY)


def vmem_spec():
    return pl.BlockSpec(memory_space=pltpu.VMEM)


def smem_spec():
    return pl.BlockSpec(memory_space=pltpu.SMEM)


ROW_AXES = ("chip", "core")


def own_place():
    return lax.axis_index(ROW_AXES), lax.axis_index("tx")


def odd_column():
    return lax.rem(lax.axis_index("tx"), 2)


def side_kernel(inputs, cot, one, two, cots, side32, sems):
    odd = odd_column()
    copies = [
        pltpu.make_async_copy(inputs.at[:, 7 - 7 * odd], one.at[pl.ds(1, ROWS)], sems.at[0]),
        pltpu.make_async_copy(inputs.at[:, 7 * odd], two.at[pl.ds(1, ROWS)], sems.at[1]),
    ]
    for copy in copies:
        copy.start()
    for target, at_left in ((one, odd == 1), (two, odd == 0)):
        for r in range(12):
            line = cot[r].astype(F32)
            for h in range(2):
                lanes = slice(h * 128, (h + 1) * 128)
                side32[pl.ds(r * 4 + h * 2, 2)] = jnp.where(at_left, line[0:2, lanes], line[30:32, lanes])
        side = side32[...].astype(BF16).reshape(3, 16, 128)
        target[pl.ds(0, 1)] = side[0:1]
        target[pl.ds(1 + ROWS, 3)] = side
    for at, start in ((0, 10), (1, 0)):
        for r in range(2):
            for h in range(2):
                cots[at, pl.ds((r * 2 + h) * 2, 2)] = cot[start + r, :, h * 128 : (h + 1) * 128].reshape(2, 16, 128)
    for copy in copies:
        copy.wait()


def sides(inputs, cot):
    return pl.pallas_call(
        side_kernel,
        out_shape=[jax.ShapeDtypeStruct((ROWS + 4, 16, 128), BF16)] * 2 + [jax.ShapeDtypeStruct((2, 8, 16, 128), BF16)],
        in_specs=[any_spec(), vmem_spec()],
        out_specs=[vmem_spec()] * 3,
        scratch_shapes=[pltpu.VMEM((48, 128), F32), pltpu.SemaphoreType.DMA((2,))],
        compiler_params=pltpu.CompilerParams(vmem_limit_bytes=8 * MIB),
        name="pack_columns",
    )(inputs, cot)


def rim_kernel(inputs, cots, one, two, _, off, near, sems):
    core = lax.axis_index("core")
    copies = []

    def fetch(source, target):
        copy = pltpu.make_async_copy(source, target, sems.at[len(copies)])
        copy.start()
        copies.append(copy)

    body = pl.ds(0, HALO)
    for target, low in ((off, core), (near, 1 - core)):
        row = (ROWS - HALO) * low
        fetch(inputs.at[pl.ds(row, HALO)], target.at[body, pl.ds(0, 8)])
        fetch(cots.at[1 - low], target.at[HALO, pl.ds(0, 8)])
        for unit, side in ((8, one), (9, two)):
            fetch(side.at[pl.ds(1 + row, HALO)], target.at[body, unit])
            fetch(side.at[(3 + ROWS) * low], target.at[HALO, unit])
    for copy in copies:
        copy.wait()


def rims(*args):
    return pl.pallas_call(
        rim_kernel,
        out_shape=[jax.ShapeDtypeStruct((HALO + 1, 10, 16, 128), BF16)] * 2,
        in_specs=[any_spec()] * len(args),
        out_specs=[vmem_spec()] * 2,
        scratch_shapes=[pltpu.SemaphoreType.DMA((12,))],
        compiler_params=pltpu.CompilerParams(vmem_limit_bytes=8 * MIB),
        name="pack_rows",
    )(*args)


def weight_forms(w1, w2, w3, w1t, w1b, w2t, w2b, w3b):
    zero = jnp.zeros((128, 128), BF16)
    for source, ahead, back in ((w1, w1t, w1b), (w2, w2t, w2b)):
        for u in range(3):
            for v in range(3):
                tap = source[pl.ds((3 * u + v) * 128, 128), :]
                for i in range(2):
                    side = slice(i * 128, (i + 1) * 128)
                    ahead[pl.ds((4 * u + v + i) * 128, 128), side] = tap
                    at = (4 * (2 - u) + 2 - v + i) * 128
                    back[side, at : at + 128] = tap
            for i, j in ((0, 3), (1, 0)):
                at = (4 * u + j) * 128
                side = slice(i * 128, (i + 1) * 128)
                ahead[pl.ds(at, 128), side] = zero
                back[side, at : at + 128] = zero
    for u in range(3):
        for v in range(3):
            at = (3 * (2 - u) + 2 - v) * 256
            w3b[:, at : at + 256] = w3[pl.ds((3 * u + v) * 128, 128), :]


def wave_tables(grid_rows, grid_cols, anchor, frequency, rows_sc, cols_sc):
    own_row, own_col = own_place()
    row = lax.broadcasted_iota(jnp.int32, (PAD_ROWS, 128), 0) - HALO + own_row * ROWS
    angle = (row + anchor[0]).astype(F32) * frequency[0:1, :]
    keep = jnp.where((row >= 0) & (row < grid_rows), 1.0, 0.0)
    rows_sc[0] = jnp.sin(angle) * keep
    rows_sc[1] = jnp.cos(angle) * keep
    for p in range(4):
        k = lax.broadcasted_iota(jnp.int32, (KP, 128), 0)
        col = 4 * jnp.where(k < KO + 4, k, k - KP) + p + own_col * (4 * KO)
        angle = (col + anchor[1]).astype(F32) * frequency[1:2, :]
        keep = jnp.where((col >= 0) & (col < grid_cols), 1.0, 0.0)
        cols_sc[0, p] = jnp.sin(angle) * keep
        cols_sc[1, p] = jnp.cos(angle) * keep


def prep_kernel(grid_rows, grid_cols, anchor, w1, w2, w3, frequency, w1t, w1b, w2t, w2b, w3b, rows_sc, cols_sc):
    weight_forms(w1, w2, w3, w1t, w1b, w2t, w2b, w3b)
    wave_tables(grid_rows, grid_cols, anchor, frequency, rows_sc, cols_sc)


def prep(grid_rows, grid_cols, anchor, w1, w2, w3, frequency):
    def kernel(*refs):
        prep_kernel(grid_rows, grid_cols, *refs)

    shape = jax.ShapeDtypeStruct
    return pl.pallas_call(
        kernel,
        out_shape=[
            shape((1536, 256), BF16),
            shape((256, 1536), BF16),
            shape((1536, 256), BF16),
            shape((256, 1536), BF16),
            shape((128, 2304), BF16),
            shape((2, PAD_ROWS, 128), F32),
            shape((2, 4, KP, 128), F32),
        ],
        in_specs=[smem_spec()] + [vmem_spec()] * 4,
        out_specs=[vmem_spec()] * 7,
        compiler_params=pltpu.CompilerParams(vmem_limit_bytes=12 * MIB),
        name="weight_forms",
    )(anchor, w1, w2, w3, frequency)


def fill_mask(low_rows, low_cols, mask):
    own_row, own_col = own_place()
    k = lax.broadcasted_iota(jnp.int32, (KP, 128), 0)
    col = jnp.where(k < KO + 4, k, k - KP) + own_col * KO
    inside = jnp.where((col >= 0) & (col < low_cols), 1.0, 0.0)

    def step(at, _):
        row = at - 4 + own_row * 12
        mask[at] = inside * jnp.where((row >= 0) & (row < low_rows), 1.0, 0.0)
        return 0

    lax.fori_loop(0, LOWS, step, 0)


def widened(line):
    rest = jnp.zeros((KW - KP, line.shape[1]), F32)
    return jnp.concatenate([line, rest], axis=0).astype(BF16)


def put_line(ref, row, planes):
    width = planes[0].shape[1]
    for n, plane in enumerate(planes):
        ref[row, :, n * width : (n + 1) * width] = widened(plane)


def before(line):
    return pltpu.roll(line, 1, 0)


def after(line):
    return pltpu.roll(line, KP - 1, 0)


def silu_parts(half):
    th = jnp.tanh(half)
    act = half + half * th
    return act, (1.0 + act) + th * (1.0 - act)


def rounded(value):
    return value.astype(BF16).astype(F32)


def flat(block):
    return block.reshape(128, 128)


def modulation(noise, noise_index):
    modulate = noise[pl.ds(noise_index[0], 1), :]
    return 1.0 + modulate[:, 0:128], modulate[:, 128:256]


def first_lines(load, base, at, tables, stage, x1):
    rows_sc, cols_sc = tables
    for i in range(4):
        own, right, left = load(i)
        stage[i, 0:128] = own.astype(F32)
        stage[i, 128:144] = right.astype(F32)
        stage[i, 144:160] = left.astype(F32)
        sin_row = rows_sc[0, pl.ds(base + i, 1), :]
        cos_row = rows_sc[1, pl.ds(base + i, 1), :]
        planes = []
        for p in range(4):
            value = stage[i, pl.ds(p, KP, stride=4), :]
            planes.append(value + (sin_row * cols_sc[1, p] + cos_row * cols_sc[0, p]))
        put_line(x1, at + i, [before(planes[3])] + planes + [after(planes[0])])


def around(ref, at, count, lanes, cols=KW):
    parts = [ref[pl.ds(at - 1 + u, count), 0:cols, lanes] for u in range(3)]
    return jnp.concatenate([part.reshape(count * cols, part.shape[-1]) for part in parts], axis=1)


def product(left, right):
    return jnp.dot(left, right, preferred_element_type=F32)


def product_turned(left, right):
    return lax.dot_general(left, right, (((1,), (1,)), ((), ())), preferred_element_type=F32)


def weight_terms(grad, field):
    return lax.dot_general(grad, field, (((0,), (0,)), ((), ())), preferred_element_type=F32)


def pipeline(steps, dot, post, z0, z1):
    z = (z0, z1)
    for t in range(steps + 1):
        if t < steps:
            total = dot(t)
            z[t % 2][0 : total.shape[0], 0 : total.shape[1]] = total
        if t > 0:
            post(t - 1, z[(t - 1) % 2])


def conv_one_dot(x1, row, w1t):
    one = around(x1, row, 4, slice(0, 512))
    two = around(x1, row, 4, slice(256, 768))
    return product(jnp.concatenate([one, two], axis=0), w1t[...])


def conv_one_post(z, scale, shift, keeps, d1, d1_row, x2, x2_row):
    half_scale, half_shift = 0.5 * scale, 0.5 * shift
    slope_scale = half_scale.astype(BF16)
    for s in range(2):
        halves = []
        for q in range(2):
            sums = []
            for p in (2 * q, 2 * q + 1):
                lanes = slice((p % 2) * 128, (p % 2 + 1) * 128)
                acts = []
                for r in range(2):
                    at = q * 4 * KW + (2 * s + r) * KW
                    act, slope = silu_parts((z[at : at + KW, lanes] * half_scale + half_shift).astype(BF16))
                    d1[d1_row + 2 * s + r, :, p * 128 : (p + 1) * 128] = slope_scale * slope
                    acts.append(act)
                sums.append((acts[0] + acts[1]).astype(F32))
            halves.append((sums[0] + sums[1])[:KP] * (0.25 * keeps[s]))
        put_line(x2, x2_row + s, [before(halves[1]), halves[0], halves[1], after(halves[0])])


def own_kernel(
    grid_rows, grid_cols,
    noise_index, rows_sc, cols_sc, noise, inputs_in, one, two, w1t_in,
    x1_out, d1_out, x2_out,
    x1, stage, d1, x2, mask, side, inputs, w1t, z0, z1, sems,
):
    odd = odd_column()
    halos = [
        pltpu.make_async_copy(one, side.at[1 - odd], sems.at[0]),
        pltpu.make_async_copy(two, side.at[odd], sems.at[1]),
    ]
    early = pltpu.make_async_copy(inputs_in.at[pl.ds(0, 12)], inputs.at[pl.ds(0, 12)], sems.at[5])
    got_w1t = pltpu.make_async_copy(w1t_in, w1t, sems.at[6])
    late = pltpu.make_async_copy(inputs_in.at[pl.ds(12, 36)], inputs.at[pl.ds(12, 36)], sems.at[7])
    for copy in (*halos, early, got_w1t, late):
        copy.start()
    fill_mask(grid_rows // 4, grid_cols // 4, mask)
    scale, shift = modulation(noise, noise_index)
    for copy in (*halos, early):
        copy.wait()

    def first(q):
        def load(i):
            row = 4 * q + i
            return flat(inputs[row]), side[1, 1 + row], side[0, 1 + row]

        first_lines(load, HALO + 4 * q, 4 * q, (rows_sc, cols_sc), stage, x1)

    def dot(t):
        return conv_one_dot(x1, 4 * t + 2, w1t)

    def post(t, z):
        keeps = [mask[(9 + 2 * t) // 2], mask[(10 + 2 * t) // 2]]
        conv_one_post(z, scale, shift, keeps, d1, 4 * t, x2, 2 * t)

    first(0)
    first(1)
    got_w1t.wait()
    late.wait()
    z = (z0, z1)
    for t in range(11):
        z[t % 2][...] = dot(t)
        if t + 2 < 12:
            first(t + 2)
        if t > 0:
            post(t - 1, z[(t - 1) % 2])
        if t == 9:
            put_x1 = pltpu.make_async_copy(x1, x1_out, sems.at[2])
            put_x1.start()
    post(10, z0)
    put_d1 = pltpu.make_async_copy(d1, d1_out, sems.at[3])
    put_x2 = pltpu.make_async_copy(x2, x2_out, sems.at[4])
    put_d1.start()
    put_x2.start()
    put_x1.wait()
    put_d1.wait()
    put_x2.wait()


def own_rows(grid_rows, grid_cols, *args):
    def kernel(*refs):
        own_kernel(grid_rows, grid_cols, *refs)

    vm = pltpu.VMEM
    shape = jax.ShapeDtypeStruct
    return pl.pallas_call(
        kernel,
        out_shape=[shape((48, KW, 768), BF16), shape((44, KW, 512), BF16), shape((22, KW, 512), BF16)],
        in_specs=[smem_spec()] + [vmem_spec()] * 3 + [any_spec()] * 4,
        out_specs=[any_spec()] * 3,
        scratch_shapes=[
            vm((48, KW, 768), BF16),
            vm((4, 160, 128), F32),
            vm((44, KW, 512), BF16),
            vm((22, KW, 512), BF16),
            vm((LOWS, KP, 128), F32),
            vm((2, ROWS + 4, 16, 128), BF16),
            vm((ROWS, 8, 16, 128), BF16),
            vm((1536, 256), BF16),
            vm((8 * KW, 256), F32),
            vm((8 * KW, 256), F32),
            pltpu.SemaphoreType.DMA((8,)),
        ],
        compiler_params=pltpu.CompilerParams(vmem_limit_bytes=18 * MIB),
        cost_estimate=pl.CostEstimate(flops=4 * 10**9, bytes_accessed=30 * 10**6, transcendentals=0),
        name="own_rows",
    )(*args)


def lines_kernel(
    grid_rows, grid_cols,
    noise_index, rows_sc, cols_sc, noise,
    cot_in, w1t_in, off, near, one, two, w2t_in, w2b_in, w3_in, w3b_in, x1_in, d1_in, x2_in,
    coarse_out, g1_out, keep_out, give_out,
    rim, stage, x1, d1, x2, d2, x3, cp, side, side32, g3, xb2, g2, g1, coarse,
    acc, acc3, gw, msg, mask, z0, z1, cot, w1t, w2t, w2b, w3, w3b, sems,
):
    core = lax.axis_index("core")
    odd = odd_column()

    def fetch(source, target, at):
        copy = pltpu.make_async_copy(source, target, sems.at[at])
        copy.start()
        return copy

    got_rims = [fetch(off, rim.at[core], 0), fetch(near, rim.at[1 - core], 1)]
    got_edges = [
        fetch(x1_in.at[pl.ds(0, 4)], x1.at[pl.ds(16, 4)], 2),
        fetch(x1_in.at[pl.ds(44, 4)], x1.at[pl.ds(60, 4)], 3),
    ]
    got_w1t = fetch(w1t_in, w1t, 13)
    got_x2 = fetch(x2_in, x2.at[pl.ds(9, 22)], 4)
    units = pl.ds(ROWS + 1, 3)
    got_sides = [fetch(one.at[units], side.at[1 - odd], 5), fetch(two.at[units], side.at[odd], 6)]
    got_cot = fetch(cot_in, cot, 14)
    got_w2t = fetch(w2t_in, w2t, 7)
    got_w3 = [fetch(w3_in, w3, 8), fetch(w3b_in, w3b, 9)]
    got_w2b = fetch(w2b_in, w2b, 10)
    got_d1 = fetch(d1_in, d1.at[pl.ds(18, 44)], 11)
    got_x1 = fetch(x1_in.at[pl.ds(4, 40)], x1.at[pl.ds(20, 40)], 12)
    fill_mask(grid_rows // 4, grid_cols // 4, mask)
    gw[:, 0:8, :] = jnp.zeros((4, 8, 128), F32)
    gw[:, 1160:1168, :] = jnp.zeros((4, 8, 128), F32)
    scale, shift = modulation(noise, noise_index)
    for copy in got_rims:
        copy.wait()

    def first(n):
        below, start = n // 4, 4 * (n % 4)
        base = start + (HALO + ROWS) * below

        def load(i):
            row = start + i
            return flat(rim[below, row, 0:8]), rim[below, row, 8 + odd], rim[below, row, 9 - odd]

        first_lines(load, base, base, (rows_sc, cols_sc), stage, x1)

    def mid_of(t):
        return 1 + 2 * t if t < 4 else 23 + 2 * t

    def dot(t):
        return conv_one_dot(x1, 2 * mid_of(t), w1t)

    def post(t, z):
        m = mid_of(t)
        conv_one_post(z, scale, shift, [mask[m // 2], mask[(m + 1) // 2]], d1, 2 * m, x2, m)

    first(0)
    first(1)
    for copy in (*got_edges, got_w1t):
        copy.wait()
    z = (z0, z1)
    for t in range(8):
        z[t % 2][0 : 8 * KW, :] = dot(t)
        if t + 2 < 8:
            first(t + 2)
        if t > 0:
            post(t - 1, z[(t - 1) % 2])
    post(7, z1)
    got_x2.wait()
    got_w2t.wait()

    def conv_two_post(t, z):
        for s in range(6):
            low = 1 + 6 * t + s
            total = None
            for q in range(2):
                lanes = slice(q * 128, (q + 1) * 128)
                for r in range(2):
                    row, at = 2 * low + r, (2 * s + r) * KW
                    act, slope = silu_parts(0.5 * z[at : at + KP, lanes])
                    d2[row, :, lanes] = 0.5 * slope
                    down = x2[row, :, (q + 1) * 128 : (q + 2) * 128].astype(F32)[:KP]
                    act = rounded(down + act)
                    total = act if total is None else total + act
            line = total * (0.25 * mask[low])
            put_line(x3, low, [before(line), line, after(line)])

    pipeline(3, lambda t: product(around(x2, 2 + 12 * t, 12, slice(0, 512)), w2t[...]), conv_two_post, z0, z1)

    cp[...] = jnp.zeros_like(cp)
    for copy in (*got_sides, got_cot):
        copy.wait()
    for h in range(2):
        lanes = slice(h * 128, (h + 1) * 128)
        for r in range(2):
            units = pl.ds((r * 2 + h) * 2, 2)
            cp[r, 0:KO, lanes] = rim[0, HALO, units].reshape(KO, 128).astype(F32)
            cp[14 + r, 0:KO, lanes] = rim[1, HALO, units].reshape(KO, 128).astype(F32)
    for r in range(12):
        cp[2 + r, 0:KO, :] = cot[r].astype(F32)
    for which, at in ((1, KO), (0, KP - 2)):
        side32[...] = side[which].reshape(48, 128).astype(F32)
        for h in range(2):
            for r in range(12):
                cp[2 + r, at : at + 2, h * 128 : (h + 1) * 128] = side32[r * 4 + h * 2 : r * 4 + h * 2 + 2]
    for below, skip, row in ((0, 8, 0), (1, 0, 14)):
        for unit, at in ((9 - odd, KP - 2), (8 + odd, KO)):
            side32[0:16] = rim[below, HALO, unit].astype(F32)
            for h in range(2):
                for r in range(2):
                    start = skip + r * 4 + h * 2
                    cp[row + r, at : at + 2, h * 128 : (h + 1) * 128] = side32[start : start + 2]
    for copy in got_w3:
        copy.wait()
    g3[1] = jnp.zeros((KW, 768), BF16)
    g3[18] = jnp.zeros((KW, 768), BF16)

    def conv_three_post(t, z):
        for i in range(8):
            row = 2 + 8 * t + i
            act, slope = silu_parts(0.5 * z[i * KW : i * KW + KP, :])
            keep = 0.5 * mask[row]
            line = cp[row - 2] * slope * jnp.concatenate([keep, keep], axis=1)
            put_line(g3, row, [before(line), line, after(line)])
            coarse[row - 2] = act[:KO].astype(BF16)

    pipeline(2, lambda t: product(around(x3, 2 + 8 * t, 8, slice(0, 384)), w3[...]), conv_three_post, z0, z1)
    put_coarse = fetch(coarse.at[pl.ds(2, 12)], coarse_out, 0)

    def back_three_post(t, z):
        for i in range(8):
            low = 2 + 8 * t + i
            line = 0.25 * z[i * KW : i * KW + KP, 0:128]
            xb2[low] = line
            line = line * mask[low]
            for r in range(2):
                row = 2 * low + r
                zero, one = (line * d2[row, :, q * 128 : (q + 1) * 128] for q in range(2))
                put_line(g2, row, [before(one), zero, one, after(zero)])

    def back_three_dot(t):
        return product_turned(around(g3, 2 + 8 * t, 8, slice(0, 768)), w3b[...])

    pipeline(2, back_three_dot, back_three_post, z0, z1)
    acc3[...] = weight_terms(
        g3[4:16, 0:KO, 256:512].reshape(12 * KO, 256), around(x3, 4, 12, slice(0, 384), KO)
    )
    acc[...] = weight_terms(
        g2[8:32, 0:KO, 128:384].reshape(24 * KO, 256), around(x2, 8, 24, slice(0, 512), KO)
    )
    got_w2b.wait()
    got_d1.wait()

    def back_two_post(t, z):
        for i in range(7):
            m = 6 + 7 * t + i
            low = m // 2
            keep = 0.25 * mask[low]
            base = xb2[low]
            both = [(base + z[i * KW : i * KW + KP, q * 128 : (q + 1) * 128]) * keep for q in range(2)]
            for r in range(2):
                row = 2 * m + r
                slopes = [d1[row, :, p * 128 : (p + 1) * 128].astype(F32)[:KP] for p in range(4)]
                planes = [both[p // 2] * slopes[p] for p in range(4)]
                for n, line in enumerate([before(planes[3])] + planes + [after(planes[0])]):
                    g1[row - 12, :, n * 128 : (n + 1) * 128] = line[:KO].astype(BF16)

    pipeline(
        4, lambda t: product_turned(around(g2, 6 + 7 * t, 7, slice(0, 512)), w2b[...]), back_two_post, z0, z1
    )
    put_g1 = fetch(g1.at[pl.ds(3, 50)], g1_out, 1)
    got_x1.wait()

    def fold_weights(at):
        for u in range(3):
            for v in range(3):
                left = (4 * u + v) * 128
                term = acc[0:128, left : left + 128] + acc[128:256, left + 128 : left + 256]
                gw[at, pl.ds(8 + (3 * u + v) * 128, 128), :] = term.T

    def one_chunk(t):
        grads = jnp.concatenate(
            [g1[4 + 16 * t : 20 + 16 * t, :, lanes].reshape(512, 256) for lanes in (slice(128, 384), slice(384, 640))],
            axis=0,
        )
        fields = jnp.concatenate(
            [around(x1, 16 + 16 * t, 16, lanes, KO) for lanes in (slice(0, 512), slice(256, 768))], axis=0
        )
        return weight_terms(grads, fields)

    fold_weights(1)
    acc[...] = one_chunk(0)
    for tap in range(9):
        turned = acc3[:, tap * 128 : (tap + 1) * 128].T
        gw[2, pl.ds(8 + tap * 128, 128), :] = turned[:, 0:128]
        gw[3, pl.ds(8 + tap * 128, 128), :] = turned[:, 128:256]
    acc[...] += one_chunk(1)
    acc[...] += one_chunk(2)
    fold_weights(0)
    line = lax.broadcasted_iota(jnp.int32, (8, 128), 0)
    none = jnp.zeros((8, 128), F32)
    for owner in range(128):
        at = 8 + 9 * owner
        parts = [gw[0, at : at + 8, :]]
        for t in range(1, 5):
            rest = gw[t - 1, at + 9 - t : at + 17 - t, :]
            start = gw[t, at - t : at + 8 - t, :] if t < 4 else none
            parts.append(jnp.where(line < t, rest, start))
        row, col = divmod(owner, 8)
        msg[row % 2, col * 8 + row // 2] = jnp.concatenate(parts, axis=0).astype(BF16)
    put_keep = fetch(msg.at[core], keep_out, 2)
    put_give = fetch(msg.at[1 - core], give_out, 3)
    put_keep.wait()
    put_give.wait()
    put_coarse.wait()
    put_g1.wait()


def levels(grid_rows, grid_cols, *args):
    def kernel(*refs):
        lines_kernel(grid_rows, grid_cols, *refs)

    vm = pltpu.VMEM
    return pl.pallas_call(
        kernel,
        out_shape=[
            jax.ShapeDtypeStruct((12, KO, 256), BF16),
            jax.ShapeDtypeStruct((50, KO, 768), BF16),
            jax.ShapeDtypeStruct((64, 40, 128), BF16),
            jax.ShapeDtypeStruct((64, 40, 128), BF16),
        ],
        in_specs=[smem_spec()] + [vmem_spec()] * 3 + [any_spec()] * 13,
        out_specs=[any_spec()] * 4,
        scratch_shapes=[
            vm((2, HALO + 1, 10, 16, 128), BF16),
            vm((4, 160, 128), F32),
            vm((PAD_ROWS, KW, 768), BF16),
            vm((PAD_ROWS, KW, 512), BF16),
            vm((PAIRS, KW, 512), BF16),
            vm((PAIRS, KP, 256), F32),
            vm((LOWS, KW, 384), BF16),
            vm((16, KP, 256), F32),
            vm((2, 3, 16, 128), BF16),
            vm((48, 128), F32),
            vm((LOWS, KW, 768), BF16),
            vm((LOWS, KP, 128), F32),
            vm((PAIRS, KW, 512), BF16),
            vm((56, KO, 768), BF16),
            vm((16, KO, 256), BF16),
            vm((256, 1536), F32),
            vm((256, 1152), F32),
            vm((4, 1168, 128), F32),
            vm((2, 64, 40, 128), BF16),
            vm((LOWS, KP, 128), F32),
            vm((12 * KW, 256), F32),
            vm((12 * KW, 256), F32),
            vm((12, KO, 256), BF16),
            vm((1536, 256), BF16),
            vm((1536, 256), BF16),
            vm((256, 1536), BF16),
            vm((1152, 256), BF16),
            vm((128, 2304), BF16),
            pltpu.SemaphoreType.DMA((15,)),
        ],
        compiler_params=pltpu.CompilerParams(vmem_limit_bytes=38 * MIB),
        name="encoder_levels",
    )(*args)


def input_kernel(g1, g1_next, w1b, out, stage):
    for t in range(2):
        halves = []
        for lanes in (slice(0, 512), slice(256, 768)):
            rows = jnp.concatenate([g1[:, :, lanes], g1_next[:, :, lanes]], axis=0)
            parts = [rows[4 * t + u : 4 * t + u + 4].reshape(128, 512) for u in range(3)]
            halves.append(jnp.concatenate(parts, axis=1))
        total = product_turned(jnp.concatenate(halves, axis=0), w1b[...])
        for r in range(4):
            for p in range(4):
                rows = (p // 2) * 128 + r * 32
                value = total[rows : rows + 32, (p % 2) * 128 : (p % 2 + 1) * 128]
                stage[4 * t + r, pl.ds(p, 32, stride=4), :] = value
            out[4 * t + r] = stage[4 * t + r].astype(BF16)


def input_grad(g1, w1b):
    return pl.pallas_call(
        input_kernel,
        grid=(6,),
        out_shape=jax.ShapeDtypeStruct((ROWS, 128, 128), BF16),
        in_specs=[
            pl.BlockSpec((8, KO, 768), lambda i: (i, 0, 0)),
            pl.BlockSpec((2, KO, 768), lambda i: (4 * i + 4, 0, 0)),
            pl.BlockSpec((256, 1536), lambda i: (0, 0)),
        ],
        out_specs=pl.BlockSpec((8, 128, 128), lambda i: (i, 0, 0)),
        scratch_shapes=[pltpu.VMEM((8, 128, 128), F32)],
        compiler_params=pltpu.CompilerParams(vmem_limit_bytes=16 * MIB),
        cost_estimate=pl.CostEstimate(flops=2 * 6144 * 1152 * 128, bytes_accessed=8 * 1024 * 1024, transcendentals=0),
        name="input_grad",
    )(g1, g1, w1b)


def collect(got):
    sums = got.astype(F32).sum(axis=0)
    return sums[0:9], sums[9:18], jnp.concatenate([sums[18:27], sums[27:36]], axis=1)


def swapped(block, axis, odd_first):
    devices = lax.axis_size(axis)
    pairs = []
    for i in range(1 if odd_first else 0, devices - 1, 2):
        pairs += [(i, i + 1), (i + 1, i)]
    return lax.ppermute(block, axis, pairs)


def body(inputs, weight_one, weight_two, weight_three, noise_table, frequency, anchor, noise_index, cotangent):
    grid = (lax.axis_size(ROW_AXES) * ROWS, lax.axis_size("tx") * 4 * KO)
    inputs = inputs.reshape(ROWS, 8, 16, 128)
    one, two, cots = sides(inputs, cotangent)
    two = swapped(two, "tx", True)
    one = swapped(one, "tx", False)
    w1t, w1b, w2t, w2b, w3b, rows_sc, cols_sc = prep(*grid, anchor, weight_one, weight_two, weight_three, frequency)
    off, near = rims(inputs, cots, one, two, rows_sc)
    off = swapped(off, ROW_AXES, True)
    near = lax.ppermute(near, "core", [(0, 1), (1, 0)])
    x1, d1, x2 = own_rows(*grid, noise_index, rows_sc, cols_sc, noise_table, inputs, one, two, w1t)
    coarse, g1, keep_msg, give_msg = levels(
        *grid, noise_index, rows_sc, cols_sc, noise_table, cotangent, w1t,
        off, near, one, two, w2t, w2b, weight_three, w3b, x1, d1, x2,
    )
    other = lax.ppermute(give_msg, "core", [(0, 1), (1, 0)])
    msg = (keep_msg.astype(F32) + other.astype(F32)).astype(BF16)
    got = lax.all_to_all(msg, "tx", 0, 0, tiled=True)
    grad_inputs = input_grad(g1, w1b)
    got, grad_inputs = lax.optimization_barrier((got, grad_inputs))
    msg = got.reshape(8, 8, 40, 128).astype(F32).sum(axis=0).astype(BF16)
    got = lax.all_to_all(msg, "chip", 0, 0, tiled=True)
    return (coarse, grad_inputs, *collect(got))


def solution(mesh):
    halves = jax.sharding.Mesh(mesh.devices.reshape(-1, 2, mesh.devices.shape[1]), ("chip", "core", "tx"))
    placed = (P(ROW_AXES, "tx", None), P(), P(), P(), P(), P(), P(), P(), P(ROW_AXES, "tx", None))
    return jax.shard_map(
        body,
        mesh=halves,
        in_specs=placed,
        out_specs=(
            P(ROW_AXES, "tx", None),
            P(ROW_AXES, "tx", None),
            P((*ROW_AXES, "tx"), None),
            P((*ROW_AXES, "tx"), None),
            P((*ROW_AXES, "tx"), None),
        ),
        check_vma=False,
    )
```

```python
import jax
import jax.numpy as jnp
from jax import lax
from jax.experimental import pallas as pl
from jax.experimental.pallas import tpu as pltpu
from jax.sharding import PartitionSpec as P

BF16 = jnp.bfloat16
F32 = jnp.float32

KO = 32
KP = 40
KW = 48
HALO = 16
ROWS = 48
PAD_ROWS = ROWS + 2 * HALO
PAIRS = PAD_ROWS // 2
LOWS = PAIRS // 2
MIB = 1024 * 1024


def any_spec():
    return pl.BlockSpec(memory_space=pl.ANY)


def vmem_spec():
    return pl.BlockSpec(memory_space=pltpu.VMEM)


def smem_spec():
    return pl.BlockSpec(memory_space=pltpu.SMEM)


ROW_AXES = ("chip", "core")


def own_place():
    return lax.axis_index(ROW_AXES), lax.axis_index("tx")


def odd_column():
    return lax.rem(lax.axis_index("tx"), 2)


def side_kernel(inputs, cot, one, two, side32, sems):
    odd = odd_column()
    copies = [
        pltpu.make_async_copy(inputs.at[:, 7 - 7 * odd], one.at[pl.ds(1, ROWS)], sems.at[0]),
        pltpu.make_async_copy(inputs.at[:, 7 * odd], two.at[pl.ds(1, ROWS)], sems.at[1]),
    ]
    for copy in copies:
        copy.start()
    for target, at_left in ((one, odd == 1), (two, odd == 0)):
        for r in range(12):
            line = cot[r].astype(F32)
            for h in range(2):
                lanes = slice(h * 128, (h + 1) * 128)
                side32[pl.ds(r * 4 + h * 2, 2)] = jnp.where(at_left, line[0:2, lanes], line[30:32, lanes])
        side = side32[...].astype(BF16).reshape(3, 16, 128)
        target[pl.ds(0, 1)] = side[0:1]
        target[pl.ds(1 + ROWS, 3)] = side
    for copy in copies:
        copy.wait()


def sides(inputs, cot):
    return pl.pallas_call(
        side_kernel,
        out_shape=[jax.ShapeDtypeStruct((ROWS + 4, 16, 128), BF16)] * 2,
        in_specs=[any_spec(), vmem_spec()],
        out_specs=[vmem_spec()] * 2,
        scratch_shapes=[pltpu.VMEM((48, 128), F32), pltpu.SemaphoreType.DMA((2,))],
        compiler_params=pltpu.CompilerParams(vmem_limit_bytes=8 * MIB),
        name="pack_columns",
    )(inputs, cot)


def edge_kernel(inputs, cot, _, off, cots, sem):
    core = lax.axis_index("core")
    copy = pltpu.make_async_copy(inputs.at[pl.ds((ROWS - HALO) * core, HALO)], off.at[pl.ds(0, HALO)], sem)
    copy.start()
    for r in range(2):
        for h in range(2):
            lanes, units = slice(h * 128, (h + 1) * 128), pl.ds((r * 2 + h) * 2, 2)
            off[HALO, units] = cot[10 * core + r, :, lanes].reshape(2, 16, 128)
            cots[units] = cot[10 - 10 * core + r, :, lanes].reshape(2, 16, 128)
    copy.wait()


def edges(*args):
    return pl.pallas_call(
        edge_kernel,
        out_shape=[jax.ShapeDtypeStruct((HALO + 1, 8, 16, 128), BF16), jax.ShapeDtypeStruct((8, 16, 128), BF16)],
        in_specs=[any_spec(), vmem_spec(), any_spec()],
        out_specs=[vmem_spec()] * 2,
        scratch_shapes=[pltpu.SemaphoreType.DMA],
        compiler_params=pltpu.CompilerParams(vmem_limit_bytes=8 * MIB),
        name="pack_off_rows",
    )(*args)


def rim_kernel(inputs, cots, one, two, _, near, corner, sems):
    core = lax.axis_index("core")
    copies = []

    def fetch(source, target):
        copy = pltpu.make_async_copy(source, target, sems.at[len(copies)])
        copy.start()
        copies.append(copy)

    body = pl.ds(0, HALO)
    fetch(inputs.at[pl.ds((ROWS - HALO) * (1 - core), HALO)], near.at[body, pl.ds(0, 8)])
    fetch(cots, near.at[HALO, pl.ds(0, 8)])
    for target, low, first in ((near, 1 - core, 8), (corner, core, 0)):
        for unit, side in ((first, one), (first + 1, two)):
            fetch(side.at[pl.ds(1 + (ROWS - HALO) * low, HALO)], target.at[body, unit])
            fetch(side.at[(3 + ROWS) * low], target.at[HALO, unit])
    for copy in copies:
        copy.wait()


def rims(*args):
    return pl.pallas_call(
        rim_kernel,
        out_shape=[jax.ShapeDtypeStruct((HALO + 1, units, 16, 128), BF16) for units in (10, 2)],
        in_specs=[any_spec()] * len(args),
        out_specs=[vmem_spec()] * 2,
        scratch_shapes=[pltpu.SemaphoreType.DMA((10,))],
        compiler_params=pltpu.CompilerParams(vmem_limit_bytes=8 * MIB),
        name="pack_rows",
    )(*args)


def weight_forms(w1, w2, w3, w1t, w1b, w2t, w2b, w3b):
    zero = jnp.zeros((128, 128), BF16)
    for source, ahead, back in ((w1, w1t, w1b), (w2, w2t, w2b)):
        for u in range(3):
            for v in range(3):
                tap = source[pl.ds((3 * u + v) * 128, 128), :]
                for i in range(2):
                    side = slice(i * 128, (i + 1) * 128)
                    ahead[pl.ds((4 * u + v + i) * 128, 128), side] = tap
                    at = (4 * (2 - u) + 2 - v + i) * 128
                    back[side, at : at + 128] = tap
            for i, j in ((0, 3), (1, 0)):
                at = (4 * u + j) * 128
                side = slice(i * 128, (i + 1) * 128)
                ahead[pl.ds(at, 128), side] = zero
                back[side, at : at + 128] = zero
    for u in range(3):
        for v in range(3):
            at = (3 * (2 - u) + 2 - v) * 256
            w3b[:, at : at + 256] = w3[pl.ds((3 * u + v) * 128, 128), :]


def wave_tables(grid_rows, grid_cols, anchor, frequency, rows_sc, cols_sc):
    own_row, own_col = own_place()
    row = lax.broadcasted_iota(jnp.int32, (PAD_ROWS, 128), 0) - HALO + own_row * ROWS
    angle = (row + anchor[0]).astype(F32) * frequency[0:1, :]
    keep = jnp.where((row >= 0) & (row < grid_rows), 1.0, 0.0)
    rows_sc[0] = jnp.sin(angle) * keep
    rows_sc[1] = jnp.cos(angle) * keep
    for p in range(4):
        k = lax.broadcasted_iota(jnp.int32, (KP, 128), 0)
        col = 4 * jnp.where(k < KO + 4, k, k - KP) + p + own_col * (4 * KO)
        angle = (col + anchor[1]).astype(F32) * frequency[1:2, :]
        keep = jnp.where((col >= 0) & (col < grid_cols), 1.0, 0.0)
        cols_sc[0, p] = jnp.sin(angle) * keep
        cols_sc[1, p] = jnp.cos(angle) * keep


def prep_kernel(grid_rows, grid_cols, anchor, w1, w2, w3, frequency, w1t, w1b, w2t, w2b, w3b, rows_sc, cols_sc):
    weight_forms(w1, w2, w3, w1t, w1b, w2t, w2b, w3b)
    wave_tables(grid_rows, grid_cols, anchor, frequency, rows_sc, cols_sc)


def prep(grid_rows, grid_cols, anchor, w1, w2, w3, frequency):
    def kernel(*refs):
        prep_kernel(grid_rows, grid_cols, *refs)

    shape = jax.ShapeDtypeStruct
    return pl.pallas_call(
        kernel,
        out_shape=[
            shape((1536, 256), BF16),
            shape((256, 1536), BF16),
            shape((1536, 256), BF16),
            shape((256, 1536), BF16),
            shape((128, 2304), BF16),
            shape((2, PAD_ROWS, 128), F32),
            shape((2, 4, KP, 128), F32),
        ],
        in_specs=[smem_spec()] + [vmem_spec()] * 4,
        out_specs=[vmem_spec()] * 7,
        compiler_params=pltpu.CompilerParams(vmem_limit_bytes=12 * MIB),
        name="weight_forms",
    )(anchor, w1, w2, w3, frequency)


def fill_mask(low_rows, low_cols, mask):
    own_row, own_col = own_place()
    k = lax.broadcasted_iota(jnp.int32, (KP, 128), 0)
    col = jnp.where(k < KO + 4, k, k - KP) + own_col * KO
    inside = jnp.where((col >= 0) & (col < low_cols), 1.0, 0.0)

    def step(at, _):
        row = at - 4 + own_row * 12
        mask[at] = inside * jnp.where((row >= 0) & (row < low_rows), 1.0, 0.0)
        return 0

    lax.fori_loop(0, LOWS, step, 0)


def widened(line):
    rest = jnp.zeros((KW - KP, line.shape[1]), F32)
    return jnp.concatenate([line, rest], axis=0).astype(BF16)


def put_line(ref, row, planes):
    width = planes[0].shape[1]
    for n, plane in enumerate(planes):
        ref[row, :, n * width : (n + 1) * width] = widened(plane)


def before(line):
    return pltpu.roll(line, 1, 0)


def after(line):
    return pltpu.roll(line, KP - 1, 0)


def silu_parts(half):
    th = jnp.tanh(half)
    act = half + half * th
    return act, (1.0 + act) + th * (1.0 - act)


def rounded(value):
    return value.astype(BF16).astype(F32)


def flat(block):
    return block.reshape(128, 128)


def modulation(noise, noise_index):
    modulate = noise[pl.ds(noise_index[0], 1), :]
    return 1.0 + modulate[:, 0:128], modulate[:, 128:256]


def first_lines(load, base, at, tables, stage, x1):
    rows_sc, cols_sc = tables
    for i in range(4):
        own, right, left = load(i)
        stage[i, 0:128] = own.astype(F32)
        stage[i, 128:144] = right.astype(F32)
        stage[i, 144:160] = left.astype(F32)
        sin_row = rows_sc[0, pl.ds(base + i, 1), :]
        cos_row = rows_sc[1, pl.ds(base + i, 1), :]
        planes = []
        for p in range(4):
            value = stage[i, pl.ds(p, KP, stride=4), :]
            planes.append(value + (sin_row * cols_sc[1, p] + cos_row * cols_sc[0, p]))
        put_line(x1, at + i, [before(planes[3])] + planes + [after(planes[0])])


def around(ref, at, count, lanes, cols=KW):
    parts = [ref[pl.ds(at - 1 + u, count), 0:cols, lanes] for u in range(3)]
    return jnp.concatenate([part.reshape(count * cols, part.shape[-1]) for part in parts], axis=1)


def product(left, right):
    return jnp.dot(left, right, preferred_element_type=F32)


def product_turned(left, right):
    return lax.dot_general(left, right, (((1,), (1,)), ((), ())), preferred_element_type=F32)


def weight_terms(grad, field):
    return lax.dot_general(grad, field, (((0,), (0,)), ((), ())), preferred_element_type=F32)


def pipeline(steps, dot, post, z0, z1):
    z = (z0, z1)
    for t in range(steps + 1):
        if t < steps:
            total = dot(t)
            z[t % 2][0 : total.shape[0], 0 : total.shape[1]] = total
        if t > 0:
            post(t - 1, z[(t - 1) % 2])


def conv_one_dot(x1, row, w1t):
    one = around(x1, row, 4, slice(0, 512))
    two = around(x1, row, 4, slice(256, 768))
    return product(jnp.concatenate([one, two], axis=0), w1t[...])


def conv_one_post(z, scale, shift, keeps, d1, d1_row, x2, x2_row):
    half_scale, half_shift = 0.5 * scale, 0.5 * shift
    slope_scale = half_scale.astype(BF16)
    for s in range(2):
        halves = []
        for q in range(2):
            sums = []
            for p in (2 * q, 2 * q + 1):
                lanes = slice((p % 2) * 128, (p % 2 + 1) * 128)
                acts = []
                for r in range(2):
                    at = q * 4 * KW + (2 * s + r) * KW
                    act, slope = silu_parts((z[at : at + KW, lanes] * half_scale + half_shift).astype(BF16))
                    d1[d1_row + 2 * s + r, :, p * 128 : (p + 1) * 128] = slope_scale * slope
                    acts.append(act)
                sums.append((acts[0] + acts[1]).astype(F32))
            halves.append((sums[0] + sums[1])[:KP] * (0.25 * keeps[s]))
        put_line(x2, x2_row + s, [before(halves[1]), halves[0], halves[1], after(halves[0])])


def own_kernel(
    grid_rows, grid_cols,
    noise_index, rows_sc, cols_sc, noise, inputs, w1t, one, two,
    x1_out, d1_out, x2_out,
    x1, stage, d1, x2, mask, side, z0, z1, sems,
):
    odd = odd_column()
    halos = [
        pltpu.make_async_copy(one, side.at[1 - odd], sems.at[0]),
        pltpu.make_async_copy(two, side.at[odd], sems.at[1]),
    ]
    for copy in halos:
        copy.start()
    fill_mask(grid_rows // 4, grid_cols // 4, mask)
    scale, shift = modulation(noise, noise_index)
    for copy in halos:
        copy.wait()

    def first(q):
        def load(i):
            row = 4 * q + i
            return flat(inputs[row]), side[1, 1 + row], side[0, 1 + row]

        first_lines(load, HALO + 4 * q, 4 * q, (rows_sc, cols_sc), stage, x1)

    def dot(t):
        return conv_one_dot(x1, 4 * t + 2, w1t)

    def post(t, z):
        keeps = [mask[(9 + 2 * t) // 2], mask[(10 + 2 * t) // 2]]
        conv_one_post(z, scale, shift, keeps, d1, 4 * t, x2, 2 * t)

    first(0)
    first(1)
    z = (z0, z1)
    for t in range(11):
        z[t % 2][...] = dot(t)
        if t + 2 < 12:
            first(t + 2)
        if t > 0:
            post(t - 1, z[(t - 1) % 2])
        if t == 9:
            put_x1 = pltpu.make_async_copy(x1, x1_out, sems.at[2])
            put_x1.start()
    post(10, z0)
    put_d1 = pltpu.make_async_copy(d1, d1_out, sems.at[3])
    put_x2 = pltpu.make_async_copy(x2, x2_out, sems.at[4])
    put_d1.start()
    put_x2.start()
    put_x1.wait()
    put_d1.wait()
    put_x2.wait()


def own_rows(grid_rows, grid_cols, *args):
    def kernel(*refs):
        own_kernel(grid_rows, grid_cols, *refs)

    vm = pltpu.VMEM
    shape = jax.ShapeDtypeStruct
    return pl.pallas_call(
        kernel,
        out_shape=[shape((48, KW, 768), BF16), shape((44, KW, 512), BF16), shape((22, KW, 512), BF16)],
        in_specs=[smem_spec()] + [vmem_spec()] * 5 + [any_spec()] * 2,
        out_specs=[any_spec()] * 3,
        scratch_shapes=[
            vm((48, KW, 768), BF16),
            vm((4, 160, 128), F32),
            vm((44, KW, 512), BF16),
            vm((22, KW, 512), BF16),
            vm((LOWS, KP, 128), F32),
            vm((2, ROWS + 4, 16, 128), BF16),
            vm((8 * KW, 256), F32),
            vm((8 * KW, 256), F32),
            pltpu.SemaphoreType.DMA((5,)),
        ],
        compiler_params=pltpu.CompilerParams(vmem_limit_bytes=18 * MIB),
        cost_estimate=pl.CostEstimate(flops=4 * 10**9, bytes_accessed=30 * 10**6, transcendentals=0),
        name="own_rows",
    )(*args)


def lines_kernel(
    grid_rows, grid_cols,
    noise_index, rows_sc, cols_sc, noise,
    cot, w1t, w2t, w2b, w3, w3b, off, corner, near, one, two, x1_in, d1_in, x2_in,
    coarse_out, g1_out, keep_out, give_out,
    rim, stage, x1, d1, x2, d2, x3, cp, side, side32, g3, xb2, g2, g1, coarse,
    acc, acc3, gw, msg, mask, z0, z1, sems,
):
    core = lax.axis_index("core")
    odd = odd_column()

    def fetch(source, target, at):
        copy = pltpu.make_async_copy(source, target, sems.at[at])
        copy.start()
        return copy

    got_rims = [
        fetch(off, rim.at[core, :, pl.ds(0, 8)], 0),
        fetch(corner, rim.at[core, :, pl.ds(8, 2)], 7),
        fetch(near, rim.at[1 - core], 1),
    ]
    got_edges = [
        fetch(x1_in.at[pl.ds(0, 4)], x1.at[pl.ds(16, 4)], 2),
        fetch(x1_in.at[pl.ds(44, 4)], x1.at[pl.ds(60, 4)], 3),
    ]
    got_x2 = fetch(x2_in, x2.at[pl.ds(9, 22)], 4)
    units = pl.ds(ROWS + 1, 3)
    got_sides = [fetch(one.at[units], side.at[1 - odd], 5), fetch(two.at[units], side.at[odd], 6)]
    got_d1 = fetch(d1_in, d1.at[pl.ds(18, 44)], 8)
    got_x1 = fetch(x1_in.at[pl.ds(4, 40)], x1.at[pl.ds(20, 40)], 9)
    fill_mask(grid_rows // 4, grid_cols // 4, mask)
    gw[:, 0:8, :] = jnp.zeros((4, 8, 128), F32)
    gw[:, 1160:1168, :] = jnp.zeros((4, 8, 128), F32)
    scale, shift = modulation(noise, noise_index)
    for copy in got_rims:
        copy.wait()

    def first(n):
        below, start = n // 4, 4 * (n % 4)
        base = start + (HALO + ROWS) * below

        def load(i):
            row = start + i
            return flat(rim[below, row, 0:8]), rim[below, row, 8 + odd], rim[below, row, 9 - odd]

        first_lines(load, base, base, (rows_sc, cols_sc), stage, x1)

    def mid_of(t):
        return 1 + 2 * t if t < 4 else 23 + 2 * t

    def dot(t):
        return conv_one_dot(x1, 2 * mid_of(t), w1t)

    def post(t, z):
        m = mid_of(t)
        conv_one_post(z, scale, shift, [mask[m // 2], mask[(m + 1) // 2]], d1, 2 * m, x2, m)

    first(0)
    first(1)
    for copy in got_edges:
        copy.wait()
    z = (z0, z1)
    for t in range(8):
        z[t % 2][0 : 8 * KW, :] = dot(t)
        if t + 2 < 8:
            first(t + 2)
        if t > 0:
            post(t - 1, z[(t - 1) % 2])
    post(7, z1)
    got_x2.wait()

    def conv_two_post(t, z):
        for s in range(6):
            low = 1 + 6 * t + s
            total = None
            for q in range(2):
                lanes = slice(q * 128, (q + 1) * 128)
                for r in range(2):
                    row, at = 2 * low + r, (2 * s + r) * KW
                    act, slope = silu_parts(0.5 * z[at : at + KP, lanes])
                    d2[row, :, lanes] = 0.5 * slope
                    down = x2[row, :, (q + 1) * 128 : (q + 2) * 128].astype(F32)[:KP]
                    act = rounded(down + act)
                    total = act if total is None else total + act
            line = total * (0.25 * mask[low])
            put_line(x3, low, [before(line), line, after(line)])

    pipeline(3, lambda t: product(around(x2, 2 + 12 * t, 12, slice(0, 512)), w2t[...]), conv_two_post, z0, z1)

    cp[...] = jnp.zeros_like(cp)
    for copy in got_sides:
        copy.wait()
    for h in range(2):
        lanes = slice(h * 128, (h + 1) * 128)
        for r in range(2):
            units = pl.ds((r * 2 + h) * 2, 2)
            cp[r, 0:KO, lanes] = rim[0, HALO, units].reshape(KO, 128).astype(F32)
            cp[14 + r, 0:KO, lanes] = rim[1, HALO, units].reshape(KO, 128).astype(F32)
    for r in range(12):
        cp[2 + r, 0:KO, :] = cot[r].astype(F32)
    for which, at in ((1, KO), (0, KP - 2)):
        side32[...] = side[which].reshape(48, 128).astype(F32)
        for h in range(2):
            for r in range(12):
                cp[2 + r, at : at + 2, h * 128 : (h + 1) * 128] = side32[r * 4 + h * 2 : r * 4 + h * 2 + 2]
    for below, skip, row in ((0, 8, 0), (1, 0, 14)):
        for unit, at in ((9 - odd, KP - 2), (8 + odd, KO)):
            side32[0:16] = rim[below, HALO, unit].astype(F32)
            for h in range(2):
                for r in range(2):
                    start = skip + r * 4 + h * 2
                    cp[row + r, at : at + 2, h * 128 : (h + 1) * 128] = side32[start : start + 2]
    g3[1] = jnp.zeros((KW, 768), BF16)
    g3[18] = jnp.zeros((KW, 768), BF16)

    def conv_three_post(t, z):
        for i in range(8):
            row = 2 + 8 * t + i
            act, slope = silu_parts(0.5 * z[i * KW : i * KW + KP, :])
            keep = 0.5 * mask[row]
            line = cp[row - 2] * slope * jnp.concatenate([keep, keep], axis=1)
            put_line(g3, row, [before(line), line, after(line)])
            coarse[row - 2] = act[:KO].astype(BF16)

    pipeline(2, lambda t: product(around(x3, 2 + 8 * t, 8, slice(0, 384)), w3[...]), conv_three_post, z0, z1)
    put_coarse = fetch(coarse.at[pl.ds(2, 12)], coarse_out, 0)

    def back_three_post(t, z):
        for i in range(8):
            low = 2 + 8 * t + i
            line = 0.25 * z[i * KW : i * KW + KP, 0:128]
            xb2[low] = line
            line = line * mask[low]
            for r in range(2):
                row = 2 * low + r
                zero, one = (line * d2[row, :, q * 128 : (q + 1) * 128] for q in range(2))
                put_line(g2, row, [before(one), zero, one, after(zero)])

    def back_three_dot(t):
        return product_turned(around(g3, 2 + 8 * t, 8, slice(0, 768)), w3b[...])

    pipeline(2, back_three_dot, back_three_post, z0, z1)
    acc3[...] = weight_terms(
        g3[4:16, 0:KO, 256:512].reshape(12 * KO, 256), around(x3, 4, 12, slice(0, 384), KO)
    )
    acc[...] = weight_terms(
        g2[8:32, 0:KO, 128:384].reshape(24 * KO, 256), around(x2, 8, 24, slice(0, 512), KO)
    )
    got_d1.wait()

    def back_two_post(t, z):
        for i in range(7):
            m = 6 + 7 * t + i
            low = m // 2
            keep = 0.25 * mask[low]
            base = xb2[low]
            both = [(base + z[i * KW : i * KW + KP, q * 128 : (q + 1) * 128]) * keep for q in range(2)]
            for r in range(2):
                row = 2 * m + r
                slopes = [d1[row, :, p * 128 : (p + 1) * 128].astype(F32)[:KP] for p in range(4)]
                planes = [both[p // 2] * slopes[p] for p in range(4)]
                for n, line in enumerate([before(planes[3])] + planes + [after(planes[0])]):
                    g1[row - 12, :, n * 128 : (n + 1) * 128] = line[:KO].astype(BF16)

    pipeline(
        4, lambda t: product_turned(around(g2, 6 + 7 * t, 7, slice(0, 512)), w2b[...]), back_two_post, z0, z1
    )
    put_g1 = fetch(g1.at[pl.ds(3, 50)], g1_out, 1)
    got_x1.wait()

    def fold_weights(at):
        for u in range(3):
            for v in range(3):
                left = (4 * u + v) * 128
                term = acc[0:128, left : left + 128] + acc[128:256, left + 128 : left + 256]
                gw[at, pl.ds(8 + (3 * u + v) * 128, 128), :] = term.T

    def one_chunk(t):
        grads = jnp.concatenate(
            [g1[4 + 16 * t : 20 + 16 * t, :, lanes].reshape(512, 256) for lanes in (slice(128, 384), slice(384, 640))],
            axis=0,
        )
        fields = jnp.concatenate(
            [around(x1, 16 + 16 * t, 16, lanes, KO) for lanes in (slice(0, 512), slice(256, 768))], axis=0
        )
        return weight_terms(grads, fields)

    fold_weights(1)
    acc[...] = one_chunk(0)
    for tap in range(9):
        turned = acc3[:, tap * 128 : (tap + 1) * 128].T
        gw[2, pl.ds(8 + tap * 128, 128), :] = turned[:, 0:128]
        gw[3, pl.ds(8 + tap * 128, 128), :] = turned[:, 128:256]
    acc[...] += one_chunk(1)
    acc[...] += one_chunk(2)
    fold_weights(0)
    line = lax.broadcasted_iota(jnp.int32, (8, 128), 0)
    none = jnp.zeros((8, 128), F32)
    for owner in range(128):
        at = 8 + 9 * owner
        parts = [gw[0, at : at + 8, :]]
        for t in range(1, 5):
            rest = gw[t - 1, at + 9 - t : at + 17 - t, :]
            start = gw[t, at - t : at + 8 - t, :] if t < 4 else none
            parts.append(jnp.where(line < t, rest, start))
        row, col = divmod(owner, 8)
        msg[row % 2, (row // 2) * 8 + col] = jnp.concatenate(parts, axis=0).astype(BF16)
    put_keep = fetch(msg.at[core], keep_out, 2)
    put_give = fetch(msg.at[1 - core], give_out, 3)
    put_keep.wait()
    put_give.wait()
    put_coarse.wait()
    put_g1.wait()


def levels(grid_rows, grid_cols, *args):
    def kernel(*refs):
        lines_kernel(grid_rows, grid_cols, *refs)

    vm = pltpu.VMEM
    return pl.pallas_call(
        kernel,
        out_shape=[
            jax.ShapeDtypeStruct((12, KO, 256), BF16),
            jax.ShapeDtypeStruct((50, KO, 768), BF16),
            jax.ShapeDtypeStruct((64, 40, 128), BF16),
            jax.ShapeDtypeStruct((64, 40, 128), BF16),
        ],
        in_specs=[smem_spec()] + [vmem_spec()] * 9 + [any_spec()] * 8,
        out_specs=[any_spec()] * 4,
        scratch_shapes=[
            vm((2, HALO + 1, 10, 16, 128), BF16),
            vm((4, 160, 128), F32),
            vm((PAD_ROWS, KW, 768), BF16),
            vm((PAD_ROWS, KW, 512), BF16),
            vm((PAIRS, KW, 512), BF16),
            vm((PAIRS, KP, 256), F32),
            vm((LOWS, KW, 384), BF16),
            vm((16, KP, 256), F32),
            vm((2, 3, 16, 128), BF16),
            vm((48, 128), F32),
            vm((LOWS, KW, 768), BF16),
            vm((LOWS, KP, 128), F32),
            vm((PAIRS, KW, 512), BF16),
            vm((56, KO, 768), BF16),
            vm((16, KO, 256), BF16),
            vm((256, 1536), F32),
            vm((256, 1152), F32),
            vm((4, 1168, 128), F32),
            vm((2, 64, 40, 128), BF16),
            vm((LOWS, KP, 128), F32),
            vm((12 * KW, 256), F32),
            vm((12 * KW, 256), F32),
            pltpu.SemaphoreType.DMA((10,)),
        ],
        compiler_params=pltpu.CompilerParams(vmem_limit_bytes=36 * MIB),
        name="encoder_levels",
    )(*args)


def input_kernel(g1, g1_next, w1b, out, stage):
    for t in range(2):
        halves = []
        for lanes in (slice(0, 512), slice(256, 768)):
            rows = jnp.concatenate([g1[:, :, lanes], g1_next[:, :, lanes]], axis=0)
            parts = [rows[4 * t + u : 4 * t + u + 4].reshape(128, 512) for u in range(3)]
            halves.append(jnp.concatenate(parts, axis=1))
        total = product_turned(jnp.concatenate(halves, axis=0), w1b[...])
        for r in range(4):
            for p in range(4):
                rows = (p // 2) * 128 + r * 32
                value = total[rows : rows + 32, (p % 2) * 128 : (p % 2 + 1) * 128]
                stage[4 * t + r, pl.ds(p, 32, stride=4), :] = value
            out[4 * t + r] = stage[4 * t + r].astype(BF16)


def input_grad(g1, w1b):
    return pl.pallas_call(
        input_kernel,
        grid=(6,),
        out_shape=jax.ShapeDtypeStruct((ROWS, 128, 128), BF16),
        in_specs=[
            pl.BlockSpec((8, KO, 768), lambda i: (i, 0, 0)),
            pl.BlockSpec((2, KO, 768), lambda i: (4 * i + 4, 0, 0)),
            pl.BlockSpec((256, 1536), lambda i: (0, 0)),
        ],
        out_specs=pl.BlockSpec((8, 128, 128), lambda i: (i, 0, 0)),
        scratch_shapes=[pltpu.VMEM((8, 128, 128), F32)],
        compiler_params=pltpu.CompilerParams(vmem_limit_bytes=16 * MIB),
        cost_estimate=pl.CostEstimate(flops=2 * 6144 * 1152 * 128, bytes_accessed=8 * 1024 * 1024, transcendentals=0),
        name="input_grad",
    )(g1, g1, w1b)


def collect(got):
    sums = got.astype(F32).sum(axis=0)
    return sums[0:9], sums[9:18], jnp.concatenate([sums[18:27], sums[27:36]], axis=1)


def swapped(block, axis, odd_first):
    devices = lax.axis_size(axis)
    pairs = []
    for i in range(1 if odd_first else 0, devices - 1, 2):
        pairs += [(i, i + 1), (i + 1, i)]
    return lax.ppermute(block, axis, pairs)


def body(inputs, weight_one, weight_two, weight_three, noise_table, frequency, anchor, noise_index, cotangent):
    grid = (lax.axis_size(ROW_AXES) * ROWS, lax.axis_size("tx") * 4 * KO)
    inputs = inputs.reshape(ROWS, 8, 16, 128)
    one, two = sides(inputs, cotangent)
    off, cots = edges(inputs, cotangent, two)
    two = swapped(two, "tx", True)
    one = swapped(one, "tx", False)
    off = swapped(off, ROW_AXES, True)
    w1t, w1b, w2t, w2b, w3b, rows_sc, cols_sc = prep(*grid, anchor, weight_one, weight_two, weight_three, frequency)
    near, corner = rims(inputs, cots, one, two, rows_sc)
    near = lax.ppermute(near, "core", [(0, 1), (1, 0)])
    corner, off = lax.optimization_barrier((corner, off))
    corner = swapped(corner, ROW_AXES, True)
    x1, d1, x2 = own_rows(*grid, noise_index, rows_sc, cols_sc, noise_table, inputs, w1t, one, two)
    coarse, g1, keep_msg, give_msg = levels(
        *grid, noise_index, rows_sc, cols_sc, noise_table,
        cotangent, w1t, w2t, w2b, weight_three, w3b, off, corner, near, one, two, x1, d1, x2,
    )
    other = lax.ppermute(give_msg, "core", [(0, 1), (1, 0)])
    msg = (keep_msg.astype(F32) + other.astype(F32)).astype(BF16)
    got = lax.all_to_all(msg, ("chip", "tx"), 0, 0, tiled=True)
    grad_inputs = input_grad(g1, w1b)
    return (coarse, grad_inputs, *collect(got))


def solution(mesh):
    halves = jax.sharding.Mesh(mesh.devices.reshape(-1, 2, mesh.devices.shape[1]), ("chip", "core", "tx"))
    placed = (P(ROW_AXES, "tx", None), P(), P(), P(), P(), P(), P(), P(), P(ROW_AXES, "tx", None))
    return jax.shard_map(
        body,
        mesh=halves,
        in_specs=placed,
        out_specs=(
            P(ROW_AXES, "tx", None),
            P(ROW_AXES, "tx", None),
            P((*ROW_AXES, "tx"), None),
            P((*ROW_AXES, "tx"), None),
            P((*ROW_AXES, "tx"), None),
        ),
        check_vma=False,
    )
```

```python
import jax
import jax.numpy as jnp
from jax import lax
from jax.experimental import pallas as pl
from jax.experimental.pallas import tpu as pltpu
from jax.sharding import PartitionSpec as P

BF16 = jnp.bfloat16
F32 = jnp.float32

KO = 32
KP = 40
KW = 48
HALO = 16
ROWS = 48
PAD_ROWS = ROWS + 2 * HALO
PAIRS = PAD_ROWS // 2
LOWS = PAIRS // 2
MIB = 1024 * 1024


def any_spec():
    return pl.BlockSpec(memory_space=pl.ANY)


def vmem_spec():
    return pl.BlockSpec(memory_space=pltpu.VMEM)


def smem_spec():
    return pl.BlockSpec(memory_space=pltpu.SMEM)


ROW_AXES = ("chip", "core")


def own_place():
    return lax.axis_index(ROW_AXES), lax.axis_index("tx")


def odd_column():
    return lax.rem(lax.axis_index("tx"), 2)


def side_kernel(inputs, cot, one, two, cots, side32, sems):
    odd = odd_column()
    copies = [
        pltpu.make_async_copy(inputs.at[:, 7 - 7 * odd], one.at[pl.ds(1, ROWS)], sems.at[0]),
        pltpu.make_async_copy(inputs.at[:, 7 * odd], two.at[pl.ds(1, ROWS)], sems.at[1]),
    ]
    for copy in copies:
        copy.start()
    for target, at_left in ((one, odd == 1), (two, odd == 0)):
        for r in range(12):
            line = cot[r].astype(F32)
            for h in range(2):
                lanes = slice(h * 128, (h + 1) * 128)
                side32[pl.ds(r * 4 + h * 2, 2)] = jnp.where(at_left, line[0:2, lanes], line[30:32, lanes])
        side = side32[...].astype(BF16).reshape(3, 16, 128)
        target[pl.ds(0, 1)] = side[0:1]
        target[pl.ds(1 + ROWS, 3)] = side
    for at, start in ((0, 10), (1, 0)):
        for r in range(2):
            for h in range(2):
                cots[at, pl.ds((r * 2 + h) * 2, 2)] = cot[start + r, :, h * 128 : (h + 1) * 128].reshape(2, 16, 128)
    for copy in copies:
        copy.wait()


def sides(inputs, cot):
    return pl.pallas_call(
        side_kernel,
        out_shape=[jax.ShapeDtypeStruct((ROWS + 4, 16, 128), BF16)] * 2 + [jax.ShapeDtypeStruct((2, 8, 16, 128), BF16)],
        in_specs=[any_spec(), vmem_spec()],
        out_specs=[vmem_spec()] * 3,
        scratch_shapes=[pltpu.VMEM((48, 128), F32), pltpu.SemaphoreType.DMA((2,))],
        compiler_params=pltpu.CompilerParams(vmem_limit_bytes=8 * MIB),
        name="pack_columns",
    )(inputs, cot)


def rim_kernel(inputs, cots, one, two, _, off, near, sems):
    core = lax.axis_index("core")
    copies = []

    def fetch(source, target):
        copy = pltpu.make_async_copy(source, target, sems.at[len(copies)])
        copy.start()
        copies.append(copy)

    body = pl.ds(0, HALO)
    for target, low in ((off, core), (near, 1 - core)):
        row = (ROWS - HALO) * low
        fetch(inputs.at[pl.ds(row, HALO)], target.at[body, pl.ds(0, 8)])
        fetch(cots.at[1 - low], target.at[HALO, pl.ds(0, 8)])
        for unit, side in ((8, one), (9, two)):
            fetch(side.at[pl.ds(1 + row, HALO)], target.at[body, unit])
            fetch(side.at[(3 + ROWS) * low], target.at[HALO, unit])
    for copy in copies:
        copy.wait()


def rims(*args):
    return pl.pallas_call(
        rim_kernel,
        out_shape=[jax.ShapeDtypeStruct((HALO + 1, 10, 16, 128), BF16)] * 2,
        in_specs=[any_spec()] * len(args),
        out_specs=[vmem_spec()] * 2,
        scratch_shapes=[pltpu.SemaphoreType.DMA((12,))],
        compiler_params=pltpu.CompilerParams(vmem_limit_bytes=8 * MIB),
        name="pack_rows",
    )(*args)


def weight_forms(w1, w2, w3, w1t, w1b, w2t, w2b, w3b):
    zero = jnp.zeros((128, 128), BF16)
    for source, ahead, back in ((w1, w1t, w1b), (w2, w2t, w2b)):
        for u in range(3):
            for v in range(3):
                tap = source[pl.ds((3 * u + v) * 128, 128), :]
                for i in range(2):
                    side = slice(i * 128, (i + 1) * 128)
                    ahead[pl.ds((4 * u + v + i) * 128, 128), side] = tap
                    at = (4 * (2 - u) + 2 - v + i) * 128
                    back[side, at : at + 128] = tap
            for i, j in ((0, 3), (1, 0)):
                at = (4 * u + j) * 128
                side = slice(i * 128, (i + 1) * 128)
                ahead[pl.ds(at, 128), side] = zero
                back[side, at : at + 128] = zero
    for u in range(3):
        for v in range(3):
            at = (3 * (2 - u) + 2 - v) * 256
            w3b[:, at : at + 256] = w3[pl.ds((3 * u + v) * 128, 128), :]


def wave_tables(grid_rows, grid_cols, anchor, frequency, rows_sc, cols_sc):
    own_row, own_col = own_place()
    row = lax.broadcasted_iota(jnp.int32, (PAD_ROWS, 128), 0) - HALO + own_row * ROWS
    angle = (row + anchor[0]).astype(F32) * frequency[0:1, :]
    keep = jnp.where((row >= 0) & (row < grid_rows), 1.0, 0.0)
    rows_sc[0] = jnp.sin(angle) * keep
    rows_sc[1] = jnp.cos(angle) * keep
    for p in range(4):
        k = lax.broadcasted_iota(jnp.int32, (KP, 128), 0)
        col = 4 * jnp.where(k < KO + 4, k, k - KP) + p + own_col * (4 * KO)
        angle = (col + anchor[1]).astype(F32) * frequency[1:2, :]
        keep = jnp.where((col >= 0) & (col < grid_cols), 1.0, 0.0)
        cols_sc[0, p] = jnp.sin(angle) * keep
        cols_sc[1, p] = jnp.cos(angle) * keep


def prep_kernel(grid_rows, grid_cols, anchor, w1, w2, w3, frequency, w1t, w1b, w2t, w2b, w3b, rows_sc, cols_sc):
    weight_forms(w1, w2, w3, w1t, w1b, w2t, w2b, w3b)
    wave_tables(grid_rows, grid_cols, anchor, frequency, rows_sc, cols_sc)


def prep(grid_rows, grid_cols, anchor, w1, w2, w3, frequency):
    def kernel(*refs):
        prep_kernel(grid_rows, grid_cols, *refs)

    shape = jax.ShapeDtypeStruct
    return pl.pallas_call(
        kernel,
        out_shape=[
            shape((1536, 256), BF16),
            shape((256, 1536), BF16),
            shape((1536, 256), BF16),
            shape((256, 1536), BF16),
            shape((128, 2304), BF16),
            shape((2, PAD_ROWS, 128), F32),
            shape((2, 4, KP, 128), F32),
        ],
        in_specs=[smem_spec()] + [vmem_spec()] * 4,
        out_specs=[vmem_spec()] * 7,
        compiler_params=pltpu.CompilerParams(vmem_limit_bytes=12 * MIB),
        name="weight_forms",
    )(anchor, w1, w2, w3, frequency)


def fill_mask(low_rows, low_cols, mask):
    own_row, own_col = own_place()
    k = lax.broadcasted_iota(jnp.int32, (KP, 128), 0)
    col = jnp.where(k < KO + 4, k, k - KP) + own_col * KO
    inside = jnp.where((col >= 0) & (col < low_cols), 1.0, 0.0)

    def step(at, _):
        row = at - 4 + own_row * 12
        mask[at] = inside * jnp.where((row >= 0) & (row < low_rows), 1.0, 0.0)
        return 0

    lax.fori_loop(0, LOWS, step, 0)


def widened(line):
    rest = jnp.zeros((KW - KP, line.shape[1]), F32)
    return jnp.concatenate([line, rest], axis=0).astype(BF16)


def put_line(ref, row, planes):
    width = planes[0].shape[1]
    for n, plane in enumerate(planes):
        ref[row, :, n * width : (n + 1) * width] = widened(plane)


def before(line):
    return pltpu.roll(line, 1, 0)


def after(line):
    return pltpu.roll(line, KP - 1, 0)


def silu_parts(half):
    th = jnp.tanh(half)
    act = half + half * th
    return act, (1.0 + act) + th * (1.0 - act)


def rounded(value):
    return value.astype(BF16).astype(F32)


def flat(block):
    return block.reshape(128, 128)


def modulation(noise, noise_index):
    modulate = noise[pl.ds(noise_index[0], 1), :]
    return 1.0 + modulate[:, 0:128], modulate[:, 128:256]


def first_lines(load, base, at, tables, stage, x1):
    rows_sc, cols_sc = tables
    for i in range(4):
        own, right, left = load(i)
        stage[i, 0:128] = own.astype(F32)
        stage[i, 128:144] = right.astype(F32)
        stage[i, 144:160] = left.astype(F32)
        sin_row = rows_sc[0, pl.ds(base + i, 1), :]
        cos_row = rows_sc[1, pl.ds(base + i, 1), :]
        planes = []
        for p in range(4):
            value = stage[i, pl.ds(p, KP, stride=4), :]
            planes.append(value + (sin_row * cols_sc[1, p] + cos_row * cols_sc[0, p]))
        put_line(x1, at + i, [before(planes[3])] + planes + [after(planes[0])])


def around(ref, at, count, lanes, cols=KW):
    parts = [ref[pl.ds(at - 1 + u, count), 0:cols, lanes] for u in range(3)]
    return jnp.concatenate([part.reshape(count * cols, part.shape[-1]) for part in parts], axis=1)


def product(left, right):
    return jnp.dot(left, right, preferred_element_type=F32)


def product_turned(left, right):
    return lax.dot_general(left, right, (((1,), (1,)), ((), ())), preferred_element_type=F32)


def weight_terms(grad, field):
    return lax.dot_general(grad, field, (((0,), (0,)), ((), ())), preferred_element_type=F32)


def pipeline(steps, dot, post, z0, z1):
    z = (z0, z1)
    for t in range(steps + 1):
        if t < steps:
            total = dot(t)
            z[t % 2][0 : total.shape[0], 0 : total.shape[1]] = total
        if t > 0:
            post(t - 1, z[(t - 1) % 2])


def conv_one_dot(x1, row, w1t):
    one = around(x1, row, 4, slice(0, 512))
    two = around(x1, row, 4, slice(256, 768))
    return product(jnp.concatenate([one, two], axis=0), w1t[...])


def conv_one_post(z, scale, shift, keeps, d1, d1_row, x2, x2_row):
    half_scale, half_shift = 0.5 * scale, 0.5 * shift
    slope_scale = half_scale.astype(BF16)
    for s in range(2):
        halves = []
        for q in range(2):
            sums = []
            for p in (2 * q, 2 * q + 1):
                lanes = slice((p % 2) * 128, (p % 2 + 1) * 128)
                acts = []
                for r in range(2):
                    at = q * 4 * KW + (2 * s + r) * KW
                    act, slope = silu_parts((z[at : at + KW, lanes] * half_scale + half_shift).astype(BF16))
                    d1[d1_row + 2 * s + r, :, p * 128 : (p + 1) * 128] = slope_scale * slope
                    acts.append(act)
                sums.append((acts[0] + acts[1]).astype(F32))
            halves.append((sums[0] + sums[1])[:KP] * (0.25 * keeps[s]))
        put_line(x2, x2_row + s, [before(halves[1]), halves[0], halves[1], after(halves[0])])


def conv_two_post(z, at, keep, x2, d2, row, x3, low):
    total = None
    for q in range(2):
        lanes = slice(q * 128, (q + 1) * 128)
        for r in range(2):
            start = at + r * KW
            act, slope = silu_parts(0.5 * z[start : start + KP, lanes])
            d2[row + r, :, lanes] = 0.5 * slope
            down = x2[row + r, :, (q + 1) * 128 : (q + 2) * 128].astype(F32)[:KP]
            act = rounded(down + act)
            total = act if total is None else total + act
    line = total * (0.25 * keep)
    put_line(x3, low, [before(line), line, after(line)])


def own_kernel(
    grid_rows, grid_cols,
    noise_index, rows_sc, cols_sc, noise, inputs, w1t, w2t, one, two,
    x1_out, d1_out, x2_out, x3_out, d2_out,
    x1, stage, d1, x2, mask, side, z0, z1, x3, d2, sems,
):
    odd = odd_column()
    halos = [
        pltpu.make_async_copy(one, side.at[1 - odd], sems.at[0]),
        pltpu.make_async_copy(two, side.at[odd], sems.at[1]),
    ]
    for copy in halos:
        copy.start()
    fill_mask(grid_rows // 4, grid_cols // 4, mask)
    scale, shift = modulation(noise, noise_index)
    for copy in halos:
        copy.wait()

    def first(q):
        def load(i):
            row = 4 * q + i
            return flat(inputs[row]), side[1, 1 + row], side[0, 1 + row]

        first_lines(load, HALO + 4 * q, 4 * q, (rows_sc, cols_sc), stage, x1)

    def dot(t):
        return conv_one_dot(x1, 4 * t + 2, w1t)

    def post(t, z):
        keeps = [mask[(9 + 2 * t) // 2], mask[(10 + 2 * t) // 2]]
        conv_one_post(z, scale, shift, keeps, d1, 4 * t, x2, 2 * t)

    first(0)
    first(1)
    z = (z0, z1)
    for t in range(11):
        z[t % 2][0 : 8 * KW, :] = dot(t)
        if t + 2 < 12:
            first(t + 2)
        if t > 0:
            post(t - 1, z[(t - 1) % 2])
        if t == 9:
            put_x1 = pltpu.make_async_copy(x1, x1_out, sems.at[2])
            put_x1.start()
    post(10, z0)
    put_d1 = pltpu.make_async_copy(d1, d1_out, sems.at[3])
    put_x2 = pltpu.make_async_copy(x2, x2_out, sems.at[4])
    put_d1.start()
    put_x2.start()

    def conv_two_dot(t):
        return product(around(x2, 1 + 10 * t, 10, slice(0, 512)), w2t[...])

    def conv_two_steps(t, z):
        for n in range(5):
            low = 5 * t + n
            conv_two_post(z, 2 * n * KW, mask[5 + low], x2_own, d2, 2 * low, x3, low)

    x2_own = x2.at[pl.ds(1, 20)]
    pipeline(2, conv_two_dot, conv_two_steps, z0, z1)
    put_x3 = pltpu.make_async_copy(x3, x3_out, sems.at[5])
    put_d2 = pltpu.make_async_copy(d2, d2_out, sems.at[6])
    put_x3.start()
    put_d2.start()
    put_x3.wait()
    put_d2.wait()
    put_x1.wait()
    put_d1.wait()
    put_x2.wait()


def own_rows(grid_rows, grid_cols, *args):
    def kernel(*refs):
        own_kernel(grid_rows, grid_cols, *refs)

    vm = pltpu.VMEM
    shape = jax.ShapeDtypeStruct
    return pl.pallas_call(
        kernel,
        out_shape=[
            shape((48, KW, 768), BF16),
            shape((44, KW, 512), BF16),
            shape((22, KW, 512), BF16),
            shape((10, KW, 384), BF16),
            shape((20, KP, 256), F32),
        ],
        in_specs=[smem_spec()] + [vmem_spec()] * 6 + [any_spec()] * 2,
        out_specs=[any_spec()] * 5,
        scratch_shapes=[
            vm((48, KW, 768), BF16),
            vm((4, 160, 128), F32),
            vm((44, KW, 512), BF16),
            vm((22, KW, 512), BF16),
            vm((LOWS, KP, 128), F32),
            vm((2, ROWS + 4, 16, 128), BF16),
            vm((10 * KW, 256), F32),
            vm((10 * KW, 256), F32),
            vm((10, KW, 384), BF16),
            vm((20, KP, 256), F32),
            pltpu.SemaphoreType.DMA((7,)),
        ],
        compiler_params=pltpu.CompilerParams(vmem_limit_bytes=20 * MIB),
        cost_estimate=pl.CostEstimate(flops=4 * 10**9, bytes_accessed=30 * 10**6, transcendentals=0),
        name="own_rows",
    )(*args)


def lines_kernel(
    grid_rows, grid_cols,
    noise_index, rows_sc, cols_sc, noise,
    cot, w1t, w2t, w2b, w3, w3b, off, near, one, two, x1_in, d1_in, x2_in, x3_in, d2_in,
    coarse_out, g1_out, keep_out, give_out,
    rim, stage, x1, d1, x2, d2, x3, cp, side, side32, g3, xb2, g2, g1, coarse,
    acc, acc3, gw, msg, mask, z0, z1, sems,
):
    core = lax.axis_index("core")
    odd = odd_column()

    def fetch(source, target, at):
        copy = pltpu.make_async_copy(source, target, sems.at[at])
        copy.start()
        return copy

    got_rims = [fetch(off, rim.at[core], 0), fetch(near, rim.at[1 - core], 1)]
    got_edges = [
        fetch(x1_in.at[pl.ds(0, 4)], x1.at[pl.ds(16, 4)], 2),
        fetch(x1_in.at[pl.ds(44, 4)], x1.at[pl.ds(60, 4)], 3),
    ]
    got_x2 = fetch(x2_in, x2.at[pl.ds(9, 22)], 4)
    units = pl.ds(ROWS + 1, 3)
    got_sides = [fetch(one.at[units], side.at[1 - odd], 5), fetch(two.at[units], side.at[odd], 6)]
    got_low = [fetch(x3_in, x3.at[pl.ds(5, 10)], 7), fetch(d2_in, d2.at[pl.ds(10, 20)], 10)]
    got_d1 = fetch(d1_in, d1.at[pl.ds(18, 44)], 8)
    got_x1 = fetch(x1_in.at[pl.ds(4, 40)], x1.at[pl.ds(20, 40)], 9)
    fill_mask(grid_rows // 4, grid_cols // 4, mask)
    gw[:, 0:8, :] = jnp.zeros((4, 8, 128), F32)
    gw[:, 1160:1168, :] = jnp.zeros((4, 8, 128), F32)
    scale, shift = modulation(noise, noise_index)
    for copy in got_rims:
        copy.wait()

    def first(n):
        below, start = n // 4, 4 * (n % 4)
        base = start + (HALO + ROWS) * below

        def load(i):
            row = start + i
            return flat(rim[below, row, 0:8]), rim[below, row, 8 + odd], rim[below, row, 9 - odd]

        first_lines(load, base, base, (rows_sc, cols_sc), stage, x1)

    def mid_of(t):
        return 1 + 2 * t if t < 4 else 23 + 2 * t

    def dot(t):
        return conv_one_dot(x1, 2 * mid_of(t), w1t)

    def post(t, z):
        m = mid_of(t)
        conv_one_post(z, scale, shift, [mask[m // 2], mask[(m + 1) // 2]], d1, 2 * m, x2, m)

    first(0)
    first(1)
    for copy in got_edges:
        copy.wait()
    z = (z0, z1)
    for t in range(8):
        z[t % 2][0 : 8 * KW, :] = dot(t)
        if t + 2 < 8:
            first(t + 2)
        if t > 0:
            post(t - 1, z[(t - 1) % 2])
    post(7, z1)
    got_x2.wait()

    def conv_two_dot(t):
        return product(around(x2, 2 + 28 * t, 8, slice(0, 512)), w2t[...])

    def conv_two_steps(t, z):
        for n in range(4):
            low = 1 + 14 * t + n
            conv_two_post(z, 2 * n * KW, mask[low], x2, d2, 2 * low, x3, low)

    pipeline(2, conv_two_dot, conv_two_steps, z0, z1)
    for copy in got_low:
        copy.wait()

    cp[...] = jnp.zeros_like(cp)
    for copy in got_sides:
        copy.wait()
    for h in range(2):
        lanes = slice(h * 128, (h + 1) * 128)
        for r in range(2):
            units = pl.ds((r * 2 + h) * 2, 2)
            cp[r, 0:KO, lanes] = rim[0, HALO, units].reshape(KO, 128).astype(F32)
            cp[14 + r, 0:KO, lanes] = rim[1, HALO, units].reshape(KO, 128).astype(F32)
    for r in range(12):
        cp[2 + r, 0:KO, :] = cot[r].astype(F32)
    for which, at in ((1, KO), (0, KP - 2)):
        side32[...] = side[which].reshape(48, 128).astype(F32)
        for h in range(2):
            for r in range(12):
                cp[2 + r, at : at + 2, h * 128 : (h + 1) * 128] = side32[r * 4 + h * 2 : r * 4 + h * 2 + 2]
    for below, skip, row in ((0, 8, 0), (1, 0, 14)):
        for unit, at in ((9 - odd, KP - 2), (8 + odd, KO)):
            side32[0:16] = rim[below, HALO, unit].astype(F32)
            for h in range(2):
                for r in range(2):
                    start = skip + r * 4 + h * 2
                    cp[row + r, at : at + 2, h * 128 : (h + 1) * 128] = side32[start : start + 2]
    g3[1] = jnp.zeros((KW, 768), BF16)
    g3[18] = jnp.zeros((KW, 768), BF16)

    def conv_three_post(t, z):
        for i in range(8):
            row = 2 + 8 * t + i
            act, slope = silu_parts(0.5 * z[i * KW : i * KW + KP, :])
            keep = 0.5 * mask[row]
            line = cp[row - 2] * slope * jnp.concatenate([keep, keep], axis=1)
            put_line(g3, row, [before(line), line, after(line)])
            coarse[row - 2] = act[:KO].astype(BF16)

    pipeline(2, lambda t: product(around(x3, 2 + 8 * t, 8, slice(0, 384)), w3[...]), conv_three_post, z0, z1)
    put_coarse = fetch(coarse.at[pl.ds(2, 12)], coarse_out, 0)

    def back_three_post(t, z):
        for i in range(8):
            low = 2 + 8 * t + i
            line = 0.25 * z[i * KW : i * KW + KP, 0:128]
            xb2[low] = line
            line = line * mask[low]
            for r in range(2):
                row = 2 * low + r
                zero, one = (line * d2[row, :, q * 128 : (q + 1) * 128] for q in range(2))
                put_line(g2, row, [before(one), zero, one, after(zero)])

    def back_three_dot(t):
        return product_turned(around(g3, 2 + 8 * t, 8, slice(0, 768)), w3b[...])

    pipeline(2, back_three_dot, back_three_post, z0, z1)
    acc3[...] = weight_terms(
        g3[4:16, 0:KO, 256:512].reshape(12 * KO, 256), around(x3, 4, 12, slice(0, 384), KO)
    )
    acc[...] = weight_terms(
        g2[8:32, 0:KO, 128:384].reshape(24 * KO, 256), around(x2, 8, 24, slice(0, 512), KO)
    )
    got_d1.wait()

    def back_two_post(t, z):
        for i in range(7):
            m = 6 + 7 * t + i
            low = m // 2
            keep = 0.25 * mask[low]
            base = xb2[low]
            both = [(base + z[i * KW : i * KW + KP, q * 128 : (q + 1) * 128]) * keep for q in range(2)]
            for r in range(2):
                row = 2 * m + r
                slopes = [d1[row, :, p * 128 : (p + 1) * 128].astype(F32)[:KP] for p in range(4)]
                planes = [both[p // 2] * slopes[p] for p in range(4)]
                for n, line in enumerate([before(planes[3])] + planes + [after(planes[0])]):
                    g1[row - 12, :, n * 128 : (n + 1) * 128] = line[:KO].astype(BF16)

    pipeline(
        4, lambda t: product_turned(around(g2, 6 + 7 * t, 7, slice(0, 512)), w2b[...]), back_two_post, z0, z1
    )
    put_g1 = fetch(g1.at[pl.ds(3, 50)], g1_out, 1)
    got_x1.wait()

    def fold_weights(at):
        for u in range(3):
            for v in range(3):
                left = (4 * u + v) * 128
                term = acc[0:128, left : left + 128] + acc[128:256, left + 128 : left + 256]
                gw[at, pl.ds(8 + (3 * u + v) * 128, 128), :] = term.T

    def one_chunk(t):
        grads = jnp.concatenate(
            [g1[4 + 16 * t : 20 + 16 * t, :, lanes].reshape(512, 256) for lanes in (slice(128, 384), slice(384, 640))],
            axis=0,
        )
        fields = jnp.concatenate(
            [around(x1, 16 + 16 * t, 16, lanes, KO) for lanes in (slice(0, 512), slice(256, 768))], axis=0
        )
        return weight_terms(grads, fields)

    fold_weights(1)
    acc[...] = one_chunk(0)
    for tap in range(9):
        turned = acc3[:, tap * 128 : (tap + 1) * 128].T
        gw[2, pl.ds(8 + tap * 128, 128), :] = turned[:, 0:128]
        gw[3, pl.ds(8 + tap * 128, 128), :] = turned[:, 128:256]
    acc[...] += one_chunk(1)
    acc[...] += one_chunk(2)
    fold_weights(0)
    line = lax.broadcasted_iota(jnp.int32, (8, 128), 0)
    none = jnp.zeros((8, 128), F32)
    for owner in range(128):
        at = 8 + 9 * owner
        parts = [gw[0, at : at + 8, :]]
        for t in range(1, 5):
            rest = gw[t - 1, at + 9 - t : at + 17 - t, :]
            start = gw[t, at - t : at + 8 - t, :] if t < 4 else none
            parts.append(jnp.where(line < t, rest, start))
        row, col = divmod(owner, 8)
        msg[row % 2, (row // 2) * 8 + col] = jnp.concatenate(parts, axis=0).astype(BF16)
    put_keep = fetch(msg.at[core], keep_out, 2)
    put_give = fetch(msg.at[1 - core], give_out, 3)
    put_keep.wait()
    put_give.wait()
    put_coarse.wait()
    put_g1.wait()


def levels(grid_rows, grid_cols, *args):
    def kernel(*refs):
        lines_kernel(grid_rows, grid_cols, *refs)

    vm = pltpu.VMEM
    return pl.pallas_call(
        kernel,
        out_shape=[
            jax.ShapeDtypeStruct((12, KO, 256), BF16),
            jax.ShapeDtypeStruct((50, KO, 768), BF16),
            jax.ShapeDtypeStruct((64, 40, 128), BF16),
            jax.ShapeDtypeStruct((64, 40, 128), BF16),
        ],
        in_specs=[smem_spec()] + [vmem_spec()] * 9 + [any_spec()] * 9,
        out_specs=[any_spec()] * 4,
        scratch_shapes=[
            vm((2, HALO + 1, 10, 16, 128), BF16),
            vm((4, 160, 128), F32),
            vm((PAD_ROWS, KW, 768), BF16),
            vm((PAD_ROWS, KW, 512), BF16),
            vm((PAIRS, KW, 512), BF16),
            vm((PAIRS, KP, 256), F32),
            vm((LOWS, KW, 384), BF16),
            vm((16, KP, 256), F32),
            vm((2, 3, 16, 128), BF16),
            vm((48, 128), F32),
            vm((LOWS, KW, 768), BF16),
            vm((LOWS, KP, 128), F32),
            vm((PAIRS, KW, 512), BF16),
            vm((56, KO, 768), BF16),
            vm((16, KO, 256), BF16),
            vm((256, 1536), F32),
            vm((256, 1152), F32),
            vm((4, 1168, 128), F32),
            vm((2, 64, 40, 128), BF16),
            vm((LOWS, KP, 128), F32),
            vm((8 * KW, 256), F32),
            vm((8 * KW, 256), F32),
            pltpu.SemaphoreType.DMA((11,)),
        ],
        compiler_params=pltpu.CompilerParams(vmem_limit_bytes=36 * MIB),
        name="encoder_levels",
    )(*args)


def input_kernel(g1, g1_next, w1b, out, stage):
    for t in range(2):
        halves = []
        for lanes in (slice(0, 512), slice(256, 768)):
            rows = jnp.concatenate([g1[:, :, lanes], g1_next[:, :, lanes]], axis=0)
            parts = [rows[4 * t + u : 4 * t + u + 4].reshape(128, 512) for u in range(3)]
            halves.append(jnp.concatenate(parts, axis=1))
        total = product_turned(jnp.concatenate(halves, axis=0), w1b[...])
        for r in range(4):
            for p in range(4):
                rows = (p // 2) * 128 + r * 32
                value = total[rows : rows + 32, (p % 2) * 128 : (p % 2 + 1) * 128]
                stage[4 * t + r, pl.ds(p, 32, stride=4), :] = value
            out[4 * t + r] = stage[4 * t + r].astype(BF16)


def input_grad(g1, w1b):
    return pl.pallas_call(
        input_kernel,
        grid=(6,),
        out_shape=jax.ShapeDtypeStruct((ROWS, 128, 128), BF16),
        in_specs=[
            pl.BlockSpec((8, KO, 768), lambda i: (i, 0, 0)),
            pl.BlockSpec((2, KO, 768), lambda i: (4 * i + 4, 0, 0)),
            pl.BlockSpec((256, 1536), lambda i: (0, 0)),
        ],
        out_specs=pl.BlockSpec((8, 128, 128), lambda i: (i, 0, 0)),
        scratch_shapes=[pltpu.VMEM((8, 128, 128), F32)],
        compiler_params=pltpu.CompilerParams(vmem_limit_bytes=16 * MIB),
        cost_estimate=pl.CostEstimate(flops=2 * 6144 * 1152 * 128, bytes_accessed=8 * 1024 * 1024, transcendentals=0),
        name="input_grad",
    )(g1, g1, w1b)


def collect_kernel(got, one, two, three, held, total, sems):
    copies = []
    for n in range(4):
        part = pl.ds(16 * n, 16)
        copies.append(pltpu.make_async_copy(got.at[part], held.at[part], sems.at[n]))
        copies[n].start()
    sums = None
    for n, copy in enumerate(copies):
        copy.wait()
        for i in range(16):
            term = held[16 * n + i].astype(F32)
            sums = term if sums is None else sums + term
    total[...] = sums
    one[...] = total[0:9, :]
    two[...] = total[9:18, :]
    three[:, 0:128] = total[18:27, :]
    three[:, 128:256] = total[27:36, :]


def collect(got):
    shape = jax.ShapeDtypeStruct
    return pl.pallas_call(
        collect_kernel,
        out_shape=[shape((9, 128), F32), shape((9, 128), F32), shape((9, 256), F32)],
        in_specs=[any_spec()],
        out_specs=[vmem_spec()] * 3,
        scratch_shapes=[
            pltpu.VMEM((64, 40, 128), BF16),
            pltpu.VMEM((40, 128), F32),
            pltpu.SemaphoreType.DMA((4,)),
        ],
        compiler_params=pltpu.CompilerParams(vmem_limit_bytes=8 * MIB),
        name="collect_weights",
    )(got)


def swapped(block, axis, odd_first):
    devices = lax.axis_size(axis)
    pairs = []
    for i in range(1 if odd_first else 0, devices - 1, 2):
        pairs += [(i, i + 1), (i + 1, i)]
    return lax.ppermute(block, axis, pairs)


def body(inputs, weight_one, weight_two, weight_three, noise_table, frequency, anchor, noise_index, cotangent):
    grid = (lax.axis_size(ROW_AXES) * ROWS, lax.axis_size("tx") * 4 * KO)
    inputs = inputs.reshape(ROWS, 8, 16, 128)
    one, two, cots = sides(inputs, cotangent)
    two = swapped(two, "tx", True)
    one = swapped(one, "tx", False)
    w1t, w1b, w2t, w2b, w3b, rows_sc, cols_sc = prep(*grid, anchor, weight_one, weight_two, weight_three, frequency)
    off, near = rims(inputs, cots, one, two, rows_sc)
    off = swapped(off, ROW_AXES, True)
    near = lax.ppermute(near, "core", [(0, 1), (1, 0)])
    x1, d1, x2, x3, d2 = own_rows(
        *grid, noise_index, rows_sc, cols_sc, noise_table, inputs, w1t, w2t, one, two
    )
    coarse, g1, keep_msg, give_msg = levels(
        *grid, noise_index, rows_sc, cols_sc, noise_table,
        cotangent, w1t, w2t, w2b, weight_three, w3b, off, near, one, two, x1, d1, x2, x3, d2,
    )
    other = lax.ppermute(give_msg, "core", [(0, 1), (1, 0)])
    msg = (keep_msg.astype(F32) + other.astype(F32)).astype(BF16)
    got = lax.all_to_all(msg, ("chip", "tx"), 0, 0, tiled=True)
    grad_inputs = input_grad(g1, w1b)
    return (coarse, grad_inputs, *collect(got))


def solution(mesh):
    halves = jax.sharding.Mesh(mesh.devices.reshape(-1, 2, mesh.devices.shape[1]), ("chip", "core", "tx"))
    placed = (P(ROW_AXES, "tx", None), P(), P(), P(), P(), P(), P(), P(), P(ROW_AXES, "tx", None))
    return jax.shard_map(
        body,
        mesh=halves,
        in_specs=placed,
        out_specs=(
            P(ROW_AXES, "tx", None),
            P(ROW_AXES, "tx", None),
            P((*ROW_AXES, "tx"), None),
            P((*ROW_AXES, "tx"), None),
            P((*ROW_AXES, "tx"), None),
        ),
        check_vma=False,
    )
```

```python
import jax
import jax.numpy as jnp
from jax import lax
from jax.experimental import pallas as pl
from jax.experimental.pallas import tpu as pltpu
from jax.sharding import PartitionSpec as P

BF16 = jnp.bfloat16
F32 = jnp.float32

KO = 32
KP = 40
KW = 48
HALO = 16
SENT = 15
ROWS = 48
PAD_ROWS = ROWS + 2 * HALO
PAIRS = PAD_ROWS // 2
LOWS = PAIRS // 2
MIB = 1024 * 1024


def any_spec():
    return pl.BlockSpec(memory_space=pl.ANY)


def vmem_spec():
    return pl.BlockSpec(memory_space=pltpu.VMEM)


def smem_spec():
    return pl.BlockSpec(memory_space=pltpu.SMEM)


ROW_AXES = ("chip", "core")


def own_place():
    return lax.axis_index(ROW_AXES), lax.axis_index("tx")


def odd_column():
    return lax.rem(lax.axis_index("tx"), 2)


def side_kernel(inputs, cot, one, two, cots, side32, sems):
    odd = odd_column()
    copies = [
        pltpu.make_async_copy(inputs.at[:, 7 - 7 * odd], one.at[pl.ds(1, ROWS)], sems.at[0]),
        pltpu.make_async_copy(inputs.at[:, 7 * odd], two.at[pl.ds(1, ROWS)], sems.at[1]),
    ]
    for copy in copies:
        copy.start()
    for target, at_left in ((one, odd == 1), (two, odd == 0)):
        for r in range(12):
            line = cot[r].astype(F32)
            for h in range(2):
                lanes = slice(h * 128, (h + 1) * 128)
                side32[pl.ds(r * 4 + h * 2, 2)] = jnp.where(at_left, line[0:2, lanes], line[30:32, lanes])
        side = side32[...].astype(BF16).reshape(3, 16, 128)
        target[pl.ds(0, 1)] = side[0:1]
        target[pl.ds(1 + ROWS, 3)] = side
    for at, start in ((0, 10), (1, 0)):
        for r in range(2):
            for h in range(2):
                cots[at, pl.ds((r * 2 + h) * 2, 2)] = cot[start + r, :, h * 128 : (h + 1) * 128].reshape(2, 16, 128)
    for copy in copies:
        copy.wait()


def sides(inputs, cot):
    return pl.pallas_call(
        side_kernel,
        out_shape=[jax.ShapeDtypeStruct((ROWS + 4, 16, 128), BF16)] * 2 + [jax.ShapeDtypeStruct((2, 8, 16, 128), BF16)],
        in_specs=[any_spec(), vmem_spec()],
        out_specs=[vmem_spec()] * 3,
        scratch_shapes=[pltpu.VMEM((48, 128), F32), pltpu.SemaphoreType.DMA((2,))],
        compiler_params=pltpu.CompilerParams(vmem_limit_bytes=8 * MIB),
        name="pack_columns",
    )(inputs, cot)


def rim_kernel(inputs, cots, two, one, _, off, near, sems):
    core = lax.axis_index("core")
    copies = []

    def fetch(source, target):
        copy = pltpu.make_async_copy(source, target, sems.at[len(copies)])
        copy.start()
        copies.append(copy)

    body = pl.ds(0, SENT)
    for target, low in ((off, core), (near, 1 - core)):
        row = (ROWS - SENT) * low
        fetch(inputs.at[pl.ds(row, SENT)], target.at[body, pl.ds(0, 8)])
        fetch(cots.at[1 - low], target.at[SENT, pl.ds(0, 8)])
        for unit, side in ((8, one), (9, two)):
            fetch(side.at[pl.ds(1 + row, SENT)], target.at[body, unit])
            fetch(side.at[(3 + ROWS) * low], target.at[SENT, unit])
    for copy in copies:
        copy.wait()


def rims(*args):
    return pl.pallas_call(
        rim_kernel,
        out_shape=[jax.ShapeDtypeStruct((SENT + 1, 10, 16, 128), BF16)] * 2,
        in_specs=[any_spec()] * len(args),
        out_specs=[vmem_spec()] * 2,
        scratch_shapes=[pltpu.SemaphoreType.DMA((12,))],
        compiler_params=pltpu.CompilerParams(vmem_limit_bytes=8 * MIB),
        name="pack_rows",
    )(*args)


def weight_forms(w1, w2, w3, w1t, w1b, w2t, w2b, w3b):
    zero = jnp.zeros((128, 128), BF16)
    for source, ahead, back in ((w1, w1t, w1b), (w2, w2t, w2b)):
        for u in range(3):
            for v in range(3):
                tap = source[pl.ds((3 * u + v) * 128, 128), :]
                for i in range(2):
                    side = slice(i * 128, (i + 1) * 128)
                    ahead[pl.ds((4 * u + v + i) * 128, 128), side] = tap
                    at = (4 * (2 - u) + 2 - v + i) * 128
                    back[side, at : at + 128] = tap
            for i, j in ((0, 3), (1, 0)):
                at = (4 * u + j) * 128
                side = slice(i * 128, (i + 1) * 128)
                ahead[pl.ds(at, 128), side] = zero
                back[side, at : at + 128] = zero
    for u in range(3):
        for v in range(3):
            at = (3 * (2 - u) + 2 - v) * 256
            w3b[:, at : at + 256] = w3[pl.ds((3 * u + v) * 128, 128), :]


def wave_tables(grid_rows, grid_cols, anchor, frequency, rows_sc, cols_sc):
    own_row, own_col = own_place()
    row = lax.broadcasted_iota(jnp.int32, (PAD_ROWS, 128), 0) - HALO + own_row * ROWS
    angle = (row + anchor[0]).astype(F32) * frequency[0:1, :]
    keep = jnp.where((row >= 0) & (row < grid_rows), 1.0, 0.0)
    rows_sc[0] = jnp.sin(angle) * keep
    rows_sc[1] = jnp.cos(angle) * keep
    for p in range(4):
        k = lax.broadcasted_iota(jnp.int32, (KP, 128), 0)
        col = 4 * jnp.where(k < KO + 4, k, k - KP) + p + own_col * (4 * KO)
        angle = (col + anchor[1]).astype(F32) * frequency[1:2, :]
        keep = jnp.where((col >= 0) & (col < grid_cols), 1.0, 0.0)
        cols_sc[0, p] = jnp.sin(angle) * keep
        cols_sc[1, p] = jnp.cos(angle) * keep


def prep_kernel(grid_rows, grid_cols, anchor, w1, w2, w3, frequency, w1t, w1b, w2t, w2b, w3b, rows_sc, cols_sc):
    weight_forms(w1, w2, w3, w1t, w1b, w2t, w2b, w3b)
    wave_tables(grid_rows, grid_cols, anchor, frequency, rows_sc, cols_sc)


def prep(grid_rows, grid_cols, anchor, w1, w2, w3, frequency):
    def kernel(*refs):
        prep_kernel(grid_rows, grid_cols, *refs)

    shape = jax.ShapeDtypeStruct
    return pl.pallas_call(
        kernel,
        out_shape=[
            shape((1536, 256), BF16),
            shape((256, 1536), BF16),
            shape((1536, 256), BF16),
            shape((256, 1536), BF16),
            shape((128, 2304), BF16),
            shape((2, PAD_ROWS, 128), F32),
            shape((2, 4, KP, 128), F32),
        ],
        in_specs=[smem_spec()] + [vmem_spec()] * 4,
        out_specs=[vmem_spec()] * 7,
        compiler_params=pltpu.CompilerParams(vmem_limit_bytes=12 * MIB),
        name="weight_forms",
    )(anchor, w1, w2, w3, frequency)


def fill_mask(low_rows, low_cols, mask):
    own_row, own_col = own_place()
    k = lax.broadcasted_iota(jnp.int32, (KP, 128), 0)
    col = jnp.where(k < KO + 4, k, k - KP) + own_col * KO
    inside = jnp.where((col >= 0) & (col < low_cols), 1.0, 0.0)

    def step(at, _):
        row = at - 4 + own_row * 12
        mask[at] = inside * jnp.where((row >= 0) & (row < low_rows), 1.0, 0.0)
        return 0

    lax.fori_loop(0, LOWS, step, 0)


def widened(line):
    rest = jnp.zeros((KW - KP, line.shape[1]), F32)
    return jnp.concatenate([line, rest], axis=0).astype(BF16)


def put_line(ref, row, planes):
    width = planes[0].shape[1]
    for n, plane in enumerate(planes):
        ref[row, :, n * width : (n + 1) * width] = widened(plane)


def before(line):
    return pltpu.roll(line, 1, 0)


def after(line):
    return pltpu.roll(line, KP - 1, 0)


def silu_parts(half):
    th = jnp.tanh(half)
    act = half + half * th
    return act, (1.0 + act) + th * (1.0 - act)


def rounded(value):
    return value.astype(BF16).astype(F32)


def flat(block):
    return block.reshape(128, 128)


def modulation(noise, noise_index):
    modulate = noise[pl.ds(noise_index[0], 1), :]
    return 1.0 + modulate[:, 0:128], modulate[:, 128:256]


def first_lines(load, base, at, tables, stage, x1):
    rows_sc, cols_sc = tables
    for i in range(4):
        own, right, left = load(i)
        stage[i, 0:128] = own.astype(F32)
        stage[i, 128:144] = right.astype(F32)
        stage[i, 144:160] = left.astype(F32)
        sin_row = rows_sc[0, pl.ds(base + i, 1), :]
        cos_row = rows_sc[1, pl.ds(base + i, 1), :]
        planes = []
        for p in range(4):
            value = stage[i, pl.ds(p, KP, stride=4), :]
            planes.append(value + (sin_row * cols_sc[1, p] + cos_row * cols_sc[0, p]))
        put_line(x1, at + i, [before(planes[3])] + planes + [after(planes[0])])


def around(ref, at, count, lanes, cols=KW):
    parts = [ref[pl.ds(at - 1 + u, count), 0:cols, lanes] for u in range(3)]
    return jnp.concatenate([part.reshape(count * cols, part.shape[-1]) for part in parts], axis=1)


def product(left, right):
    return jnp.dot(left, right, preferred_element_type=F32)


def product_turned(left, right):
    return lax.dot_general(left, right, (((1,), (1,)), ((), ())), preferred_element_type=F32)


def weight_terms(grad, field):
    return lax.dot_general(grad, field, (((0,), (0,)), ((), ())), preferred_element_type=F32)


def pipeline(steps, dot, post, z0, z1):
    z = (z0, z1)
    for t in range(steps + 1):
        if t < steps:
            total = dot(t)
            z[t % 2][0 : total.shape[0], 0 : total.shape[1]] = total
        if t > 0:
            post(t - 1, z[(t - 1) % 2])


def conv_one_dot(x1, row, w1t):
    one = around(x1, row, 4, slice(0, 512))
    two = around(x1, row, 4, slice(256, 768))
    return product(jnp.concatenate([one, two], axis=0), w1t[...])


def conv_one_post(z, scale, shift, keeps, d1, d1_row, x2, x2_row):
    half_scale, half_shift = 0.5 * scale, 0.5 * shift
    slope_scale = half_scale.astype(BF16)
    for s in range(2):
        halves = []
        for q in range(2):
            sums = []
            for p in (2 * q, 2 * q + 1):
                lanes = slice((p % 2) * 128, (p % 2 + 1) * 128)
                acts = []
                for r in range(2):
                    at = q * 4 * KW + (2 * s + r) * KW
                    act, slope = silu_parts((z[at : at + KW, lanes] * half_scale + half_shift).astype(BF16))
                    d1[d1_row + 2 * s + r, :, p * 128 : (p + 1) * 128] = slope_scale * slope
                    acts.append(act)
                sums.append((acts[0] + acts[1]).astype(F32))
            halves.append((sums[0] + sums[1])[:KP] * (0.25 * keeps[s]))
        put_line(x2, x2_row + s, [before(halves[1]), halves[0], halves[1], after(halves[0])])


def conv_two_post(z, at, keep, x2, d2, row, x3, low):
    total = None
    for q in range(2):
        lanes = slice(q * 128, (q + 1) * 128)
        for r in range(2):
            start = at + r * KW
            act, slope = silu_parts(0.5 * z[start : start + KP, lanes])
            d2[row + r, :, lanes] = 0.5 * slope
            down = x2[row + r, :, (q + 1) * 128 : (q + 2) * 128].astype(F32)[:KP]
            act = rounded(down + act)
            total = act if total is None else total + act
    line = total * (0.25 * keep)
    put_line(x3, low, [before(line), line, after(line)])


def own_kernel(
    grid_rows, grid_cols,
    noise_index, rows_sc, cols_sc, noise, inputs, w1t, w2t, two, one,
    x1_out, d1_out, x2_out, x3_out, d2_out,
    x1, stage, d1, x2, mask, side, z0, z1, x3, d2, sems,
):
    odd = odd_column()
    halos = [
        pltpu.make_async_copy(one, side.at[1 - odd], sems.at[0]),
        pltpu.make_async_copy(two, side.at[odd], sems.at[1]),
    ]
    for copy in halos:
        copy.start()
    fill_mask(grid_rows // 4, grid_cols // 4, mask)
    scale, shift = modulation(noise, noise_index)
    for copy in halos:
        copy.wait()

    def first(q):
        def load(i):
            row = 4 * q + i
            return flat(inputs[row]), side[1, 1 + row], side[0, 1 + row]

        first_lines(load, HALO + 4 * q, 4 * q, (rows_sc, cols_sc), stage, x1)

    def dot(t):
        return conv_one_dot(x1, 4 * t + 2, w1t)

    def post(t, z):
        keeps = [mask[(9 + 2 * t) // 2], mask[(10 + 2 * t) // 2]]
        conv_one_post(z, scale, shift, keeps, d1, 4 * t, x2, 2 * t)

    first(0)
    first(1)
    z = (z0, z1)
    for t in range(11):
        z[t % 2][0 : 8 * KW, :] = dot(t)
        if t + 2 < 12:
            first(t + 2)
        if t > 0:
            post(t - 1, z[(t - 1) % 2])
        if t == 9:
            put_x1 = pltpu.make_async_copy(x1, x1_out, sems.at[2])
            put_x1.start()
    post(10, z0)
    put_d1 = pltpu.make_async_copy(d1, d1_out, sems.at[3])
    put_x2 = pltpu.make_async_copy(x2, x2_out, sems.at[4])
    put_d1.start()
    put_x2.start()

    def conv_two_dot(t):
        return product(around(x2, 1 + 10 * t, 10, slice(0, 512)), w2t[...])

    def conv_two_steps(t, z):
        for n in range(5):
            low = 5 * t + n
            conv_two_post(z, 2 * n * KW, mask[5 + low], x2_own, d2, 2 * low, x3, low)

    x2_own = x2.at[pl.ds(1, 20)]
    pipeline(2, conv_two_dot, conv_two_steps, z0, z1)
    put_x3 = pltpu.make_async_copy(x3, x3_out, sems.at[5])
    put_d2 = pltpu.make_async_copy(d2, d2_out, sems.at[6])
    put_x3.start()
    put_d2.start()
    put_x3.wait()
    put_d2.wait()
    put_x1.wait()
    put_d1.wait()
    put_x2.wait()


def own_rows(grid_rows, grid_cols, *args):
    def kernel(*refs):
        own_kernel(grid_rows, grid_cols, *refs)

    vm = pltpu.VMEM
    shape = jax.ShapeDtypeStruct
    return pl.pallas_call(
        kernel,
        out_shape=[
            shape((48, KW, 768), BF16),
            shape((44, KW, 512), BF16),
            shape((22, KW, 512), BF16),
            shape((10, KW, 384), BF16),
            shape((20, KP, 256), F32),
        ],
        in_specs=[smem_spec()] + [vmem_spec()] * 6 + [any_spec()] * 2,
        out_specs=[any_spec()] * 5,
        scratch_shapes=[
            vm((48, KW, 768), BF16),
            vm((4, 160, 128), F32),
            vm((44, KW, 512), BF16),
            vm((22, KW, 512), BF16),
            vm((LOWS, KP, 128), F32),
            vm((2, ROWS + 4, 16, 128), BF16),
            vm((10 * KW, 256), F32),
            vm((10 * KW, 256), F32),
            vm((10, KW, 384), BF16),
            vm((20, KP, 256), F32),
            pltpu.SemaphoreType.DMA((7,)),
        ],
        compiler_params=pltpu.CompilerParams(vmem_limit_bytes=20 * MIB),
        cost_estimate=pl.CostEstimate(flops=4 * 10**9, bytes_accessed=30 * 10**6, transcendentals=0),
        name="own_rows",
    )(*args)


def lines_kernel(
    grid_rows, grid_cols,
    noise_index, rows_sc, cols_sc, noise,
    cot, w1t, w2t, w2b, w3, w3b, off, near, two, one, x1_in, d1_in, x2_in, x3_in, d2_in,
    coarse_out, g1_out, keep_out, give_out,
    rim, stage, x1, d1, x2, d2, x3, cp, side, side32, g3, xb2, g2, g1, coarse,
    acc, acc3, gw, msg, mask, z0, z1, sems,
):
    core = lax.axis_index("core")
    odd = odd_column()

    def fetch(source, target, at):
        copy = pltpu.make_async_copy(source, target, sems.at[at])
        copy.start()
        return copy

    got_rims = []
    for n, (source, below) in enumerate(((off, core), (near, 1 - core))):
        rows = pl.ds(1 - below, SENT)
        got_rims.append(fetch(source.at[pl.ds(0, SENT)], rim.at[below, rows], n))
        got_rims.append(fetch(source.at[SENT], rim.at[below, HALO], 11 + n))
    got_edges = [
        fetch(x1_in.at[pl.ds(0, 4)], x1.at[pl.ds(16, 4)], 2),
        fetch(x1_in.at[pl.ds(44, 4)], x1.at[pl.ds(60, 4)], 3),
    ]
    got_x2 = fetch(x2_in, x2.at[pl.ds(9, 22)], 4)
    units = pl.ds(ROWS + 1, 3)
    got_sides = [fetch(one.at[units], side.at[1 - odd], 5), fetch(two.at[units], side.at[odd], 6)]
    got_low = [fetch(x3_in, x3.at[pl.ds(5, 10)], 7), fetch(d2_in, d2.at[pl.ds(10, 20)], 10)]
    got_d1 = fetch(d1_in, d1.at[pl.ds(18, 44)], 8)
    got_x1 = fetch(x1_in.at[pl.ds(4, 40)], x1.at[pl.ds(20, 40)], 9)
    fill_mask(grid_rows // 4, grid_cols // 4, mask)
    gw[:, 0:8, :] = jnp.zeros((4, 8, 128), F32)
    gw[:, 1160:1168, :] = jnp.zeros((4, 8, 128), F32)
    scale, shift = modulation(noise, noise_index)
    for copy in got_rims:
        copy.wait()
    rim[0, 0] = jnp.zeros((10, 16, 128), BF16)
    rim[1, SENT] = jnp.zeros((10, 16, 128), BF16)

    def first(n):
        below, start = n // 4, 4 * (n % 4)
        base = start + (HALO + ROWS) * below

        def load(i):
            row = start + i
            return flat(rim[below, row, 0:8]), rim[below, row, 8 + odd], rim[below, row, 9 - odd]

        first_lines(load, base, base, (rows_sc, cols_sc), stage, x1)

    def mid_of(t):
        return 1 + 2 * t if t < 4 else 23 + 2 * t

    def dot(t):
        return conv_one_dot(x1, 2 * mid_of(t), w1t)

    def post(t, z):
        m = mid_of(t)
        conv_one_post(z, scale, shift, [mask[m // 2], mask[(m + 1) // 2]], d1, 2 * m, x2, m)

    first(0)
    first(1)
    for copy in got_edges:
        copy.wait()
    z = (z0, z1)
    for t in range(8):
        z[t % 2][0 : 8 * KW, :] = dot(t)
        if t + 2 < 8:
            first(t + 2)
        if t > 0:
            post(t - 1, z[(t - 1) % 2])
    post(7, z1)
    got_x2.wait()

    def conv_two_dot(t):
        return product(around(x2, 2 + 28 * t, 8, slice(0, 512)), w2t[...])

    def conv_two_steps(t, z):
        for n in range(4):
            low = 1 + 14 * t + n
            conv_two_post(z, 2 * n * KW, mask[low], x2, d2, 2 * low, x3, low)

    pipeline(2, conv_two_dot, conv_two_steps, z0, z1)
    for copy in got_low:
        copy.wait()

    cp[...] = jnp.zeros_like(cp)
    for copy in got_sides:
        copy.wait()
    for h in range(2):
        lanes = slice(h * 128, (h + 1) * 128)
        for r in range(2):
            units = pl.ds((r * 2 + h) * 2, 2)
            cp[r, 0:KO, lanes] = rim[0, HALO, units].reshape(KO, 128).astype(F32)
            cp[14 + r, 0:KO, lanes] = rim[1, HALO, units].reshape(KO, 128).astype(F32)
    for r in range(12):
        cp[2 + r, 0:KO, :] = cot[r].astype(F32)
    for which, at in ((1, KO), (0, KP - 2)):
        side32[...] = side[which].reshape(48, 128).astype(F32)
        for h in range(2):
            for r in range(12):
                cp[2 + r, at : at + 2, h * 128 : (h + 1) * 128] = side32[r * 4 + h * 2 : r * 4 + h * 2 + 2]
    for below, skip, row in ((0, 8, 0), (1, 0, 14)):
        for unit, at in ((9 - odd, KP - 2), (8 + odd, KO)):
            side32[0:16] = rim[below, HALO, unit].astype(F32)
            for h in range(2):
                for r in range(2):
                    start = skip + r * 4 + h * 2
                    cp[row + r, at : at + 2, h * 128 : (h + 1) * 128] = side32[start : start + 2]
    g3[1] = jnp.zeros((KW, 768), BF16)
    g3[18] = jnp.zeros((KW, 768), BF16)

    def conv_three_post(t, z):
        for i in range(8):
            row = 2 + 8 * t + i
            act, slope = silu_parts(0.5 * z[i * KW : i * KW + KP, :])
            keep = 0.5 * mask[row]
            line = cp[row - 2] * slope * jnp.concatenate([keep, keep], axis=1)
            put_line(g3, row, [before(line), line, after(line)])
            coarse[row - 2] = act[:KO].astype(BF16)

    pipeline(2, lambda t: product(around(x3, 2 + 8 * t, 8, slice(0, 384)), w3[...]), conv_three_post, z0, z1)
    put_coarse = fetch(coarse.at[pl.ds(2, 12)], coarse_out, 0)

    def back_three_post(t, z):
        for i in range(8):
            low = 2 + 8 * t + i
            line = 0.25 * z[i * KW : i * KW + KP, 0:128]
            xb2[low] = line
            line = line * mask[low]
            for r in range(2):
                row = 2 * low + r
                zero, one = (line * d2[row, :, q * 128 : (q + 1) * 128] for q in range(2))
                put_line(g2, row, [before(one), zero, one, after(zero)])

    def back_three_dot(t):
        return product_turned(around(g3, 2 + 8 * t, 8, slice(0, 768)), w3b[...])

    pipeline(2, back_three_dot, back_three_post, z0, z1)
    acc3[...] = weight_terms(
        g3[4:16, 0:KO, 256:512].reshape(12 * KO, 256), around(x3, 4, 12, slice(0, 384), KO)
    )
    acc[...] = weight_terms(
        g2[8:32, 0:KO, 128:384].reshape(24 * KO, 256), around(x2, 8, 24, slice(0, 512), KO)
    )
    got_d1.wait()

    def back_two_post(t, z):
        for i in range(7):
            m = 6 + 7 * t + i
            low = m // 2
            keep = 0.25 * mask[low]
            base = xb2[low]
            both = [(base + z[i * KW : i * KW + KP, q * 128 : (q + 1) * 128]) * keep for q in range(2)]
            for r in range(2):
                row = 2 * m + r
                slopes = [d1[row, :, p * 128 : (p + 1) * 128].astype(F32)[:KP] for p in range(4)]
                planes = [both[p // 2] * slopes[p] for p in range(4)]
                for n, line in enumerate([before(planes[3])] + planes + [after(planes[0])]):
                    g1[row - 12, :, n * 128 : (n + 1) * 128] = line[:KO].astype(BF16)

    pipeline(
        4, lambda t: product_turned(around(g2, 6 + 7 * t, 7, slice(0, 512)), w2b[...]), back_two_post, z0, z1
    )
    put_g1 = fetch(g1.at[pl.ds(3, 50)], g1_out, 1)
    got_x1.wait()

    def fold_weights(at):
        for u in range(3):
            for v in range(3):
                left = (4 * u + v) * 128
                term = acc[0:128, left : left + 128] + acc[128:256, left + 128 : left + 256]
                gw[at, pl.ds(8 + (3 * u + v) * 128, 128), :] = term.T

    fold_weights(1)
    for tap in range(9):
        turned = acc3[:, tap * 128 : (tap + 1) * 128].T
        gw[2, pl.ds(8 + tap * 128, 128), :] = turned[:, 0:128]
        gw[3, pl.ds(8 + tap * 128, 128), :] = turned[:, 128:256]
    grads = [g1[4:52, :, lanes].reshape(ROWS * KO, 256) for lanes in (slice(128, 384), slice(384, 640))]
    fields = [around(x1, 16, ROWS, lanes, KO) for lanes in (slice(0, 512), slice(256, 768))]
    acc[...] = weight_terms(jnp.concatenate(grads, axis=0), jnp.concatenate(fields, axis=0))
    fold_weights(0)
    line = lax.broadcasted_iota(jnp.int32, (8, 128), 0)
    none = jnp.zeros((8, 128), F32)
    for owner in range(128):
        at = 8 + 9 * owner
        parts = [gw[0, at : at + 8, :]]
        for t in range(1, 5):
            rest = gw[t - 1, at + 9 - t : at + 17 - t, :]
            start = gw[t, at - t : at + 8 - t, :] if t < 4 else none
            parts.append(jnp.where(line < t, rest, start))
        row, col = divmod(owner, 8)
        msg[row % 2, (row // 2) * 8 + col] = jnp.concatenate(parts, axis=0).astype(BF16)
    put_keep = fetch(msg.at[core], keep_out, 2)
    put_give = fetch(msg.at[1 - core], give_out, 3)
    put_keep.wait()
    put_give.wait()
    put_coarse.wait()
    put_g1.wait()


def levels(grid_rows, grid_cols, *args):
    def kernel(*refs):
        lines_kernel(grid_rows, grid_cols, *refs)

    vm = pltpu.VMEM
    return pl.pallas_call(
        kernel,
        out_shape=[
            jax.ShapeDtypeStruct((12, KO, 256), BF16),
            jax.ShapeDtypeStruct((50, KO, 768), BF16),
            jax.ShapeDtypeStruct((64, 40, 128), BF16),
            jax.ShapeDtypeStruct((64, 40, 128), BF16),
        ],
        in_specs=[smem_spec()] + [vmem_spec()] * 9 + [any_spec()] * 9,
        out_specs=[any_spec()] * 4,
        scratch_shapes=[
            vm((2, HALO + 1, 10, 16, 128), BF16),
            vm((4, 160, 128), F32),
            vm((PAD_ROWS, KW, 768), BF16),
            vm((PAD_ROWS, KW, 512), BF16),
            vm((PAIRS, KW, 512), BF16),
            vm((PAIRS, KP, 256), F32),
            vm((LOWS, KW, 384), BF16),
            vm((16, KP, 256), F32),
            vm((2, 3, 16, 128), BF16),
            vm((48, 128), F32),
            vm((LOWS, KW, 768), BF16),
            vm((LOWS, KP, 128), F32),
            vm((PAIRS, KW, 512), BF16),
            vm((56, KO, 768), BF16),
            vm((16, KO, 256), BF16),
            vm((256, 1536), F32),
            vm((256, 1152), F32),
            vm((4, 1168, 128), F32),
            vm((2, 64, 40, 128), BF16),
            vm((LOWS, KP, 128), F32),
            vm((8 * KW, 256), F32),
            vm((8 * KW, 256), F32),
            pltpu.SemaphoreType.DMA((13,)),
        ],
        compiler_params=pltpu.CompilerParams(vmem_limit_bytes=36 * MIB),
        name="encoder_levels",
    )(*args)


def input_kernel(g1, g1_next, w1b, out, stage):
    for t in range(2):
        halves = []
        for lanes in (slice(0, 512), slice(256, 768)):
            rows = jnp.concatenate([g1[:, :, lanes], g1_next[:, :, lanes]], axis=0)
            parts = [rows[4 * t + u : 4 * t + u + 4].reshape(128, 512) for u in range(3)]
            halves.append(jnp.concatenate(parts, axis=1))
        total = product_turned(jnp.concatenate(halves, axis=0), w1b[...])
        for r in range(4):
            for p in range(4):
                rows = (p // 2) * 128 + r * 32
                value = total[rows : rows + 32, (p % 2) * 128 : (p % 2 + 1) * 128]
                stage[4 * t + r, pl.ds(p, 32, stride=4), :] = value
            out[4 * t + r] = stage[4 * t + r].astype(BF16)


def input_grad(g1, w1b):
    return pl.pallas_call(
        input_kernel,
        grid=(6,),
        out_shape=jax.ShapeDtypeStruct((ROWS, 128, 128), BF16),
        in_specs=[
            pl.BlockSpec((8, KO, 768), lambda i: (i, 0, 0)),
            pl.BlockSpec((2, KO, 768), lambda i: (4 * i + 4, 0, 0)),
            pl.BlockSpec((256, 1536), lambda i: (0, 0)),
        ],
        out_specs=pl.BlockSpec((8, 128, 128), lambda i: (i, 0, 0)),
        scratch_shapes=[pltpu.VMEM((8, 128, 128), F32)],
        compiler_params=pltpu.CompilerParams(vmem_limit_bytes=16 * MIB),
        cost_estimate=pl.CostEstimate(flops=2 * 6144 * 1152 * 128, bytes_accessed=8 * 1024 * 1024, transcendentals=0),
        name="input_grad",
    )(g1, g1, w1b)


def collect_kernel(got, one, two, three, held, total, sems):
    copies = []
    for n in range(4):
        part = pl.ds(16 * n, 16)
        copies.append(pltpu.make_async_copy(got.at[part], held.at[part], sems.at[n]))
        copies[n].start()
    sums = None
    for n, copy in enumerate(copies):
        copy.wait()
        for i in range(16):
            term = held[16 * n + i].astype(F32)
            sums = term if sums is None else sums + term
    total[...] = sums
    one[...] = total[0:9, :]
    two[...] = total[9:18, :]
    three[:, 0:128] = total[18:27, :]
    three[:, 128:256] = total[27:36, :]


def collect(got):
    shape = jax.ShapeDtypeStruct
    return pl.pallas_call(
        collect_kernel,
        out_shape=[shape((9, 128), F32), shape((9, 128), F32), shape((9, 256), F32)],
        in_specs=[any_spec()],
        out_specs=[vmem_spec()] * 3,
        scratch_shapes=[
            pltpu.VMEM((64, 40, 128), BF16),
            pltpu.VMEM((40, 128), F32),
            pltpu.SemaphoreType.DMA((4,)),
        ],
        compiler_params=pltpu.CompilerParams(vmem_limit_bytes=8 * MIB),
        name="collect_weights",
    )(got)


def swapped(block, axis, odd_first):
    devices = lax.axis_size(axis)
    pairs = []
    for i in range(1 if odd_first else 0, devices - 1, 2):
        pairs += [(i, i + 1), (i + 1, i)]
    return lax.ppermute(block, axis, pairs)


def body(inputs, weight_one, weight_two, weight_three, noise_table, frequency, anchor, noise_index, cotangent):
    grid = (lax.axis_size(ROW_AXES) * ROWS, lax.axis_size("tx") * 4 * KO)
    inputs = inputs.reshape(ROWS, 8, 16, 128)
    one, two, cots = sides(inputs, cotangent)
    two = swapped(two, "tx", True)
    one = swapped(one, "tx", False)
    w1t, w1b, w2t, w2b, w3b, rows_sc, cols_sc = prep(*grid, anchor, weight_one, weight_two, weight_three, frequency)
    off, near = rims(inputs, cots, two, one, rows_sc)
    off = swapped(off, ROW_AXES, True)
    near = lax.ppermute(near, "core", [(0, 1), (1, 0)])
    x1, d1, x2, x3, d2 = own_rows(
        *grid, noise_index, rows_sc, cols_sc, noise_table, inputs, w1t, w2t, two, one
    )
    coarse, g1, keep_msg, give_msg = levels(
        *grid, noise_index, rows_sc, cols_sc, noise_table,
        cotangent, w1t, w2t, w2b, weight_three, w3b, off, near, two, one, x1, d1, x2, x3, d2,
    )
    other = lax.ppermute(give_msg, "core", [(0, 1), (1, 0)])
    msg = (keep_msg.astype(F32) + other.astype(F32)).astype(BF16)
    got = lax.all_to_all(msg, ("chip", "tx"), 0, 0, tiled=True)
    grad_inputs = input_grad(g1, w1b)
    return (coarse, grad_inputs, *collect(got))


def solution(mesh):
    halves = jax.sharding.Mesh(mesh.devices.reshape(-1, 2, mesh.devices.shape[1]), ("chip", "core", "tx"))
    placed = (P(ROW_AXES, "tx", None), P(), P(), P(), P(), P(), P(), P(), P(ROW_AXES, "tx", None))
    return jax.shard_map(
        body,
        mesh=halves,
        in_specs=placed,
        out_specs=(
            P(ROW_AXES, "tx", None),
            P(ROW_AXES, "tx", None),
            P((*ROW_AXES, "tx"), None),
            P((*ROW_AXES, "tx"), None),
            P((*ROW_AXES, "tx"), None),
        ),
        check_vma=False,
    )
```

```python
import jax
import jax.numpy as jnp
from jax import lax
from jax.experimental import pallas as pl
from jax.experimental.pallas import tpu as pltpu
from jax.sharding import PartitionSpec as P

BF16 = jnp.bfloat16
F32 = jnp.float32

KO = 32
KP = 40
KW = 48
HALO = 16
SENT = 15
ROWS = 48
PAD_ROWS = ROWS + 2 * HALO
PAIRS = PAD_ROWS // 2
LOWS = PAIRS // 2
MIB = 1024 * 1024


def any_spec():
    return pl.BlockSpec(memory_space=pl.ANY)


def vmem_spec():
    return pl.BlockSpec(memory_space=pltpu.VMEM)


def smem_spec():
    return pl.BlockSpec(memory_space=pltpu.SMEM)


ROW_AXES = ("chip", "core")


def own_place():
    return lax.axis_index(ROW_AXES), lax.axis_index("tx")


def odd_column():
    return lax.rem(lax.axis_index("tx"), 2)


def side_kernel(inputs, cot, one, two, cots, side32, sems):
    odd = odd_column()
    copies = [
        pltpu.make_async_copy(inputs.at[:, 7 - 7 * odd], one.at[pl.ds(1, ROWS)], sems.at[0]),
        pltpu.make_async_copy(inputs.at[:, 7 * odd], two.at[pl.ds(1, ROWS)], sems.at[1]),
    ]
    for copy in copies:
        copy.start()
    for target, at_left in ((one, odd == 1), (two, odd == 0)):
        for r in range(12):
            line = cot[r].astype(F32)
            for h in range(2):
                lanes = slice(h * 128, (h + 1) * 128)
                side32[pl.ds(r * 4 + h * 2, 2)] = jnp.where(at_left, line[0:2, lanes], line[30:32, lanes])
        side = side32[...].astype(BF16).reshape(3, 16, 128)
        target[pl.ds(0, 1)] = side[0:1]
        target[pl.ds(1 + ROWS, 3)] = side
    for at, start in ((0, 10), (1, 0)):
        for r in range(2):
            for h in range(2):
                cots[at, pl.ds((r * 2 + h) * 2, 2)] = cot[start + r, :, h * 128 : (h + 1) * 128].reshape(2, 16, 128)
    for copy in copies:
        copy.wait()


def sides(inputs, cot):
    return pl.pallas_call(
        side_kernel,
        out_shape=[jax.ShapeDtypeStruct((ROWS + 4, 16, 128), BF16)] * 2 + [jax.ShapeDtypeStruct((2, 8, 16, 128), BF16)],
        in_specs=[any_spec(), vmem_spec()],
        out_specs=[vmem_spec()] * 3,
        scratch_shapes=[pltpu.VMEM((48, 128), F32), pltpu.SemaphoreType.DMA((2,))],
        compiler_params=pltpu.CompilerParams(vmem_limit_bytes=8 * MIB),
        name="pack_columns",
    )(inputs, cot)


def rim_kernel(inputs, cots, two, one, _, off, near, sems):
    core = lax.axis_index("core")
    copies = []

    def fetch(source, target):
        copy = pltpu.make_async_copy(source, target, sems.at[len(copies)])
        copy.start()
        copies.append(copy)

    body = pl.ds(0, SENT)
    for target, low in ((off, core), (near, 1 - core)):
        row = (ROWS - SENT) * low
        fetch(inputs.at[pl.ds(row, SENT)], target.at[body, pl.ds(0, 8)])
        fetch(cots.at[1 - low], target.at[SENT, pl.ds(0, 8)])
        for unit, side in ((8, one), (9, two)):
            fetch(side.at[pl.ds(1 + row, SENT)], target.at[body, unit])
            fetch(side.at[(3 + ROWS) * low], target.at[SENT, unit])
    for copy in copies:
        copy.wait()


def rims(*args):
    return pl.pallas_call(
        rim_kernel,
        out_shape=[jax.ShapeDtypeStruct((SENT + 1, 10, 16, 128), BF16)] * 2,
        in_specs=[any_spec()] * len(args),
        out_specs=[vmem_spec()] * 2,
        scratch_shapes=[pltpu.SemaphoreType.DMA((12,))],
        compiler_params=pltpu.CompilerParams(vmem_limit_bytes=8 * MIB),
        name="pack_rows",
    )(*args)


def weight_forms(w1, w2, w3, w1t, w1b, w2t, w2b, w3b):
    zero = jnp.zeros((128, 128), BF16)
    for source, ahead, back in ((w1, w1t, w1b), (w2, w2t, w2b)):
        for u in range(3):
            for v in range(3):
                tap = source[pl.ds((3 * u + v) * 128, 128), :]
                for i in range(2):
                    side = slice(i * 128, (i + 1) * 128)
                    ahead[pl.ds((4 * u + v + i) * 128, 128), side] = tap
                    at = (4 * (2 - u) + 2 - v + i) * 128
                    back[side, at : at + 128] = tap
            for i, j in ((0, 3), (1, 0)):
                at = (4 * u + j) * 128
                side = slice(i * 128, (i + 1) * 128)
                ahead[pl.ds(at, 128), side] = zero
                back[side, at : at + 128] = zero
    for u in range(3):
        for v in range(3):
            at = (3 * (2 - u) + 2 - v) * 256
            w3b[:, at : at + 256] = w3[pl.ds((3 * u + v) * 128, 128), :]


def wave_tables(grid_rows, grid_cols, anchor, frequency, rows_sc, cols_sc):
    own_row, own_col = own_place()
    row = lax.broadcasted_iota(jnp.int32, (PAD_ROWS, 128), 0) - HALO + own_row * ROWS
    angle = (row + anchor[0]).astype(F32) * frequency[0:1, :]
    keep = jnp.where((row >= 0) & (row < grid_rows), 1.0, 0.0)
    rows_sc[0] = jnp.sin(angle) * keep
    rows_sc[1] = jnp.cos(angle) * keep
    for p in range(4):
        k = lax.broadcasted_iota(jnp.int32, (KP, 128), 0)
        col = 4 * jnp.where(k < KO + 4, k, k - KP) + p + own_col * (4 * KO)
        angle = (col + anchor[1]).astype(F32) * frequency[1:2, :]
        keep = jnp.where((col >= 0) & (col < grid_cols), 1.0, 0.0)
        cols_sc[0, p] = jnp.sin(angle) * keep
        cols_sc[1, p] = jnp.cos(angle) * keep


def prep_kernel(grid_rows, grid_cols, anchor, w1, w2, w3, frequency, w1t, w1b, w2t, w2b, w3b, rows_sc, cols_sc):
    weight_forms(w1, w2, w3, w1t, w1b, w2t, w2b, w3b)
    wave_tables(grid_rows, grid_cols, anchor, frequency, rows_sc, cols_sc)


def prep(grid_rows, grid_cols, anchor, w1, w2, w3, frequency):
    def kernel(*refs):
        prep_kernel(grid_rows, grid_cols, *refs)

    shape = jax.ShapeDtypeStruct
    return pl.pallas_call(
        kernel,
        out_shape=[
            shape((1536, 256), BF16),
            shape((256, 1536), BF16),
            shape((1536, 256), BF16),
            shape((256, 1536), BF16),
            shape((128, 2304), BF16),
            shape((2, PAD_ROWS, 128), F32),
            shape((2, 4, KP, 128), F32),
        ],
        in_specs=[smem_spec()] + [vmem_spec()] * 4,
        out_specs=[vmem_spec()] * 7,
        compiler_params=pltpu.CompilerParams(vmem_limit_bytes=12 * MIB),
        name="weight_forms",
    )(anchor, w1, w2, w3, frequency)


def fill_mask(low_rows, low_cols, mask):
    own_row, own_col = own_place()
    k = lax.broadcasted_iota(jnp.int32, (KP, 128), 0)
    col = jnp.where(k < KO + 4, k, k - KP) + own_col * KO
    inside = jnp.where((col >= 0) & (col < low_cols), 1.0, 0.0)

    def step(at, _):
        row = at - 4 + own_row * 12
        mask[at] = inside * jnp.where((row >= 0) & (row < low_rows), 1.0, 0.0)
        return 0

    lax.fori_loop(0, LOWS, step, 0)


def widened(line):
    rest = jnp.zeros((KW - KP, line.shape[1]), F32)
    return jnp.concatenate([line, rest], axis=0).astype(BF16)


def put_line(ref, row, planes):
    width = planes[0].shape[1]
    for n, plane in enumerate(planes):
        ref[row, :, n * width : (n + 1) * width] = widened(plane)


def before(line):
    return pltpu.roll(line, 1, 0)


def after(line):
    return pltpu.roll(line, KP - 1, 0)


def silu_parts(half):
    th = jnp.tanh(half)
    act = half + half * th
    return act, (1.0 + act) + th * (1.0 - act)


def rounded(value):
    return value.astype(BF16).astype(F32)


def flat(block):
    return block.reshape(128, 128)


def modulation(noise, noise_index):
    modulate = noise[pl.ds(noise_index[0], 1), :]
    return 1.0 + modulate[:, 0:128], modulate[:, 128:256]


def first_lines(load, base, at, tables, stage, x1):
    rows_sc, cols_sc = tables
    for i in range(4):
        own, right, left = load(i)
        stage[i, 0:128] = own.astype(F32)
        stage[i, 128:144] = right.astype(F32)
        stage[i, 144:160] = left.astype(F32)
        sin_row = rows_sc[0, pl.ds(base + i, 1), :]
        cos_row = rows_sc[1, pl.ds(base + i, 1), :]
        planes = []
        for p in range(4):
            value = stage[i, pl.ds(p, KP, stride=4), :]
            planes.append(value + (sin_row * cols_sc[1, p] + cos_row * cols_sc[0, p]))
        put_line(x1, at + i, [before(planes[3])] + planes + [after(planes[0])])


def around(ref, at, count, lanes, cols=KW):
    parts = [ref[pl.ds(at - 1 + u, count), 0:cols, lanes] for u in range(3)]
    return jnp.concatenate([part.reshape(count * cols, part.shape[-1]) for part in parts], axis=1)


def product(left, right):
    return jnp.dot(left, right, preferred_element_type=F32)


def product_turned(left, right):
    return lax.dot_general(left, right, (((1,), (1,)), ((), ())), preferred_element_type=F32)


def weight_terms(grad, field):
    return lax.dot_general(grad, field, (((0,), (0,)), ((), ())), preferred_element_type=F32)


def pipeline(steps, dot, post, z0, z1):
    z = (z0, z1)
    for t in range(steps + 1):
        if t < steps:
            total = dot(t)
            z[t % 2][0 : total.shape[0], 0 : total.shape[1]] = total
        if t > 0:
            post(t - 1, z[(t - 1) % 2])


def conv_one_dot(x1, row, w1t):
    one = around(x1, row, 4, slice(0, 512))
    two = around(x1, row, 4, slice(256, 768))
    return product(jnp.concatenate([one, two], axis=0), w1t[...])


def conv_one_post(z, scale, shift, keeps, d1, d1_row, x2, x2_row):
    half_scale, half_shift = 0.5 * scale, 0.5 * shift
    slope_scale = half_scale.astype(BF16)
    for s in range(2):
        halves = []
        for q in range(2):
            sums = []
            for p in (2 * q, 2 * q + 1):
                lanes = slice((p % 2) * 128, (p % 2 + 1) * 128)
                acts = []
                for r in range(2):
                    at = q * 4 * KW + (2 * s + r) * KW
                    act, slope = silu_parts((z[at : at + KW, lanes] * half_scale + half_shift).astype(BF16))
                    d1[d1_row + 2 * s + r, :, p * 128 : (p + 1) * 128] = slope_scale * slope
                    acts.append(act)
                sums.append((acts[0] + acts[1]).astype(F32))
            halves.append((sums[0] + sums[1])[:KP] * (0.25 * keeps[s]))
        put_line(x2, x2_row + s, [before(halves[1]), halves[0], halves[1], after(halves[0])])


def conv_two_post(z, at, keep, x2, d2, row, x3, low):
    total = None
    for q in range(2):
        lanes = slice(q * 128, (q + 1) * 128)
        for r in range(2):
            start = at + r * KW
            act, slope = silu_parts(0.5 * z[start : start + KP, lanes])
            d2[row + r, :, lanes] = 0.5 * slope
            down = x2[row + r, :, (q + 1) * 128 : (q + 2) * 128].astype(F32)[:KP]
            act = rounded(down + act)
            total = act if total is None else total + act
    line = total * (0.25 * keep)
    put_line(x3, low, [before(line), line, after(line)])


def own_kernel(
    grid_rows, grid_cols,
    noise_index, rows_sc, cols_sc, noise, inputs, w1t, w2t, two, one,
    x1_out, d1_out, x2_out, x3_out, d2_out,
    x1, stage, d1, x2, mask, side, z0, z1, x3, d2, sems,
):
    odd = odd_column()
    halos = [
        pltpu.make_async_copy(one, side.at[1 - odd], sems.at[0]),
        pltpu.make_async_copy(two, side.at[odd], sems.at[1]),
    ]
    for copy in halos:
        copy.start()
    fill_mask(grid_rows // 4, grid_cols // 4, mask)
    scale, shift = modulation(noise, noise_index)
    for copy in halos:
        copy.wait()

    def first(q):
        def load(i):
            row = 4 * q + i
            return flat(inputs[row]), side[1, 1 + row], side[0, 1 + row]

        first_lines(load, HALO + 4 * q, 4 * q, (rows_sc, cols_sc), stage, x1)

    def dot(t):
        return conv_one_dot(x1, 4 * t + 2, w1t)

    def post(t, z):
        keeps = [mask[(9 + 2 * t) // 2], mask[(10 + 2 * t) // 2]]
        conv_one_post(z, scale, shift, keeps, d1, 4 * t, x2, 2 * t)

    first(0)
    first(1)
    z = (z0, z1)
    for t in range(11):
        z[t % 2][0 : 8 * KW, :] = dot(t)
        if t + 2 < 12:
            first(t + 2)
        if t > 0:
            post(t - 1, z[(t - 1) % 2])
        if t == 9:
            put_x1 = pltpu.make_async_copy(x1, x1_out, sems.at[2])
            put_x1.start()
    post(10, z0)
    put_d1 = pltpu.make_async_copy(d1, d1_out, sems.at[3])
    put_x2 = pltpu.make_async_copy(x2, x2_out, sems.at[4])
    put_d1.start()
    put_x2.start()

    def conv_two_dot(t):
        return product(around(x2, 1 + 10 * t, 10, slice(0, 512)), w2t[...])

    def conv_two_steps(t, z):
        for n in range(5):
            low = 5 * t + n
            conv_two_post(z, 2 * n * KW, mask[5 + low], x2_own, d2, 2 * low, x3, low)

    x2_own = x2.at[pl.ds(1, 20)]
    pipeline(2, conv_two_dot, conv_two_steps, z0, z1)
    put_x3 = pltpu.make_async_copy(x3, x3_out, sems.at[5])
    put_d2 = pltpu.make_async_copy(d2, d2_out, sems.at[6])
    put_x3.start()
    put_d2.start()
    put_x3.wait()
    put_d2.wait()
    put_x1.wait()
    put_d1.wait()
    put_x2.wait()


def own_rows(grid_rows, grid_cols, *args):
    def kernel(*refs):
        own_kernel(grid_rows, grid_cols, *refs)

    vm = pltpu.VMEM
    shape = jax.ShapeDtypeStruct
    return pl.pallas_call(
        kernel,
        out_shape=[
            shape((48, KW, 768), BF16),
            shape((44, KW, 512), BF16),
            shape((22, KW, 512), BF16),
            shape((10, KW, 384), BF16),
            shape((20, KP, 256), F32),
        ],
        in_specs=[smem_spec()] + [vmem_spec()] * 6 + [any_spec()] * 2,
        out_specs=[any_spec()] * 5,
        scratch_shapes=[
            vm((48, KW, 768), BF16),
            vm((4, 160, 128), F32),
            vm((44, KW, 512), BF16),
            vm((22, KW, 512), BF16),
            vm((LOWS, KP, 128), F32),
            vm((2, ROWS + 4, 16, 128), BF16),
            vm((10 * KW, 256), F32),
            vm((10 * KW, 256), F32),
            vm((10, KW, 384), BF16),
            vm((20, KP, 256), F32),
            pltpu.SemaphoreType.DMA((7,)),
        ],
        compiler_params=pltpu.CompilerParams(vmem_limit_bytes=20 * MIB),
        cost_estimate=pl.CostEstimate(flops=4 * 10**9, bytes_accessed=30 * 10**6, transcendentals=0),
        name="own_rows",
    )(*args)


def halo_steps(below, rim, odd, rows_sc, cols_sc, stage, x1, mask, w1t, scale, shift, d1, x2, z0, z1):
    def first(n):
        start = 4 * n
        base = start + (HALO + ROWS) * below

        def load(i):
            row = start + i
            return flat(rim[below, row, 0:8]), rim[below, row, 8 + odd], rim[below, row, 9 - odd]

        first_lines(load, base, base, (rows_sc, cols_sc), stage, x1)

    def dot(t):
        return conv_one_dot(x1, 2 * (1 + 2 * t + 30 * below), w1t)

    def post(t, z):
        m = 1 + 2 * t + 30 * below
        conv_one_post(z, scale, shift, [mask[m // 2], mask[(m + 1) // 2]], d1, 2 * m, x2, m)

    first(0)
    first(1)
    z = (z0, z1)
    for t in range(4):
        z[t % 2][0 : 8 * KW, :] = dot(t)
        if t + 2 < 4:
            first(t + 2)
        if t > 0:
            post(t - 1, z[(t - 1) % 2])
    post(3, z1)


def near_kernel(
    grid_rows, grid_cols,
    noise_index, rows_sc, cols_sc, noise, w1t, near, x1_in,
    x1_out, d1_out, x2_out,
    rim, stage, x1, d1, x2, mask, z0, z1, sems,
):
    core = lax.axis_index("core")
    odd = odd_column()
    under = 1 - core

    def fetch(source, target, at):
        copy = pltpu.make_async_copy(source, target, sems.at[at])
        copy.start()
        return copy

    gets = [
        fetch(near.at[pl.ds(0, SENT)], rim.at[under, pl.ds(1 - under, SENT)], 0),
        fetch(x1_in.at[pl.ds(0, 4)], x1.at[pl.ds(16, 4)], 1),
        fetch(x1_in.at[pl.ds(44, 4)], x1.at[pl.ds(60, 4)], 2),
    ]
    fill_mask(grid_rows // 4, grid_cols // 4, mask)
    scale, shift = modulation(noise, noise_index)
    for copy in gets:
        copy.wait()
    rim[0, 0] = jnp.zeros((10, 16, 128), BF16)
    rim[1, SENT] = jnp.zeros((10, 16, 128), BF16)
    for below in range(2):

        @pl.when(under == below)
        def _():
            halo_steps(below, rim, odd, rows_sc, cols_sc, stage, x1, mask, w1t, scale, shift, d1, x2, z0, z1)

    puts = [
        fetch(x2.at[pl.ds(1 + 30 * under, 8)], x2_out, 0),
        fetch(d1.at[pl.ds(12 + 50 * under, 6)], d1_out, 1),
        fetch(x1.at[pl.ds(15 + 49 * under, 1)], x1_out, 2),
    ]
    for copy in puts:
        copy.wait()


def near_rows(grid_rows, grid_cols, *args):
    def kernel(*refs):
        near_kernel(grid_rows, grid_cols, *refs)

    vm = pltpu.VMEM
    shape = jax.ShapeDtypeStruct
    return pl.pallas_call(
        kernel,
        out_shape=[shape((1, KW, 768), BF16), shape((6, KW, 512), BF16), shape((8, KW, 512), BF16)],
        in_specs=[smem_spec()] + [vmem_spec()] * 4 + [any_spec()] * 2,
        out_specs=[any_spec()] * 3,
        scratch_shapes=[
            vm((2, HALO, 10, 16, 128), BF16),
            vm((4, 160, 128), F32),
            vm((PAD_ROWS, KW, 768), BF16),
            vm((PAD_ROWS, KW, 512), BF16),
            vm((PAIRS, KW, 512), BF16),
            vm((LOWS, KP, 128), F32),
            vm((8 * KW, 256), F32),
            vm((8 * KW, 256), F32),
            pltpu.SemaphoreType.DMA((3,)),
        ],
        compiler_params=pltpu.CompilerParams(vmem_limit_bytes=20 * MIB),
        cost_estimate=pl.CostEstimate(flops=2 * 10**9, bytes_accessed=8 * 10**6, transcendentals=0),
        name="near_rows",
    )(*args)


def lines_kernel(
    grid_rows, grid_cols,
    noise_index, rows_sc, cols_sc, noise,
    cot, w1t, w2t, w2b, w3, w3b, off, near, two, one, x1_in, d1_in, x2_in, x3_in, d2_in, x1_near, d1_near, x2_near,
    coarse_out, g1_out, keep_out, give_out,
    rim, stage, x1, d1, x2, d2, x3, cp, side, side32, g3, xb2, g2, g1, coarse,
    acc, acc3, gw, msg, mask, z0, z1, sems,
):
    core = lax.axis_index("core")
    odd = odd_column()

    def fetch(source, target, at):
        copy = pltpu.make_async_copy(source, target, sems.at[at])
        copy.start()
        return copy

    got_rims = []
    for n, (source, below) in enumerate(((off, core), (near, 1 - core))):
        rows = pl.ds(1 - below, SENT)
        got_rims.append(fetch(source.at[pl.ds(0, SENT)], rim.at[below, rows], n))
        got_rims.append(fetch(source.at[SENT], rim.at[below, HALO], 11 + n))
    got_edges = [
        fetch(x1_in.at[pl.ds(0, 4)], x1.at[pl.ds(16, 4)], 2),
        fetch(x1_in.at[pl.ds(44, 4)], x1.at[pl.ds(60, 4)], 3),
    ]
    got_x2 = fetch(x2_in, x2.at[pl.ds(9, 22)], 4)
    under = 1 - core
    got_near = [
        fetch(x2_near, x2.at[pl.ds(1 + 30 * under, 8)], 13),
        fetch(d1_near, d1.at[pl.ds(12 + 50 * under, 6)], 14),
        fetch(x1_near, x1.at[pl.ds(15 + 49 * under, 1)], 15),
    ]
    units = pl.ds(ROWS + 1, 3)
    got_sides = [fetch(one.at[units], side.at[1 - odd], 5), fetch(two.at[units], side.at[odd], 6)]
    got_low = [fetch(x3_in, x3.at[pl.ds(5, 10)], 7), fetch(d2_in, d2.at[pl.ds(10, 20)], 10)]
    got_d1 = fetch(d1_in, d1.at[pl.ds(18, 44)], 8)
    got_x1 = fetch(x1_in.at[pl.ds(4, 40)], x1.at[pl.ds(20, 40)], 9)
    fill_mask(grid_rows // 4, grid_cols // 4, mask)
    gw[:, 0:8, :] = jnp.zeros((4, 8, 128), F32)
    gw[:, 1160:1168, :] = jnp.zeros((4, 8, 128), F32)
    scale, shift = modulation(noise, noise_index)
    for copy in (*got_rims, *got_edges):
        copy.wait()
    rim[0, 0] = jnp.zeros((10, 16, 128), BF16)
    rim[1, SENT] = jnp.zeros((10, 16, 128), BF16)

    for below in range(2):

        @pl.when(core == below)
        def _():
            halo_steps(below, rim, odd, rows_sc, cols_sc, stage, x1, mask, w1t, scale, shift, d1, x2, z0, z1)

    got_x2.wait()
    for copy in got_near:
        copy.wait()

    def conv_two_dot(t):
        return product(around(x2, 2 + 28 * t, 8, slice(0, 512)), w2t[...])

    def conv_two_steps(t, z):
        for n in range(4):
            low = 1 + 14 * t + n
            conv_two_post(z, 2 * n * KW, mask[low], x2, d2, 2 * low, x3, low)

    pipeline(2, conv_two_dot, conv_two_steps, z0, z1)
    for copy in got_low:
        copy.wait()

    cp[...] = jnp.zeros_like(cp)
    for copy in got_sides:
        copy.wait()
    for h in range(2):
        lanes = slice(h * 128, (h + 1) * 128)
        for r in range(2):
            units = pl.ds((r * 2 + h) * 2, 2)
            cp[r, 0:KO, lanes] = rim[0, HALO, units].reshape(KO, 128).astype(F32)
            cp[14 + r, 0:KO, lanes] = rim[1, HALO, units].reshape(KO, 128).astype(F32)
    for r in range(12):
        cp[2 + r, 0:KO, :] = cot[r].astype(F32)
    for which, at in ((1, KO), (0, KP - 2)):
        side32[...] = side[which].reshape(48, 128).astype(F32)
        for h in range(2):
            for r in range(12):
                cp[2 + r, at : at + 2, h * 128 : (h + 1) * 128] = side32[r * 4 + h * 2 : r * 4 + h * 2 + 2]
    for below, skip, row in ((0, 8, 0), (1, 0, 14)):
        for unit, at in ((9 - odd, KP - 2), (8 + odd, KO)):
            side32[0:16] = rim[below, HALO, unit].astype(F32)
            for h in range(2):
                for r in range(2):
                    start = skip + r * 4 + h * 2
                    cp[row + r, at : at + 2, h * 128 : (h + 1) * 128] = side32[start : start + 2]
    g3[1] = jnp.zeros((KW, 768), BF16)
    g3[18] = jnp.zeros((KW, 768), BF16)

    def conv_three_post(t, z):
        for i in range(8):
            row = 2 + 8 * t + i
            act, slope = silu_parts(0.5 * z[i * KW : i * KW + KP, :])
            keep = 0.5 * mask[row]
            line = cp[row - 2] * slope * jnp.concatenate([keep, keep], axis=1)
            put_line(g3, row, [before(line), line, after(line)])
            coarse[row - 2] = act[:KO].astype(BF16)

    pipeline(2, lambda t: product(around(x3, 2 + 8 * t, 8, slice(0, 384)), w3[...]), conv_three_post, z0, z1)
    put_coarse = fetch(coarse.at[pl.ds(2, 12)], coarse_out, 0)

    def back_three_post(t, z):
        for i in range(8):
            low = 2 + 8 * t + i
            line = 0.25 * z[i * KW : i * KW + KP, 0:128]
            xb2[low] = line
            line = line * mask[low]
            for r in range(2):
                row = 2 * low + r
                zero, one = (line * d2[row, :, q * 128 : (q + 1) * 128] for q in range(2))
                put_line(g2, row, [before(one), zero, one, after(zero)])

    def back_three_dot(t):
        return product_turned(around(g3, 2 + 8 * t, 8, slice(0, 768)), w3b[...])

    pipeline(2, back_three_dot, back_three_post, z0, z1)
    acc3[...] = weight_terms(
        g3[4:16, 0:KO, 256:512].reshape(12 * KO, 256), around(x3, 4, 12, slice(0, 384), KO)
    )
    acc[...] = weight_terms(
        g2[8:32, 0:KO, 128:384].reshape(24 * KO, 256), around(x2, 8, 24, slice(0, 512), KO)
    )
    got_d1.wait()

    def back_two_post(t, z):
        for i in range(7):
            m = 6 + 7 * t + i
            low = m // 2
            keep = 0.25 * mask[low]
            base = xb2[low]
            both = [(base + z[i * KW : i * KW + KP, q * 128 : (q + 1) * 128]) * keep for q in range(2)]
            for r in range(2):
                row = 2 * m + r
                slopes = [d1[row, :, p * 128 : (p + 1) * 128].astype(F32)[:KP] for p in range(4)]
                planes = [both[p // 2] * slopes[p] for p in range(4)]
                for n, line in enumerate([before(planes[3])] + planes + [after(planes[0])]):
                    g1[row - 12, :, n * 128 : (n + 1) * 128] = line[:KO].astype(BF16)

    pipeline(
        4, lambda t: product_turned(around(g2, 6 + 7 * t, 7, slice(0, 512)), w2b[...]), back_two_post, z0, z1
    )
    put_g1 = fetch(g1.at[pl.ds(3, 50)], g1_out, 1)
    got_x1.wait()

    def fold_weights(at):
        for u in range(3):
            for v in range(3):
                left = (4 * u + v) * 128
                term = acc[0:128, left : left + 128] + acc[128:256, left + 128 : left + 256]
                gw[at, pl.ds(8 + (3 * u + v) * 128, 128), :] = term.T

    fold_weights(1)
    for tap in range(9):
        turned = acc3[:, tap * 128 : (tap + 1) * 128].T
        gw[2, pl.ds(8 + tap * 128, 128), :] = turned[:, 0:128]
        gw[3, pl.ds(8 + tap * 128, 128), :] = turned[:, 128:256]
    line = lax.broadcasted_iota(jnp.int32, (8, 128), 0)
    none = jnp.zeros((8, 128), F32)
    order = (1, 2, 3, 0)

    def message(parts):
        for owner in range(128):
            at = 8 + 9 * owner
            rows = []
            for t in parts:
                start = gw[order[t], at - t : at + 8 - t, :] if t < 4 else none
                if t > 0:
                    rest = gw[order[t - 1], at + 9 - t : at + 17 - t, :]
                    start = jnp.where(line < t, rest, start)
                rows.append(start)
            row, col = divmod(owner, 8)
            to = slice(8 * parts[0], 8 * parts[-1] + 8)
            msg[row % 2, (row // 2) * 8 + col, to] = jnp.concatenate(rows, axis=0).astype(BF16)

    grads = [g1[4:52, :, lanes].reshape(ROWS * KO, 256) for lanes in (slice(128, 384), slice(384, 640))]
    fields = [around(x1, 16, ROWS, lanes, KO) for lanes in (slice(0, 512), slice(256, 768))]
    acc[...] = weight_terms(jnp.concatenate(grads, axis=0), jnp.concatenate(fields, axis=0))
    message((0, 1))
    fold_weights(0)
    message((2, 3, 4))
    put_keep = fetch(msg.at[core], keep_out, 2)
    put_give = fetch(msg.at[1 - core], give_out, 3)
    put_keep.wait()
    put_give.wait()
    put_coarse.wait()
    put_g1.wait()


def levels(grid_rows, grid_cols, *args):
    def kernel(*refs):
        lines_kernel(grid_rows, grid_cols, *refs)

    vm = pltpu.VMEM
    return pl.pallas_call(
        kernel,
        out_shape=[
            jax.ShapeDtypeStruct((12, KO, 256), BF16),
            jax.ShapeDtypeStruct((50, KO, 768), BF16),
            jax.ShapeDtypeStruct((64, 40, 128), BF16),
            jax.ShapeDtypeStruct((64, 40, 128), BF16),
        ],
        in_specs=[smem_spec()] + [vmem_spec()] * 9 + [any_spec()] * 12,
        out_specs=[any_spec()] * 4,
        scratch_shapes=[
            vm((2, HALO + 1, 10, 16, 128), BF16),
            vm((4, 160, 128), F32),
            vm((PAD_ROWS, KW, 768), BF16),
            vm((PAD_ROWS, KW, 512), BF16),
            vm((PAIRS, KW, 512), BF16),
            vm((PAIRS, KP, 256), F32),
            vm((LOWS, KW, 384), BF16),
            vm((16, KP, 256), F32),
            vm((2, 3, 16, 128), BF16),
            vm((48, 128), F32),
            vm((LOWS, KW, 768), BF16),
            vm((LOWS, KP, 128), F32),
            vm((PAIRS, KW, 512), BF16),
            vm((56, KO, 768), BF16),
            vm((16, KO, 256), BF16),
            vm((256, 1536), F32),
            vm((256, 1152), F32),
            vm((4, 1168, 128), F32),
            vm((2, 64, 40, 128), BF16),
            vm((LOWS, KP, 128), F32),
            vm((8 * KW, 256), F32),
            vm((8 * KW, 256), F32),
            pltpu.SemaphoreType.DMA((16,)),
        ],
        compiler_params=pltpu.CompilerParams(vmem_limit_bytes=36 * MIB),
        name="encoder_levels",
    )(*args)


def input_kernel(g1, g1_next, w1b, out, stage):
    for t in range(2):
        halves = []
        for lanes in (slice(0, 512), slice(256, 768)):
            rows = jnp.concatenate([g1[:, :, lanes], g1_next[:, :, lanes]], axis=0)
            parts = [rows[4 * t + u : 4 * t + u + 4].reshape(128, 512) for u in range(3)]
            halves.append(jnp.concatenate(parts, axis=1))
        total = product_turned(jnp.concatenate(halves, axis=0), w1b[...])
        for r in range(4):
            for p in range(4):
                rows = (p // 2) * 128 + r * 32
                value = total[rows : rows + 32, (p % 2) * 128 : (p % 2 + 1) * 128]
                stage[4 * t + r, pl.ds(p, 32, stride=4), :] = value
            out[4 * t + r] = stage[4 * t + r].astype(BF16)


def input_grad(g1, w1b):
    return pl.pallas_call(
        input_kernel,
        grid=(6,),
        out_shape=jax.ShapeDtypeStruct((ROWS, 128, 128), BF16),
        in_specs=[
            pl.BlockSpec((8, KO, 768), lambda i: (i, 0, 0)),
            pl.BlockSpec((2, KO, 768), lambda i: (4 * i + 4, 0, 0)),
            pl.BlockSpec((256, 1536), lambda i: (0, 0)),
        ],
        out_specs=pl.BlockSpec((8, 128, 128), lambda i: (i, 0, 0)),
        scratch_shapes=[pltpu.VMEM((8, 128, 128), F32)],
        compiler_params=pltpu.CompilerParams(vmem_limit_bytes=16 * MIB),
        cost_estimate=pl.CostEstimate(flops=2 * 6144 * 1152 * 128, bytes_accessed=8 * 1024 * 1024, transcendentals=0),
        name="input_grad",
    )(g1, g1, w1b)


def collect_kernel(got, one, two, three, held, total, sems):
    copies = []
    for n in range(4):
        part = pl.ds(16 * n, 16)
        copies.append(pltpu.make_async_copy(got.at[part], held.at[part], sems.at[n]))
        copies[n].start()
    sums = None
    for n, copy in enumerate(copies):
        copy.wait()
        for i in range(16):
            term = held[16 * n + i].astype(F32)
            sums = term if sums is None else sums + term
    total[...] = sums
    two[...] = total[0:9, :]
    three[:, 0:128] = total[9:18, :]
    three[:, 128:256] = total[18:27, :]
    one[...] = total[27:36, :]


def collect(got):
    shape = jax.ShapeDtypeStruct
    return pl.pallas_call(
        collect_kernel,
        out_shape=[shape((9, 128), F32), shape((9, 128), F32), shape((9, 256), F32)],
        in_specs=[any_spec()],
        out_specs=[vmem_spec()] * 3,
        scratch_shapes=[
            pltpu.VMEM((64, 40, 128), BF16),
            pltpu.VMEM((40, 128), F32),
            pltpu.SemaphoreType.DMA((4,)),
        ],
        compiler_params=pltpu.CompilerParams(vmem_limit_bytes=8 * MIB),
        name="collect_weights",
    )(got)


def swapped(block, axis, odd_first):
    devices = lax.axis_size(axis)
    pairs = []
    for i in range(1 if odd_first else 0, devices - 1, 2):
        pairs += [(i, i + 1), (i + 1, i)]
    return lax.ppermute(block, axis, pairs)


def body(inputs, weight_one, weight_two, weight_three, noise_table, frequency, anchor, noise_index, cotangent):
    grid = (lax.axis_size(ROW_AXES) * ROWS, lax.axis_size("tx") * 4 * KO)
    inputs = inputs.reshape(ROWS, 8, 16, 128)
    one, two, cots = sides(inputs, cotangent)
    two = swapped(two, "tx", True)
    one = swapped(one, "tx", False)
    w1t, w1b, w2t, w2b, w3b, rows_sc, cols_sc = prep(*grid, anchor, weight_one, weight_two, weight_three, frequency)
    off, near = rims(inputs, cots, two, one, rows_sc)
    off = swapped(off, ROW_AXES, True)
    near = lax.ppermute(near, "core", [(0, 1), (1, 0)])
    x1, d1, x2, x3, d2 = own_rows(
        *grid, noise_index, rows_sc, cols_sc, noise_table, inputs, w1t, w2t, two, one
    )
    x1_near, d1_near, x2_near = near_rows(*grid, noise_index, rows_sc, cols_sc, noise_table, w1t, near, x1)
    coarse, g1, keep_msg, give_msg = levels(
        *grid, noise_index, rows_sc, cols_sc, noise_table,
        cotangent, w1t, w2t, w2b, weight_three, w3b, off, near, two, one, x1, d1, x2, x3, d2, x1_near, d1_near, x2_near,
    )
    other = lax.ppermute(give_msg, "core", [(0, 1), (1, 0)])
    msg = (keep_msg.astype(F32) + other.astype(F32)).astype(BF16)
    got = lax.all_to_all(msg, ("chip", "tx"), 0, 0, tiled=True)
    grad_inputs = input_grad(g1, w1b)
    return (coarse, grad_inputs, *collect(got))


def solution(mesh):
    halves = jax.sharding.Mesh(mesh.devices.reshape(-1, 2, mesh.devices.shape[1]), ("chip", "core", "tx"))
    placed = (P(ROW_AXES, "tx", None), P(), P(), P(), P(), P(), P(), P(), P(ROW_AXES, "tx", None))
    return jax.shard_map(
        body,
        mesh=halves,
        in_specs=placed,
        out_specs=(
            P(ROW_AXES, "tx", None),
            P(ROW_AXES, "tx", None),
            P((*ROW_AXES, "tx"), None),
            P((*ROW_AXES, "tx"), None),
            P((*ROW_AXES, "tx"), None),
        ),
        check_vma=False,
    )
```
